32 devices in a mesh: dp: 8 (over z, x), seq: 4 (over y, core).
Axes of the slice: x: 2, y: 2, z: 4, core: 2. Of those that a mesh axis runs over, the one named last changes fastest.
Arguments:
- tokens: bfloat16 [12288, 1408], P(('dp', 'seq')), may hold values from -6 to 6
- skip: bfloat16 [12288, 1408], P(('dp', 'seq')), may hold values from -6 to 6
- segment_ids: int32 [8, 1536], P('dp'), may hold values from 0 to 2, as said below
- grid_widths: int32 [8, 3], P('dp'), may hold values from 16 to 32
- clip_lengths: int32 [8, 3], P('dp'), may hold values from 1 to 77
- t5_lengths: int32 [8, 3], P('dp'), may hold values from 1 to 256
- timestep: bfloat16 [8, 3, 1408], P('dp'), may hold values from -6 to 6
- captions: bfloat16 [8, 999, 1024], P('dp'), may hold values from -6 to 6
- ln_gains: float32 [5, 1408], replicated, may hold values from 0.5 to 1.5
- ln_biases: float32 [5, 1408], replicated, may hold values from -1.25 to 1.25
- qk_gains: float32 [2, 88], replicated, may hold values from 0.5 to 1.5
- qk_biases: float32 [2, 88], replicated, may hold values from -1.25 to 1.25
- w_skip: bfloat16 [2816, 1408], P('dp'), may hold values from -0.109375 to 0.109375
- w_mod: bfloat16 [1408, 1408], P('dp'), may hold values from -0.15625 to 0.15625
- w_qkv: bfloat16 [1408, 4224], P('dp'), may hold values from -0.15625 to 0.15625
- w_out: bfloat16 [1408, 1408], P('dp'), may hold values from -3.5 to 3.5
- w_cq: bfloat16 [1408, 1408], P('dp'), may hold values from -0.15625 to 0.15625
- w_ckv: bfloat16 [1024, 2816], P('dp'), may hold values from -0.1875 to 0.1875
- w_co: bfloat16 [1408, 1408], P('dp'), may hold values from -1.5 to 1.5
- w_up: bfloat16 [1408, 6144], P('dp'), may hold values from -0.15625 to 0.15625
- w_down: bfloat16 [6144, 1408], P('dp'), may hold values from -0.078125 to 0.078125
- cotangent: bfloat16 [12288, 1408], P(('dp', 'seq')), may hold values from -6 to 6
Outputs:
- block_out: bfloat16 [12288, 1408], P(('dp', 'seq'))
- grad_tokens: bfloat16 [12288, 1408], P(('dp', 'seq'))
- grad_skip: bfloat16 [12288, 1408], P(('dp', 'seq'))
- grad_ln_gains: float32 [5, 1408], replicated
- grad_ln_biases: float32 [4, 1408], replicated
- grad_ff_bias: float32 [1408], replicated
- grad_qk_gains: float32 [2, 88], replicated
- grad_qk_biases: float32 [2, 88], replicated
- grad_w_skip: float32 [2816, 1408], P('dp')
- grad_w_mod: float32 [1408, 1408], P('dp')
- grad_w_qkv: float32 [1408, 4224], P('dp')
- grad_w_out: float32 [1408, 1408], P('dp')
- grad_w_cq: float32 [1408, 1408], P('dp')
- grad_w_ckv: float32 [1024, 2816], P('dp')
- grad_w_co: float32 [1408, 1408], P('dp')
- grad_w_up: float32 [1408, 6144], P('dp')
- grad_w_down: float32 [6144, 1408], P('dp')
The draws below stay inside these ranges and needn't reach their ends.
Inputs may be any that keep to these rules, and one draw needn't show every extreme that they name: `segment_ids`: in each bucket the image numbers never fall, every one of the 3 images has at least one token, and each image is one contiguous run.
All inputs are finite; a program needn't handle non-finite values.
Results may differ from the reference program's by a relative error of at most 0.025.
Values may be sent and summed in bfloat16 or wider, within the bound.
No kernel may reach another device: no remote copies, remote signals or barrier semaphores. Data moves between devices by JAX's collectives and lax.ppermute only.
A program may use at most 384 MiB of HBM per device.

```python
import jax
import jax.numpy as jnp
from jax import lax

D = 1408
HEADS = 16
HEAD = 88
FF = 6144
TEXT_W = 1024
CLIP_TOK = 77
T5_TOK = 256
IMGS = 3
TOK_DEV = 384
CAP = 333
BUCKETS = 8
BUCKET_TOK = 1536
TOKENS = 12288
N_SEQ = 4


def draw_segment_ids(key, part):
    key = jax.random.fold_in(key, 11)
    front_key, back_key = jax.random.split(key)
    margin = max(3, min(TOK_DEV, (BUCKET_TOK - 1024) // 2))
    front_cut = jax.random.randint(front_key, (BUCKETS, 1), 1, margin)
    back_cut = jax.random.randint(back_key, (BUCKETS, 1), BUCKET_TOK - margin + 1, BUCKET_TOK)
    positions = jnp.arange(BUCKET_TOK, dtype=jnp.int32)[None, :]
    return (positions >= front_cut).astype(jnp.int32) + (positions >= back_cut).astype(jnp.int32)


def touch_ends(entries, stream_key, smallest, top_value):
    dims = entries.shape
    index_at = [jax.random.randint(jax.random.fold_in(stream_key, axis), (), 0, dims[axis]) for axis in range(len(dims))]
    entries = entries.at[tuple(index_at)].set(smallest)
    longest = dims.index(max(dims))
    index_at[longest] = (index_at[longest] + 1) % dims[longest]
    return entries.at[tuple(index_at)].set(top_value)


def levels(key, shape, cuts, smallest, largest):
    def one(dim, shards_of):
        steps = jax.random.uniform(jax.random.fold_in(jax.random.fold_in(key, 6), dim), (shards_of,), jnp.float32, smallest / len(cuts), largest / len(cuts))
        return jnp.repeat(jnp.exp(steps), shape[dim] // shards_of).reshape((-1,) + (1,) * (len(shape) - dim - 1))

    factor_of = one(*cuts[0])
    for cut in cuts[1:]:
        factor_of = factor_of * one(*cut)
    return factor_of


def noise(key, shape, width, bound, pieces=(), kind=jnp.bfloat16):
    level = levels(key, shape, pieces, -0.22, 0.18) if pieces else 1.0
    values = jax.random.normal(key, shape, jnp.float32) * width * level
    return jnp.minimum(jnp.maximum(values, -bound), bound).astype(kind)


def setup_inputs(seed: int = 0) -> dict:
    keys = jax.random.split(jax.random.key(seed), 23)
    return {
        "tokens": noise(keys[0], (TOKENS, D), 1.0, 6.0, ((0, 32),)),
        "skip": noise(keys[1], (TOKENS, D), 1.0, 6.0, ((0, 32),)),
        "segment_ids": draw_segment_ids(jax.random.fold_in(keys[22], 71), 0),
        "grid_widths": touch_ends(jax.random.randint(keys[3], (BUCKETS, IMGS), max(2, BUCKET_TOK // 96), max(4, BUCKET_TOK // 48) + 1), jax.random.fold_in(keys[3], 1), max(2, BUCKET_TOK // 96), (max(4, BUCKET_TOK // 48) + 1) - 1).astype(jnp.int32),
        "clip_lengths": touch_ends(jax.random.randint(keys[4], (BUCKETS, IMGS), 1, CLIP_TOK + 1), jax.random.fold_in(keys[4], 1), 1, CLIP_TOK).astype(jnp.int32),
        "t5_lengths": touch_ends(jax.random.randint(keys[5], (BUCKETS, IMGS), 1, T5_TOK + 1), jax.random.fold_in(keys[5], 1), 1, T5_TOK).astype(jnp.int32),
        "timestep": noise(keys[6], (BUCKETS, IMGS, D), 1.0, 6.0, ((0, 8),)),
        "captions": noise(keys[7], (BUCKETS, IMGS * CAP, TEXT_W), 1.0, 6.0, ((0, 8),)),
        "ln_gains": jnp.clip(1.0 + 0.1 * jax.random.normal(keys[8], (5, D), jnp.float32), 0.5, 1.5),
        "ln_biases": noise(keys[9], (5, D), 0.2, 1.25, (), jnp.float32),
        "qk_gains": jnp.clip(1.0 + 0.1 * jax.random.normal(keys[10], (2, HEAD), jnp.float32), 0.5, 1.5),
        "qk_biases": noise(keys[11], (2, HEAD), 0.2, 1.25, (), jnp.float32),
        "w_skip": noise(keys[12], (2 * D, D), (2 * D) ** -0.5, 0.109375, ((0, 8),)),
        "w_mod": noise(keys[13], (D, D), D ** -0.5, 0.15625, ((0, 8),)),
        "w_qkv": noise(keys[14], (D, 3 * D), D ** -0.5, 0.15625, ((0, 8),)),
        "w_out": noise(keys[15], (D, D), (max(1, D * 4 // (TOK_DEV * N_SEQ))) ** -0.5, 3.5, ((0, 8),)),
        "w_cq": noise(keys[16], (D, D), D ** -0.5, 0.15625, ((0, 8),)),
        "w_ckv": noise(keys[17], (TEXT_W, 2 * D), TEXT_W ** -0.5, 0.1875, ((0, 8),)),
        "w_co": noise(keys[18], (D, D), (max(1, D * 4 // CAP)) ** -0.5, 1.5, ((0, 8),)),
        "w_up": noise(keys[19], (D, FF), D ** -0.5, 0.15625, ((0, 8),)),
        "w_down": noise(keys[20], (FF, D), FF ** -0.5, 0.078125, ((0, 8),)),
        "cotangent": noise(keys[21], (TOKENS, D), 1.0, 6.0, ((0, 32),)),
    }


@jax.custom_vjp
def low(v):
    return lax.optimization_barrier(v.astype(jnp.bfloat16)).astype(jnp.float32)

@jax.custom_vjp
def low_back(v):
    return v

def low_keep(v):
    return (low(v), None)

def low_pass(kept, grad):
    return (grad,)

def back_keep(v):
    return (v, None)

def back_low(kept, grad):
    return (low(grad),)
low.defvjp(low_keep, low_pass)
low_back.defvjp(back_keep, back_low)
eps_norm = 1e-06
masked_score = -1e+30

def exact_product(left, right):
    return jnp.dot(left, right, precision=lax.Precision.HIGHEST, preferred_element_type=jnp.float32)

def layer_norm(values, norm_gain, norm_bias):
    center = values - lax.optimization_barrier(jnp.mean(values, axis=-1, keepdims=True))
    spread = lax.optimization_barrier(jnp.mean(center * center, axis=-1, keepdims=True))
    return center * lax.rsqrt(spread + eps_norm) * norm_gain + norm_bias

def gelu_tanh(values):
    return 0.5 * values * (1.0 + jnp.tanh(0.7978845608028654 * (values + 0.044715 * values * values * values)))

def silu_gate(values):
    return values * jax.nn.sigmoid(values)

def soft_rows(scores):
    row_max = lax.optimization_barrier(jnp.max(scores, axis=-1, keepdims=True))
    exp_scores = jnp.exp(scores - row_max)
    return exp_scores / lax.optimization_barrier(jnp.sum(exp_scores, axis=-1, keepdims=True))

def rotate_half(values, cos_part, sin_part):
    quarter = values.shape[-1] // 2
    front_half = values[..., :quarter]
    back_half = values[..., quarter:]
    return jnp.concatenate([front_half * cos_part - back_half * sin_part, front_half * sin_part + back_half * cos_part], axis=-1)

def rope_two(values, row_pos, col_pos):
    head_dim = values.shape[-1]
    half_dim = head_dim // 2
    frequency = 10000.0 ** (-(jnp.arange(head_dim // 4, dtype=jnp.float32) * 4.0 / head_dim))
    row_angle = (row_pos[:, None] * frequency[None, :])[:, None, :]
    col_angle = (col_pos[:, None] * frequency[None, :])[:, None, :]
    row_part = rotate_half(values[..., :half_dim], jnp.cos(row_angle), jnp.sin(row_angle))
    col_part = rotate_half(values[..., half_dim:], jnp.cos(col_angle), jnp.sin(col_angle))
    return jnp.concatenate([row_part, col_part], axis=-1)

def head_prep(qkv_pre, qk_gains, qk_biases, row_pos, col_pos):
    head_split = qkv_pre.reshape(qkv_pre.shape[0], 3, HEADS, HEAD)
    queries = rope_two(layer_norm(head_split[:, 0], qk_gains[0], qk_biases[0]), row_pos, col_pos)
    keyset = rope_two(layer_norm(head_split[:, 1], qk_gains[1], qk_biases[1]), row_pos, col_pos)
    return (queries, keyset, head_split[:, 2])

def grid_positions(seg_all, widths, first_tok, tok_count):
    images = jnp.arange(IMGS, dtype=jnp.int32)
    starts = lax.optimization_barrier(jnp.sum((seg_all[None, :] < images[:, None]).astype(jnp.int32), axis=1))
    seg_part = lax.dynamic_slice_in_dim(seg_all, first_tok, tok_count)
    member = seg_part[:, None] == images[None, :]
    start_tok = lax.optimization_barrier(jnp.sum(jnp.where(member, starts[None, :], 0), axis=1))
    width_tok = lax.optimization_barrier(jnp.sum(jnp.where(member, widths[None, :], 0), axis=1))
    in_image = first_tok + jnp.arange(tok_count, dtype=jnp.int32) - start_tok
    return (seg_part, member, (in_image // width_tok).astype(jnp.float32), (in_image % width_tok).astype(jnp.float32))

def caption_allowed(seg_part, clip_len, t5_len):
    images = jnp.arange(IMGS, dtype=jnp.int32)
    key_spots = jnp.arange(IMGS * CAP, dtype=jnp.int32)
    key_image = key_spots // CAP
    key_slot = key_spots % CAP
    key_member = key_image[:, None] == images[None, :]
    clip_own = lax.optimization_barrier(jnp.sum(jnp.where(key_member, clip_len[None, :], 0), axis=1))
    t5_own = lax.optimization_barrier(jnp.sum(jnp.where(key_member, t5_len[None, :], 0), axis=1))
    key_valid = jnp.where(key_slot < CLIP_TOK, key_slot < clip_own, key_slot - CLIP_TOK < t5_own)
    return (seg_part[:, None] == key_image[None, :]) & key_valid[None, :]

def bucket_forward(weights, inputs):
    norm_gains, norm_biases, qk_gains, qk_biases, w_skip, w_mod, w_qkv, w_out, w_cq, w_ckv, w_co, w_up, w_down = weights
    tok_rows, skip_rows, seg_all, widths, clip_len, t5_len, time_emb, text_rows = inputs
    model_width = tok_rows.shape[1]
    bucket_len = tok_rows.shape[0]
    score_scale = HEAD ** (-0.5)
    seg_part, member, row_pos, col_pos = grid_positions(seg_all, widths, 0, bucket_len)
    joined = jnp.concatenate([tok_rows, skip_rows], axis=1)
    h_zero = low(layer_norm(joined, norm_gains[0:2].reshape(-1), norm_biases[0:2].reshape(-1)))
    x_one = low_back(exact_product(h_zero, w_skip))
    time_cond = low(silu_gate(exact_product(member.astype(jnp.float32), time_emb)))
    time_shift = low_back(exact_product(time_cond, w_mod))
    n_one = low(layer_norm(x_one, norm_gains[2], norm_biases[2]) + time_shift)
    qkv_pre = low_back(exact_product(n_one, w_qkv))
    queries, keyset, values = head_prep(qkv_pre, qk_gains, qk_biases, row_pos, col_pos)
    queries = low(low_back(queries))
    keyset = low(low_back(keyset))
    values = low(low_back(values))
    allowed = seg_all[:, None] == seg_all[None, :]

    def self_head(head_items):
        query_h, key_h, value_h = head_items
        scores = jnp.where(allowed, low_back(exact_product(query_h, key_h.T) * score_scale), masked_score)
        return exact_product(low(soft_rows(scores)), value_h)
    attn_o = lax.map(jax.checkpoint(self_head), (queries.transpose(1, 0, 2), keyset.transpose(1, 0, 2), values.transpose(1, 0, 2)))
    attn_o = low(low_back(attn_o.transpose(1, 0, 2).reshape(bucket_len, model_width)))
    x_two = x_one + low_back(exact_product(attn_o, w_out))
    n_three = low(layer_norm(x_two, norm_gains[3], norm_biases[3]))
    cross_q = low(low_back(exact_product(n_three, w_cq))).reshape(bucket_len, HEADS, HEAD)
    text_kv = exact_product(text_rows, w_ckv)
    cross_k = low(text_kv[:, :model_width]).reshape(-1, HEADS, HEAD)
    cross_v = low(text_kv[:, model_width:]).reshape(-1, HEADS, HEAD)
    cross_mask = caption_allowed(seg_part, clip_len, t5_len)

    def cross_head(head_items):
        query_h, key_h, value_h = head_items
        scores = jnp.where(cross_mask, low_back(exact_product(query_h, key_h.T) * score_scale), masked_score)
        return exact_product(low(soft_rows(scores)), value_h)
    cross_o = lax.map(jax.checkpoint(cross_head), (cross_q.transpose(1, 0, 2), cross_k.transpose(1, 0, 2), cross_v.transpose(1, 0, 2)))
    cross_o = low(low_back(cross_o.transpose(1, 0, 2).reshape(bucket_len, model_width)))
    x_three = x_two + low_back(exact_product(cross_o, w_co))
    n_two = low(layer_norm(x_three, norm_gains[4], norm_biases[4]))
    up_proj = low_back(exact_product(n_two, w_up))
    act_low = low(gelu_tanh(up_proj))
    return x_three + low_back(exact_product(act_low, w_down))

def reference(tokens, skip, segment_ids, grid_widths, clip_lengths, t5_lengths, timestep, captions, ln_gains, ln_biases, qk_gains, qk_biases, w_skip, w_mod, w_qkv, w_out, w_cq, w_ckv, w_co, w_up, w_down, cotangent):
    params = tuple((item.astype(jnp.float32) for item in (ln_gains, ln_biases, qk_gains, qk_biases, w_skip, w_mod, w_qkv, w_out, w_cq, w_ckv, w_co, w_up, w_down)))
    tok_rows = tokens.astype(jnp.float32).reshape(BUCKETS, BUCKET_TOK, D)
    skip_rows = skip.astype(jnp.float32).reshape(BUCKETS, BUCKET_TOK, D)
    fixed_inputs = (segment_ids, grid_widths, clip_lengths, t5_lengths, timestep.astype(jnp.float32), captions.astype(jnp.float32))

    def forward(tok_in, skip_in, weights):

        def one_bucket(bucket_items):
            return bucket_forward(weights, bucket_items)
        return lax.map(jax.checkpoint(one_bucket), (tok_in, skip_in) + fixed_inputs)
    block, pullback = jax.vjp(forward, tok_rows, skip_rows, params)
    d_tok, d_skip, d_params = pullback(cotangent.astype(jnp.float32).reshape(BUCKETS, BUCKET_TOK, D))
    return (block.reshape(TOKENS, D).astype(jnp.bfloat16), d_tok.reshape(TOKENS, D).astype(jnp.bfloat16), d_skip.reshape(TOKENS, D).astype(jnp.bfloat16), d_params[0], d_params[1][0:4], d_params[1][4], d_params[2], d_params[3], d_params[4], d_params[5], d_params[6], d_params[7], d_params[8], d_params[9], d_params[10], d_params[11], d_params[12])
```

```python
import jax
import jax.numpy as jnp
from jax import lax
from jax.sharding import PartitionSpec as P

HEADS = 16
HEAD = 88
CLIP_TOK = 77
IMGS = 3
CAP = 333


eps_norm = 1e-06
masked_score = -1e30


def matmul(left, right):
    return jnp.dot(left, right, preferred_element_type=jnp.float32)


def layer_norm(values, norm_gain, norm_bias):
    center = values - jnp.mean(values, axis=-1, keepdims=True)
    spread = jnp.mean(center * center, axis=-1, keepdims=True)
    return center * lax.rsqrt(spread + eps_norm) * norm_gain + norm_bias


def gelu_tanh(values):
    return (
        0.5
        * values
        * (1.0 + jnp.tanh(0.7978845608028654 * (values + 0.044715 * values * values * values)))
    )


def silu_gate(values):
    return values * jax.nn.sigmoid(values)


def soft_rows(scores):
    row_max = jnp.max(scores, axis=-1, keepdims=True)
    exp_scores = jnp.exp(scores - row_max)
    return exp_scores / jnp.sum(exp_scores, axis=-1, keepdims=True)


def rotate_half(values, cos_part, sin_part):
    quarter = values.shape[-1] // 2
    front_half = values[..., :quarter]
    back_half = values[..., quarter:]
    return jnp.concatenate(
        [
            front_half * cos_part - back_half * sin_part,
            front_half * sin_part + back_half * cos_part,
        ],
        axis=-1,
    )


def rope_two(values, row_pos, col_pos):
    head_dim = values.shape[-1]
    half_dim = head_dim // 2
    frequency = 10000.0 ** (-(jnp.arange(head_dim // 4, dtype=jnp.float32) * 4.0 / head_dim))
    row_angle = (row_pos[:, None] * frequency[None, :])[:, None, :]
    col_angle = (col_pos[:, None] * frequency[None, :])[:, None, :]
    row_part = rotate_half(values[..., :half_dim], jnp.cos(row_angle), jnp.sin(row_angle))
    col_part = rotate_half(values[..., half_dim:], jnp.cos(col_angle), jnp.sin(col_angle))
    return jnp.concatenate([row_part, col_part], axis=-1)


def head_prep(qkv_pre, qk_gains, qk_biases, row_pos, col_pos):
    head_split = qkv_pre.reshape(qkv_pre.shape[0], 3, -1, HEAD)
    queries = rope_two(layer_norm(head_split[:, 0], qk_gains[0], qk_biases[0]), row_pos, col_pos)
    keyset = rope_two(layer_norm(head_split[:, 1], qk_gains[1], qk_biases[1]), row_pos, col_pos)
    return (queries, keyset, head_split[:, 2])


def grid_positions(seg_all, widths, first_tok, tok_count):
    images = jnp.arange(IMGS, dtype=jnp.int32)
    starts = jnp.sum((seg_all[None, :] < images[:, None]).astype(jnp.int32), axis=1)
    seg_part = lax.dynamic_slice_in_dim(seg_all, first_tok, tok_count)
    member = seg_part[:, None] == images[None, :]
    start_tok = jnp.sum(jnp.where(member, starts[None, :], 0), axis=1)
    width_tok = jnp.sum(jnp.where(member, widths[None, :], 0), axis=1)
    in_image = first_tok + jnp.arange(tok_count, dtype=jnp.int32) - start_tok
    return (
        seg_part,
        member,
        (in_image // width_tok).astype(jnp.float32),
        (in_image % width_tok).astype(jnp.float32),
    )


def caption_allowed(seg_part, clip_len, t5_len):
    images = jnp.arange(IMGS, dtype=jnp.int32)
    key_spots = jnp.arange(IMGS * CAP, dtype=jnp.int32)
    key_image = key_spots // CAP
    key_slot = key_spots % CAP
    key_member = key_image[:, None] == images[None, :]
    clip_own = jnp.sum(jnp.where(key_member, clip_len[None, :], 0), axis=1)
    t5_own = jnp.sum(jnp.where(key_member, t5_len[None, :], 0), axis=1)
    key_valid = jnp.where(key_slot < CLIP_TOK, key_slot < clip_own, key_slot - CLIP_TOK < t5_own)
    return (seg_part[:, None] == key_image[None, :]) & key_valid[None, :]


def swap_pairs(count, mask):
    return [(rank, rank ^ mask) for rank in range(count)]


def seq_blocks(block, count):
    held = {0: block}
    bit = count // 2
    while bit:
        for mask in list(held):
            held[mask | bit] = lax.ppermute(held[mask], "seq", swap_pairs(count, bit))
        bit //= 2
    return [held[mask] for mask in range(count)]


def seq_sum(parts, count):
    held = dict(enumerate(parts))
    bit = 1
    while bit < count:
        for mask in [m for m in held if m & bit]:
            came = lax.ppermute(
                held.pop(mask).astype(jnp.bfloat16), "seq", swap_pairs(count, bit)
            )
            held[mask ^ bit] = held[mask ^ bit] + came.astype(jnp.float32)
        bit *= 2
    return held[0]


def seq_exchange(parts, count):
    return [parts[0]] + [
        lax.ppermute(parts[mask], "seq", swap_pairs(count, mask)) for mask in range(1, count)
    ]


def gather_rows(weight, seq_count, seq_rank):
    rows = weight.shape[0]
    if rows % seq_count:
        return lax.all_gather(weight, "dp", axis=0, tiled=True)
    own = lax.dynamic_slice_in_dim(weight, seq_rank * (rows // seq_count), rows // seq_count)
    return lax.all_gather(own, ("dp", "seq"), axis=0, tiled=True)


def scatter_rows(grad, dp_count, seq_count):
    low = grad.astype(jnp.bfloat16)
    if (grad.shape[0] // dp_count) % seq_count:
        total = lax.psum_scatter(low, "dp", scatter_dimension=0, tiled=True)
        return lax.psum(total, "seq").astype(jnp.float32)
    total = lax.psum_scatter(low, ("dp", "seq"), scatter_dimension=0, tiled=True)
    return lax.all_gather(total, "seq", axis=0, tiled=True).astype(jnp.float32)


def shards(
    tokens,
    skip,
    segment_ids,
    grid_widths,
    clip_lengths,
    t5_lengths,
    timestep,
    captions,
    ln_gains,
    ln_biases,
    qk_gains,
    qk_biases,
    w_skip,
    w_mod,
    w_qkv,
    w_out,
    w_cq,
    w_ckv,
    w_co,
    w_up,
    w_down,
    cotangent,
):
    local_tok = tokens.shape[0]
    model_width = tokens.shape[1]
    seq_count = lax.axis_size("seq")
    dp_count = lax.axis_size("dp")
    seq_rank = lax.axis_index("seq")
    dp_rank = lax.axis_index("dp")
    bucket_len = local_tok * seq_count
    local_heads = HEADS // seq_count
    head_cols = local_heads * HEAD
    wide = w_up.shape[1]
    part = wide // (dp_count * seq_count)
    local_wide = part * dp_count
    row_count = w_mod.shape[0]
    score_scale = HEAD ** (-0.5)
    block_rows = min(512, bucket_len)
    block_count = bucket_len // block_rows
    order = seq_rank ^ jnp.arange(seq_count, dtype=jnp.int32)

    full_skip = gather_rows(w_skip, seq_count, seq_rank)
    own_qkv = lax.dynamic_index_in_dim(
        w_qkv.reshape(row_count, 3, seq_count, head_cols), seq_rank, 2, keepdims=False
    ).reshape(row_count, 3 * head_cols)
    part_qkv = lax.all_gather(own_qkv, "dp", axis=0, tiled=True)
    pad_rows = -(3 * row_count) % (8 * seq_count)
    square = jnp.concatenate(
        [w_out, w_cq, w_co, jnp.zeros((pad_rows, model_width), w_out.dtype)], axis=0
    )
    square = gather_rows(square, seq_count, seq_rank).reshape(dp_count, -1, model_width)
    full_out, full_cq, full_co = (
        square[:, i * row_count : (i + 1) * row_count].reshape(model_width, model_width)
        for i in range(3)
    )
    full_ckv = gather_rows(w_ckv, seq_count, seq_rank)
    own_up = lax.dynamic_index_in_dim(
        w_up.reshape(row_count, dp_count, seq_count, part), seq_rank, 2, keepdims=False
    ).reshape(row_count, local_wide)
    part_up = lax.all_gather(own_up, "dp", axis=0, tiled=True)
    part_down = lax.all_gather(
        lax.dynamic_slice_in_dim(w_down, seq_rank * part, part), "dp", axis=0, tiled=True
    )

    seg_all = segment_ids[0]
    seg_local, member, _, _ = grid_positions(seg_all, grid_widths[0], seq_rank * local_tok, local_tok)
    _, _, row_all, col_all = grid_positions(seg_all, grid_widths[0], 0, bucket_len)

    def reorder(values):
        return jnp.take(values.reshape(seq_count, local_tok), order, axis=0).reshape(-1)

    row_pos, col_pos, seg_all = reorder(row_all), reorder(col_all), reorder(seg_all)
    seg_blocks = seg_all.reshape(block_count, block_rows)

    cond = silu_gate(timestep[0].astype(jnp.float32)).astype(jnp.bfloat16)
    cond_all = lax.all_gather(cond, "dp", axis=0, tiled=True)
    cond_rows = lax.dynamic_slice_in_dim(cond_all, dp_rank * row_count, row_count, axis=1)
    shifts = lax.psum_scatter(matmul(cond_rows, w_mod), "dp", scatter_dimension=0, tiled=True)
    time_shift = jnp.sum(jnp.where(member[:, :, None], shifts[None], 0.0), axis=1)

    joined = jnp.concatenate([tokens, skip], axis=1).astype(jnp.float32)
    h_float, pull_skip = jax.vjp(
        layer_norm, joined, ln_gains[0:2].reshape(-1), ln_biases[0:2].reshape(-1)
    )
    h_zero = h_float.astype(jnp.bfloat16)
    x_one = matmul(h_zero, full_skip)
    n_float, pull_one = jax.vjp(layer_norm, x_one, ln_gains[2], ln_biases[2])
    n_one = (n_float + time_shift).astype(jnp.bfloat16)
    n_one_all = jnp.concatenate(seq_blocks(n_one, seq_count), axis=0)
    qkv_pre = matmul(n_one_all, part_qkv)

    def prep_local(pre_rows, gains, biases):
        return head_prep(pre_rows, gains, biases, row_pos, col_pos)

    (queries, keyset, values), pull_heads = jax.vjp(prep_local, qkv_pre, qk_gains, qk_biases)
    by_head = jnp.stack([queries, keyset, values]).astype(jnp.bfloat16).transpose(0, 2, 1, 3)

    def block_scores(query_b, seg_b, key_h):
        return jnp.where(
            seg_b[:, None] == seg_all[None, :], matmul(query_b, key_h.T) * score_scale, masked_score
        )

    def self_forward(head_items):
        query_h, key_h, value_h = head_items

        def forward_block(block_items):
            query_b, seg_b = block_items
            scores = block_scores(query_b, seg_b, key_h)
            row_max = jnp.max(scores, axis=1, keepdims=True)
            exp_scores = jnp.exp(scores - row_max)
            row_sum = jnp.sum(exp_scores, axis=1, keepdims=True)
            attn_probs = (exp_scores / row_sum).astype(jnp.bfloat16)
            return (matmul(attn_probs, value_h).astype(jnp.bfloat16), row_max, row_sum)

        outs, maxes, sums = lax.map(
            forward_block, (query_h.reshape(block_count, block_rows, HEAD), seg_blocks)
        )
        return (outs.reshape(bucket_len, HEAD), maxes, sums)

    head_out, row_maxes, row_sums = lax.map(self_forward, (by_head[0], by_head[1], by_head[2]))

    out_blocks = head_out.transpose(1, 0, 2).reshape(seq_count, local_tok, head_cols)
    came = seq_exchange([out_blocks[k] for k in range(seq_count)], seq_count)
    attn_o = jnp.take(jnp.stack(came), order, axis=0).transpose(1, 0, 2).reshape(local_tok, model_width)
    x_two = x_one + matmul(attn_o, full_out)
    n3_float, pull_three = jax.vjp(layer_norm, x_two, ln_gains[3], ln_biases[3])
    n_three = n3_float.astype(jnp.bfloat16)
    cross_q = matmul(n_three, full_cq).astype(jnp.bfloat16).reshape(local_tok, HEADS, HEAD)
    text_kv = matmul(captions[0], full_ckv)
    cross_k = text_kv[:, :model_width].astype(jnp.bfloat16).reshape(-1, HEADS, HEAD)
    cross_v = text_kv[:, model_width:].astype(jnp.bfloat16).reshape(-1, HEADS, HEAD)
    cross_mask = caption_allowed(seg_local, clip_lengths[0], t5_lengths[0])
    cross_scores = jnp.where(
        cross_mask[None],
        jnp.einsum("thd,khd->htk", cross_q, cross_k, preferred_element_type=jnp.float32)
        * score_scale,
        masked_score,
    )
    cross_probs = soft_rows(cross_scores)
    cross_low = cross_probs.astype(jnp.bfloat16)
    cross_o = (
        jnp.einsum("htk,khd->thd", cross_low, cross_v, preferred_element_type=jnp.float32)
        .astype(jnp.bfloat16)
        .reshape(local_tok, model_width)
    )
    x_three = x_two + matmul(cross_o, full_co)
    n2_float, pull_two = jax.vjp(layer_norm, x_three, ln_gains[4], ln_biases[4])
    n_two = n2_float.astype(jnp.bfloat16)

    n_two_all = jnp.concatenate(seq_blocks(n_two, seq_count), axis=0)
    cot_all = jnp.concatenate(seq_blocks(cotangent, seq_count), axis=0)
    up_proj = matmul(n_two_all, part_up)
    act_float, pull_gelu = jax.vjp(gelu_tanh, up_proj)
    act_low = act_float.astype(jnp.bfloat16)
    down_part = matmul(act_low, part_down).reshape(seq_count, local_tok, model_width)
    block_out = (
        x_three + seq_sum([down_part[k] for k in range(seq_count)], seq_count)
    ).astype(jnp.bfloat16)
    grad_down = matmul(act_low.T, cot_all)
    d_act = matmul(cot_all, part_down.T)
    d_up = pull_gelu(d_act)[0].astype(jnp.bfloat16)
    grad_up = matmul(n_two_all.T, d_up)
    d_two_part = matmul(d_up, part_up.T).reshape(seq_count, local_tok, model_width)
    d_n_two = seq_sum([d_two_part[k] for k in range(seq_count)], seq_count)
    back_three_x, gain_four, bias_four = pull_two(d_n_two)
    d_x_three = cotangent.astype(jnp.float32) + back_three_x
    d_co = d_x_three.astype(jnp.bfloat16)
    grad_co = matmul(cross_o.T, d_co)
    d_cross_o = matmul(d_co, full_co.T).astype(jnp.bfloat16).reshape(local_tok, HEADS, HEAD)
    d_cprobs = jnp.einsum("thd,khd->htk", d_cross_o, cross_v, preferred_element_type=jnp.float32)
    d_cscores = (
        cross_probs * (d_cprobs - jnp.sum(d_cprobs * cross_probs, axis=-1, keepdims=True))
    ).astype(jnp.bfloat16)
    d_cross_q = (
        (
            jnp.einsum("htk,khd->thd", d_cscores, cross_k, preferred_element_type=jnp.float32)
            * score_scale
        )
        .astype(jnp.bfloat16)
        .reshape(local_tok, model_width)
    )
    d_cross_k = (
        jnp.einsum("htk,thd->khd", d_cscores, cross_q, preferred_element_type=jnp.float32)
        * score_scale
    )
    d_cross_v = jnp.einsum("htk,thd->khd", cross_low, d_cross_o, preferred_element_type=jnp.float32)
    d_text_kv = jnp.concatenate(
        [d_cross_k.reshape(-1, model_width), d_cross_v.reshape(-1, model_width)], axis=1
    )
    grad_ckv = jnp.dot(
        captions[0].astype(jnp.float32).T,
        d_text_kv,
        precision=lax.Precision.HIGHEST,
        preferred_element_type=jnp.float32,
    )
    grad_cq = matmul(n_three.T, d_cross_q)
    d_n_three = matmul(d_cross_q, full_cq.T)
    back_two_x, gain_three, bias_three = pull_three(d_n_three)
    d_x_two = d_x_three + back_two_x
    d_attn = d_x_two.astype(jnp.bfloat16)
    grad_out = matmul(attn_o.T, d_attn)
    d_attn_o = matmul(d_attn, full_out.T).astype(jnp.bfloat16)

    d_turned = jnp.take(
        d_attn_o.reshape(local_tok, seq_count, head_cols).transpose(1, 0, 2), order, axis=0
    )
    d_came = seq_exchange([d_turned[k] for k in range(seq_count)], seq_count)
    d_by_head = (
        jnp.concatenate(d_came, axis=0).reshape(bucket_len, local_heads, HEAD).transpose(1, 0, 2)
    )

    def self_backward(head_items):
        query_h, key_h, value_h, d_out_h, row_max, row_sum = head_items

        def backward_block(carry, block_items):
            key_total, value_total = carry
            query_b, seg_b, d_out_b, max_b, sum_b = block_items
            scores = block_scores(query_b, seg_b, key_h)
            attn_probs = jnp.exp(scores - max_b) / sum_b
            probs_low = attn_probs.astype(jnp.bfloat16)
            d_probs = matmul(d_out_b, value_h.T)
            d_scores = (
                attn_probs * (d_probs - jnp.sum(d_probs * attn_probs, axis=1, keepdims=True))
            ).astype(jnp.bfloat16)
            d_query = (matmul(d_scores, key_h) * score_scale).astype(jnp.bfloat16)
            key_total = key_total + matmul(d_scores.T, query_b) * score_scale
            value_total = value_total + matmul(probs_low.T, d_out_b)
            return ((key_total, value_total), d_query)

        start = (
            jnp.zeros((bucket_len, HEAD), jnp.float32),
            jnp.zeros((bucket_len, HEAD), jnp.float32),
        )
        (key_total, value_total), d_query_blocks = lax.scan(
            backward_block,
            start,
            (
                query_h.reshape(block_count, block_rows, HEAD),
                seg_blocks,
                d_out_h.reshape(block_count, block_rows, HEAD),
                row_max,
                row_sum,
            ),
        )
        return jnp.stack(
            [
                d_query_blocks.reshape(bucket_len, HEAD),
                key_total.astype(jnp.bfloat16),
                value_total.astype(jnp.bfloat16),
            ]
        )

    d_heads = lax.map(
        self_backward, (by_head[0], by_head[1], by_head[2], d_by_head, row_maxes, row_sums)
    )

    d_parts = d_heads.transpose(1, 2, 0, 3).astype(jnp.float32)
    d_qkv_float, grad_qk_gain, grad_qk_bias = pull_heads((d_parts[0], d_parts[1], d_parts[2]))
    d_qkv = d_qkv_float.astype(jnp.bfloat16)
    grad_qkv = matmul(n_one_all.T, d_qkv)
    d_one_part = matmul(d_qkv, part_qkv.T).reshape(seq_count, local_tok, model_width)
    d_n_one = seq_sum([d_one_part[k] for k in range(seq_count)], seq_count)
    d_shift = d_n_one.astype(jnp.bfloat16)
    d_image = matmul(member.astype(jnp.bfloat16).T, d_shift)
    d_image_all = jnp.sum(lax.all_gather(d_image, ("dp", "seq"), axis=0, tiled=True).reshape(
        dp_count, seq_count, IMGS, model_width
    ), axis=1).reshape(dp_count * IMGS, model_width)
    grad_mod = jnp.dot(
        cond_rows.astype(jnp.float32).T,
        d_image_all,
        precision=lax.Precision.HIGHEST,
        preferred_element_type=jnp.float32,
    )
    back_one_x, gain_one, bias_one = pull_one(d_n_one)
    d_x_one = d_x_two + back_one_x
    d_y = d_x_one.astype(jnp.bfloat16)
    grad_skip_w = matmul(h_zero.T, d_y)
    d_h_zero = matmul(d_y, full_skip.T)
    d_joined, gain_skip, bias_skip = pull_skip(d_h_zero)
    grad_tokens = d_joined[:, :model_width].astype(jnp.bfloat16)
    grad_skip = d_joined[:, model_width:].astype(jnp.bfloat16)
    gain_rows = jnp.stack(
        [gain_skip[:model_width], gain_skip[model_width:], gain_one, gain_three, gain_four]
    )
    bias_rows = jnp.stack([bias_skip[:model_width], bias_skip[model_width:], bias_one, bias_three])
    gain_total, bias_total, ff_bias_total, qk_gain_total, qk_bias_total = lax.psum(
        (gain_rows, bias_rows, bias_four, grad_qk_gain, grad_qk_bias), ("dp", "seq")
    )

    square_grad = jnp.concatenate(
        [g.reshape(dp_count, row_count, model_width) for g in (grad_out, grad_cq, grad_co)]
        + [jnp.zeros((dp_count, pad_rows, model_width), jnp.float32)],
        axis=1,
    ).reshape(-1, model_width)
    square_total = scatter_rows(square_grad, dp_count, seq_count)
    grad_out, grad_cq, grad_co = (
        square_total[i * row_count : (i + 1) * row_count] for i in range(3)
    )
    total_qkv = lax.psum_scatter(
        grad_qkv.astype(jnp.bfloat16), "dp", scatter_dimension=0, tiled=True
    )
    grad_qkv = (
        lax.all_gather(total_qkv, "seq", axis=0)
        .reshape(seq_count, row_count, 3, head_cols)
        .transpose(1, 2, 0, 3)
        .reshape(row_count, 3 * model_width)
        .astype(jnp.float32)
    )
    total_up = lax.psum_scatter(grad_up.astype(jnp.bfloat16), "dp", scatter_dimension=0, tiled=True)
    grad_up = (
        lax.all_gather(total_up, "seq", axis=0)
        .reshape(seq_count, row_count, dp_count, part)
        .transpose(1, 2, 0, 3)
        .reshape(row_count, wide)
        .astype(jnp.float32)
    )
    total_down = lax.psum_scatter(
        grad_down.astype(jnp.bfloat16), "dp", scatter_dimension=0, tiled=True
    )
    grad_down = lax.all_gather(total_down, "seq", axis=0, tiled=True).astype(jnp.float32)
    return (
        block_out,
        grad_tokens,
        grad_skip,
        gain_total,
        bias_total,
        ff_bias_total,
        qk_gain_total,
        qk_bias_total,
        scatter_rows(grad_skip_w, dp_count, seq_count),
        grad_mod,
        grad_qkv,
        grad_out,
        grad_cq,
        scatter_rows(grad_ckv, dp_count, seq_count),
        grad_co,
        grad_up,
        grad_down,
    )


def solution(mesh):
    in_specs = (
        P(("dp", "seq"), None),
        P(("dp", "seq"), None),
        P("dp", None),
        P("dp", None),
        P("dp", None),
        P("dp", None),
        P("dp", None, None),
        P("dp", None, None),
        P(),
        P(),
        P(),
        P(),
        P("dp", None),
        P("dp", None),
        P("dp", None),
        P("dp", None),
        P("dp", None),
        P("dp", None),
        P("dp", None),
        P("dp", None),
        P("dp", None),
        P(("dp", "seq"), None),
    )
    out_specs = (
        P(("dp", "seq"), None),
        P(("dp", "seq"), None),
        P(("dp", "seq"), None),
        P(),
        P(),
        P(),
        P(),
        P(),
        P("dp", None),
        P("dp", None),
        P("dp", None),
        P("dp", None),
        P("dp", None),
        P("dp", None),
        P("dp", None),
        P("dp", None),
        P("dp", None),
    )
    return jax.shard_map(shards, mesh=mesh, in_specs=in_specs, out_specs=out_specs, check_vma=False)
```

```python
import functools
import jax
import jax.numpy as jnp
import numpy as np
from jax import lax
from jax.experimental import pallas as pl
from jax.experimental.pallas import tpu as pltpu
from jax.sharding import PartitionSpec as P

HEADS = 16
HEAD = 88
IMGS = 3
CAP = 333
CLIP_TOK = 77
LANES = 128
LOG2E = 1.4426950408889634
eps_norm = 1e-06
masked_score = -1e30
vmem_bytes = 60 * 1024 * 1024


def dot_nt(left, right):
    return lax.dot_general(
        left, right, (((1,), (1,)), ((), ())), preferred_element_type=jnp.float32
    )


def dot_tn(left, right):
    return lax.dot_general(
        left, right, (((0,), (0,)), ((), ())), preferred_element_type=jnp.float32
    )


def matmul(left, right):
    return jnp.dot(left, right, preferred_element_type=jnp.float32)


def widen(value):
    pad = jnp.zeros((value.shape[0], LANES - HEAD), value.dtype)
    return jnp.concatenate([value, pad], axis=1)


def lane_of(shape):
    return lax.broadcasted_iota(jnp.int32, shape, len(shape) - 1)


def head_norm(value):
    mean = jnp.sum(value, axis=1, keepdims=True) * (1.0 / HEAD)
    center = jnp.where(lane_of(value.shape) < HEAD, value - mean, 0.0)
    spread = jnp.sum(center * center, axis=1, keepdims=True) * (1.0 / HEAD)
    factor = lax.rsqrt(spread + eps_norm)
    return center * factor, factor


def turn(value, cos_t, sin_a, sin_b):
    ahead = pltpu.roll(value, LANES - HEAD // 4, 1)
    behind = pltpu.roll(value, HEAD // 4, 1)
    return value * cos_t + ahead * sin_a + behind * sin_b


def turn_back(value, cos_t, sin_a, sin_b):
    return (
        value * cos_t
        + pltpu.roll(value * sin_a, HEAD // 4, 1)
        + pltpu.roll(value * sin_b, LANES - HEAD // 4, 1)
    )


def prep_kernel(heads, pre_ref, cos_ref, sa_ref, sb_ref, seg_ref, gain_ref, bias_ref, out_ref):
    cos_t, sin_a, sin_b = cos_ref[...], sa_ref[...], sb_ref[...]
    seg = seg_ref[...]
    lane = lane_of(cos_t.shape)
    image = lane - HEAD
    own = jnp.where(image == seg, 1.0, 0.0)
    other = jnp.where((image >= 0) & (image < IMGS) & (image != seg), masked_score, 0.0)
    ones = jnp.where(image == 0, 1.0, 0.0)
    for kind in range(3):
        for head in range(heads):
            at = (kind * heads + head) * LANES
            value = pre_ref[:, at : at + LANES]
            if kind < 2:
                normed, _ = head_norm(value)
                value = normed * gain_ref[kind : kind + 1, :] + bias_ref[kind : kind + 1, :]
                value = turn(value, cos_t, sin_a, sin_b) + (own if kind == 0 else other)
            else:
                value = value + ones
            out_ref[:, at : at + LANES] = value.astype(jnp.bfloat16)


def prep_heads(pre, tables, seg, gains, biases, heads, rows):
    count = pre.shape[0]
    cols = 3 * heads * LANES
    wide = pl.BlockSpec((rows, LANES), lambda i: (i, 0))
    return pl.pallas_call(
        functools.partial(prep_kernel, heads),
        grid=(count // rows,),
        in_specs=[
            pl.BlockSpec((rows, pre.shape[1]), lambda i: (i, 0)),
            wide,
            wide,
            wide,
            pl.BlockSpec((rows, 1), lambda i: (i, 0)),
            pl.BlockSpec((2, LANES), lambda i: (0, 0)),
            pl.BlockSpec((2, LANES), lambda i: (0, 0)),
        ],
        out_specs=pl.BlockSpec((rows, cols), lambda i: (i, 0)),
        out_shape=jax.ShapeDtypeStruct((count, cols), jnp.bfloat16),
        compiler_params=pltpu.CompilerParams(vmem_limit_bytes=vmem_bytes),
        cost_estimate=pl.CostEstimate(
            flops=20 * count * cols, bytes_accessed=8 * count * cols, transcendentals=0
        ),
    )(pre, *tables, seg, gains, biases)


score_shift = 10.0


def self_exp(scores):
    return jnp.exp2(scores * (HEAD ** (-0.5) * LOG2E) - score_shift * LOG2E)


def self_forward_kernel(heads, q_ref, k_ref, v_ref, out_ref, inv_ref):
    outs = []
    invs = []
    for head in range(heads):
        cols = slice(head * LANES, (head + 1) * LANES)
        exps = self_exp(dot_nt(k_ref[:, cols], q_ref[:, cols])).astype(jnp.bfloat16)
        total = dot_tn(v_ref[:, cols], exps)
        inverse = 1.0 / total[HEAD : HEAD + 1, :]
        invs.append(inverse)
        outs.append((total * inverse).T[:, :HEAD].astype(jnp.bfloat16))
    out_ref[...] = jnp.concatenate(outs, axis=1)
    for head in range(heads):
        inv_ref[head : head + 1, :] = invs[head]


def self_forward(packed, heads, rows):
    count = packed.shape[0]
    cols = heads * LANES
    return pl.pallas_call(
        functools.partial(self_forward_kernel, heads),
        grid=(count // rows,),
        in_specs=[
            pl.BlockSpec((rows, cols), lambda i: (i, 0)),
            pl.BlockSpec((count, cols), lambda i: (0, 1)),
            pl.BlockSpec((count, cols), lambda i: (0, 2)),
        ],
        out_specs=[
            pl.BlockSpec((rows, heads * HEAD), lambda i: (i, 0)),
            pl.BlockSpec((heads, rows), lambda i: (0, i)),
        ],
        out_shape=[
            jax.ShapeDtypeStruct((count, heads * HEAD), jnp.bfloat16),
            jax.ShapeDtypeStruct((heads, count), jnp.float32),
        ],
        compiler_params=pltpu.CompilerParams(vmem_limit_bytes=vmem_bytes),
        cost_estimate=pl.CostEstimate(
            flops=4 * count * count * cols,
            bytes_accessed=8 * count * cols,
            transcendentals=count * count * heads,
        ),
    )(packed, packed, packed)


def self_backward_kernel(heads, blocks, q_ref, k_ref, v_ref, d_ref, inv_ref, dq_ref, dk_ref, dv_ref, key_sum, value_sum):
    step = pl.program_id(0)

    @pl.when(step == 0)
    def _():
        key_sum[...] = jnp.zeros_like(key_sum)
        value_sum[...] = jnp.zeros_like(value_sum)

    scale = HEAD ** (-0.5)
    for head in range(heads):
        cols = slice(head * LANES, (head + 1) * LANES)
        d_out = widen(d_ref[:, head * HEAD : (head + 1) * HEAD])
        query, key = q_ref[:, cols], k_ref[:, cols]
        probs = self_exp(dot_nt(key, query)) * inv_ref[head : head + 1, :]
        d_probs = dot_nt(v_ref[:, cols], d_out)
        weight = jnp.sum(probs * d_probs, axis=0, keepdims=True)
        d_scores = (probs * (d_probs - weight)).astype(jnp.bfloat16)
        value_sum[:, cols] += matmul(probs.astype(jnp.bfloat16), d_out)
        key_sum[:, cols] += matmul(d_scores, query)
        dq_ref[:, cols] = (dot_tn(d_scores, key) * scale).astype(jnp.bfloat16)

    @pl.when(step == blocks - 1)
    def _():
        dk_ref[...] = (key_sum[...] * scale).astype(jnp.bfloat16)
        dv_ref[...] = value_sum[...].astype(jnp.bfloat16)


def self_backward(packed, d_out, inverse, heads, rows):
    count = packed.shape[0]
    cols = heads * LANES
    blocks = count // rows
    whole = pl.BlockSpec((count, cols), lambda i: (0, 0))
    return pl.pallas_call(
        functools.partial(self_backward_kernel, heads, blocks),
        grid=(blocks,),
        in_specs=[
            pl.BlockSpec((rows, cols), lambda i: (i, 0)),
            pl.BlockSpec((count, cols), lambda i: (0, 1)),
            pl.BlockSpec((count, cols), lambda i: (0, 2)),
            pl.BlockSpec((rows, heads * HEAD), lambda i: (i, 0)),
            pl.BlockSpec((heads, rows), lambda i: (0, i)),
        ],
        out_specs=[pl.BlockSpec((rows, cols), lambda i: (i, 0)), whole, whole],
        out_shape=[jax.ShapeDtypeStruct((count, cols), jnp.bfloat16)] * 3,
        scratch_shapes=[pltpu.VMEM((count, cols), jnp.float32)] * 2,
        compiler_params=pltpu.CompilerParams(vmem_limit_bytes=vmem_bytes),
        cost_estimate=pl.CostEstimate(
            flops=10 * count * count * cols,
            bytes_accessed=14 * count * cols,
            transcendentals=count * count * heads,
        ),
    )(packed, packed, packed, d_out, inverse)


def prep_back_kernel(heads, pre_ref, dq_ref, dk_ref, dv_ref, cos_ref, sa_ref, sb_ref, gain_ref, out_ref, dg_ref, db_ref):
    step = pl.program_id(0)

    @pl.when(step == 0)
    def _():
        dg_ref[...] = jnp.zeros_like(dg_ref)
        db_ref[...] = jnp.zeros_like(db_ref)

    cos_t, sin_a, sin_b = cos_ref[...], sa_ref[...], sb_ref[...]
    live = lane_of(cos_t.shape) < HEAD
    for kind, d_ref in enumerate((dq_ref, dk_ref)):
        gain = gain_ref[kind : kind + 1, :]
        gain_sum = jnp.zeros((1, LANES), jnp.float32)
        bias_sum = jnp.zeros((1, LANES), jnp.float32)
        for head in range(heads):
            at = (kind * heads + head) * LANES
            normed, factor = head_norm(pre_ref[:, at : at + LANES])
            given = jnp.where(live, d_ref[:, head * LANES : (head + 1) * LANES].astype(jnp.float32), 0.0)
            d_normed = turn_back(given, cos_t, sin_a, sin_b)
            gain_sum = gain_sum + jnp.sum(d_normed * normed, axis=0, keepdims=True)
            bias_sum = bias_sum + jnp.sum(d_normed, axis=0, keepdims=True)
            scaled = d_normed * gain
            mean = jnp.sum(scaled, axis=1, keepdims=True) * (1.0 / HEAD)
            slope = jnp.sum(scaled * normed, axis=1, keepdims=True) * (1.0 / HEAD)
            result = jnp.where(live, factor * (scaled - mean - normed * slope), 0.0)
            out_ref[:, at : at + LANES] = result.astype(jnp.bfloat16)
        dg_ref[kind : kind + 1, :] += gain_sum
        db_ref[kind : kind + 1, :] += bias_sum
    out_ref[:, 2 * heads * LANES :] = dv_ref[...]


def prep_back(pre, d_query, d_key, d_value, tables, gains, heads, rows):
    count = pre.shape[0]
    cols = heads * LANES
    wide = pl.BlockSpec((rows, LANES), lambda i: (i, 0))
    headed = pl.BlockSpec((rows, cols), lambda i: (i, 0))
    small = pl.BlockSpec((2, LANES), lambda i: (0, 0))
    return pl.pallas_call(
        functools.partial(prep_back_kernel, heads),
        grid=(count // rows,),
        in_specs=[
            pl.BlockSpec((rows, pre.shape[1]), lambda i: (i, 0)),
            headed,
            headed,
            headed,
            wide,
            wide,
            wide,
            small,
        ],
        out_specs=[pl.BlockSpec((rows, pre.shape[1]), lambda i: (i, 0)), small, small],
        out_shape=[
            jax.ShapeDtypeStruct(pre.shape, jnp.bfloat16),
            jax.ShapeDtypeStruct((2, LANES), jnp.float32),
            jax.ShapeDtypeStruct((2, LANES), jnp.float32),
        ],
        compiler_params=pltpu.CompilerParams(vmem_limit_bytes=vmem_bytes),
        cost_estimate=pl.CostEstimate(
            flops=60 * count * cols, bytes_accessed=30 * count * cols, transcendentals=0
        ),
    )(pre, d_query, d_key, d_value, *tables, gains)


def cross_key(kv_ref, first, head, keys, penalty):
    key = widen(kv_ref[pl.ds(first, keys), head * HEAD : (head + 1) * HEAD])
    return jnp.where(lane_of(key.shape) == HEAD, penalty, key)


def cross_value(kv_ref, first, head, keys, width):
    at = width + head * HEAD
    value = widen(kv_ref[pl.ds(first, keys), at : at + HEAD])
    return jnp.where(lane_of(value.shape) == HEAD, jnp.bfloat16(1), value)


def cross_query(q_ref, head):
    query = widen(q_ref[:, head * HEAD : (head + 1) * HEAD])
    return jnp.where(lane_of(query.shape) == HEAD, jnp.bfloat16(1), query)


cross_factor = HEAD ** (-0.5) * LOG2E


def cross_forward_kernel(heads, keys, span_ref, q_ref, kv_ref, pen_ref, seg_ref, out_ref, top_ref, inv_ref, turned):
    width = heads * HEAD

    def image(index, carry):
        first = pl.multiple_of(index * keys, 16)
        penalty = pen_ref[pl.ds(first, keys), :]
        member = seg_ref[...] == index
        for head in range(heads):
            key = cross_key(kv_ref, first, head, keys, penalty)
            scores = dot_nt(key, cross_query(q_ref, head)) * cross_factor
            top = jnp.max(scores, axis=0, keepdims=True)
            exps = jnp.exp2(scores - top).astype(jnp.bfloat16)
            total = dot_tn(cross_value(kv_ref, first, head, keys, width), exps)
            inverse = 1.0 / total[HEAD : HEAD + 1, :]
            at = slice(head * LANES, (head + 1) * LANES)
            turned[at, :] = jnp.where(member, total * inverse, turned[at, :])
            top_ref[head : head + 1, :] = jnp.where(member, top, top_ref[head : head + 1, :])
            inv_ref[head : head + 1, :] = jnp.where(member, inverse, inv_ref[head : head + 1, :])
        return carry

    lax.fori_loop(span_ref[0], span_ref[1] + 1, image, 0)
    out_ref[...] = jnp.concatenate(
        [
            turned[head * LANES : (head + 1) * LANES, :].T[:, :HEAD].astype(jnp.bfloat16)
            for head in range(heads)
        ],
        axis=1,
    )


def cross_forward(query, text_kv, penalty, seg_row, span):
    count, width = query.shape
    heads = width // HEAD
    keys = text_kv.shape[0] // IMGS
    vmem = pl.BlockSpec(memory_space=pltpu.VMEM)
    return pl.pallas_call(
        functools.partial(cross_forward_kernel, heads, keys),
        in_specs=[pl.BlockSpec(memory_space=pltpu.SMEM)] + [vmem] * 4,
        out_specs=[vmem] * 3,
        out_shape=[
            jax.ShapeDtypeStruct((count, width), jnp.bfloat16),
            jax.ShapeDtypeStruct((heads, count), jnp.float32),
            jax.ShapeDtypeStruct((heads, count), jnp.float32),
        ],
        scratch_shapes=[pltpu.VMEM((heads * LANES, count), jnp.float32)],
        compiler_params=pltpu.CompilerParams(vmem_limit_bytes=vmem_bytes),
        cost_estimate=pl.CostEstimate(
            flops=8 * count * keys * heads * LANES,
            bytes_accessed=2 * text_kv.size + 8 * query.size,
            transcendentals=2 * count * keys * heads,
        ),
    )(span, query, text_kv, penalty, seg_row)


def cross_backward_kernel(heads, keys, span_ref, q_ref, kv_ref, pen_ref, seg_ref, top_ref, inv_ref, d_ref, dq_ref, dkv_ref, turned):
    width = heads * HEAD
    scale = HEAD ** (-0.5)
    turned[...] = jnp.zeros_like(turned)
    dkv_ref[...] = jnp.zeros_like(dkv_ref)

    def image(index, carry):
        first = pl.multiple_of(index * keys, 16)
        penalty = pen_ref[pl.ds(first, keys), :]
        member = seg_ref[...] == index
        d_keys, d_values = [], []
        for head in range(heads):
            key = cross_key(kv_ref, first, head, keys, penalty)
            query = cross_query(q_ref, head)
            d_out = widen(d_ref[:, head * HEAD : (head + 1) * HEAD])
            top = jnp.where(member, top_ref[head : head + 1, :], -masked_score)
            scores = dot_nt(key, query) * cross_factor
            probs = jnp.exp2(scores - top) * inv_ref[head : head + 1, :]
            d_probs = dot_nt(cross_value(kv_ref, first, head, keys, width), d_out)
            weight = jnp.sum(probs * d_probs, axis=0, keepdims=True)
            d_scores = (probs * (d_probs - weight)).astype(jnp.bfloat16)
            d_values.append(matmul(probs.astype(jnp.bfloat16), d_out)[:, :HEAD].astype(jnp.bfloat16))
            d_keys.append((matmul(d_scores, query) * scale)[:, :HEAD].astype(jnp.bfloat16))
            at = slice(head * LANES, (head + 1) * LANES)
            turned[at, :] += dot_tn(key, d_scores)
        dkv_ref[pl.ds(first, keys), :] = jnp.concatenate(d_keys + d_values, axis=1)
        return carry

    lax.fori_loop(span_ref[0], span_ref[1] + 1, image, 0)
    dq_ref[...] = jnp.concatenate(
        [
            (turned[head * LANES : (head + 1) * LANES, :] * scale).T[:, :HEAD].astype(jnp.bfloat16)
            for head in range(heads)
        ],
        axis=1,
    )


def cross_backward(query, text_kv, penalty, seg_row, span, top, inverse, d_out):
    count, width = query.shape
    heads = width // HEAD
    keys = text_kv.shape[0] // IMGS
    vmem = pl.BlockSpec(memory_space=pltpu.VMEM)
    return pl.pallas_call(
        functools.partial(cross_backward_kernel, heads, keys),
        in_specs=[pl.BlockSpec(memory_space=pltpu.SMEM)] + [vmem] * 7,
        out_specs=[vmem] * 2,
        out_shape=[
            jax.ShapeDtypeStruct((count, width), jnp.bfloat16),
            jax.ShapeDtypeStruct(text_kv.shape, jnp.bfloat16),
        ],
        scratch_shapes=[pltpu.VMEM((heads * LANES, count), jnp.float32)],
        compiler_params=pltpu.CompilerParams(vmem_limit_bytes=vmem_bytes),
        cost_estimate=pl.CostEstimate(
            flops=20 * count * keys * heads * LANES,
            bytes_accessed=4 * text_kv.size + 8 * query.size,
            transcendentals=2 * count * keys * heads,
        ),
    )(span, query, text_kv, penalty, seg_row, top, inverse, d_out)


def layer_norm(values, norm_gain, norm_bias):
    center = values - jnp.mean(values, axis=-1, keepdims=True)
    spread = jnp.mean(center * center, axis=-1, keepdims=True)
    return center * lax.rsqrt(spread + eps_norm) * norm_gain + norm_bias


def gelu_tanh(values):
    return (
        0.5
        * values
        * (1.0 + jnp.tanh(0.7978845608028654 * (values + 0.044715 * values * values * values)))
    )


def silu_gate(values):
    return values * jax.nn.sigmoid(values)


def grid_positions(seg_all, widths, first_tok, tok_count):
    images = jnp.arange(IMGS, dtype=jnp.int32)
    starts = jnp.sum((seg_all[None, :] < images[:, None]).astype(jnp.int32), axis=1)
    seg_part = lax.dynamic_slice_in_dim(seg_all, first_tok, tok_count)
    member = seg_part[:, None] == images[None, :]
    start_tok = jnp.sum(jnp.where(member, starts[None, :], 0), axis=1)
    width_tok = jnp.sum(jnp.where(member, widths[None, :], 0), axis=1)
    in_image = first_tok + jnp.arange(tok_count, dtype=jnp.int32) - start_tok
    return (
        seg_part,
        member,
        (in_image // width_tok).astype(jnp.float32),
        (in_image % width_tok).astype(jnp.float32),
    )


def swap(value, axis, mask):
    count = lax.axis_size(axis)
    return lax.ppermute(value, axis, [(rank, rank ^ mask) for rank in range(count)])


def blocks_of(block, axis):
    count = lax.axis_size(axis)
    held = {0: block}
    bit = count // 2
    while bit:
        for mask in list(held):
            held[mask | bit] = swap(held[mask], axis, bit)
        bit //= 2
    return [held[mask] for mask in range(count)]


def sum_parts(parts, axis, kind):
    count = lax.axis_size(axis)
    held = dict(enumerate(parts))
    bit = 1
    while bit < count:
        for mask in [m for m in held if m & bit]:
            came = swap(held.pop(mask).astype(kind), axis, bit)
            held[mask ^ bit] = held[mask ^ bit] + came.astype(jnp.float32)
        bit *= 2
    return held[0]


def gather_small(value, axis):
    bit = 1
    while bit < lax.axis_size(axis):
        value = jnp.concatenate([value, swap(value, axis, bit)])
        bit *= 2
    return value


def scatter_small(value, axis):
    bit = lax.axis_size(axis) // 2
    while bit:
        half = value.shape[0] // 2
        value = value[:half] + swap(value[half:], axis, bit)
        bit //= 2
    return value


def sum_all(value, axis):
    bit = 1
    while bit < lax.axis_size(axis):
        value = value + swap(value, axis, bit)
        bit *= 2
    return value


def exchange(parts, axis):
    return [parts[0]] + [swap(parts[mask], axis, mask) for mask in range(1, len(parts))]


def in_order(blocks, rank):
    stacked = jnp.stack(blocks)
    return [
        lax.dynamic_index_in_dim(stacked, rank ^ place, 0, keepdims=False)
        for place in range(len(blocks))
    ]


def share_of(rows, seq_count):
    if rows >= 16 * seq_count:
        return -(-rows // (16 * seq_count)) * 16
    return -(-rows // seq_count)


def rope_tables(row_pos, col_pos):
    lane = np.arange(LANES)
    half, quarter = HEAD // 2, HEAD // 4
    live = lane < HEAD
    index = lane % half % quarter
    frequency = np.where(live, 10000.0 ** (-(index * 4.0 / HEAD)), 0.0).astype(np.float32)
    front = live & (lane % half < quarter)
    back = live & (lane % half >= quarter)
    angle = jnp.where((lane < half)[None], row_pos[:, None], col_pos[:, None]) * frequency[None]
    sine = jnp.sin(angle)
    return (
        jnp.where(live[None], jnp.cos(angle), 0.0),
        jnp.where(front[None], -sine, 0.0),
        jnp.where(back[None], sine, 0.0),
    )


def caption_penalty(clip_len, t5_len, keys):
    slot = jnp.arange(keys, dtype=jnp.int32)[None]
    clip_live = (slot < CLIP_TOK) & (slot < clip_len[:, None])
    t5_live = (slot >= CLIP_TOK) & (slot < CAP) & (slot - CLIP_TOK < t5_len[:, None])
    return (
        jnp.where(clip_live | t5_live, 0.0, masked_score).astype(jnp.bfloat16).reshape(-1, 1)
    )


def piece_kernel(heads, ranks_ref, *refs):
    out = refs[-1]
    for mask, piece in enumerate(refs[:-1]):

        @pl.when(pl.program_id(0) == mask)
        def _(piece=piece):
            if not heads:
                out[...] = piece[...]
            for head in range(heads):
                out[:, head * LANES : (head + 1) * LANES] = widen(
                    piece[:, head * HEAD : (head + 1) * HEAD]
                )


def place_pieces(pieces, ranks, heads=0):
    count = len(pieces)
    rows, cols = pieces[0].shape
    out_cols = heads * LANES if heads else cols
    return pl.pallas_call(
        functools.partial(piece_kernel, heads),
        grid_spec=pltpu.PrefetchScalarGridSpec(
            num_scalar_prefetch=1,
            grid=(count,),
            in_specs=[pl.BlockSpec((rows, cols), lambda i, ranks: (0, 0))] * count,
            out_specs=pl.BlockSpec((rows, out_cols), lambda i, ranks: (ranks[0] ^ i, 0)),
        ),
        out_shape=jax.ShapeDtypeStruct((count * rows, out_cols), pieces[0].dtype),
        compiler_params=pltpu.CompilerParams(vmem_limit_bytes=vmem_bytes),
        cost_estimate=pl.CostEstimate(
            flops=0, bytes_accessed=4 * count * rows * out_cols, transcendentals=0
        ),
    )(ranks, *pieces)


def pick_kernel(moves, ranks_ref, source, out):
    for place, moved in enumerate(moves):

        @pl.when(ranks_ref[1] == place)
        def _(moved=moved):
            for first, at, size in moved:
                out[:, at : at + size] = source[:, first : first + size]


def pick_columns(weight, ranks, moves):
    cols = sum(size for _, _, size in moves[0])
    vmem = pl.BlockSpec(memory_space=pltpu.VMEM)
    return pl.pallas_call(
        functools.partial(pick_kernel, moves),
        in_specs=[pl.BlockSpec(memory_space=pltpu.SMEM), vmem],
        out_specs=vmem,
        out_shape=jax.ShapeDtypeStruct((weight.shape[0], cols), weight.dtype),
        compiler_params=pltpu.CompilerParams(vmem_limit_bytes=vmem_bytes),
    )(ranks, weight)


def put_kernel(moves, ranks_ref, *refs):
    out = refs[-1]
    for mask, block in enumerate(refs[:-1]):
        for place, moved in enumerate(moves):

            @pl.when((ranks_ref[1] ^ mask) == place)
            def _(block=block, moved=moved):
                for first, at, size in moved:
                    out[:, at : at + size] = block[:, first : first + size].astype(out.dtype)


def put_columns(blocks, ranks, moves, cols, kind):
    vmem = pl.BlockSpec(memory_space=pltpu.VMEM)
    return pl.pallas_call(
        functools.partial(put_kernel, moves),
        in_specs=[pl.BlockSpec(memory_space=pltpu.SMEM)] + [vmem] * len(blocks),
        out_specs=vmem,
        out_shape=jax.ShapeDtypeStruct((blocks[0].shape[0], cols), kind),
        compiler_params=pltpu.CompilerParams(vmem_limit_bytes=vmem_bytes),
    )(ranks, *blocks)


def quarter_kernel(row_counts, shares, ranks_ref, *refs):
    outs = refs[-len(row_counts) :]
    quarters = refs[: -len(row_counts)]
    seq_count = len(quarters) * (quarters[0].shape[1] // sum(shares))
    for mask in range(seq_count):
        quarter = quarters[mask % len(quarters)]
        base = mask // len(quarters) * sum(shares)
        for place in range(seq_count):

            @pl.when((ranks_ref[1] ^ mask) == place)
            def _(quarter=quarter, place=place, base=base):
                first = base
                for out, rows, share in zip(outs, row_counts, shares):
                    size = min(share, rows - place * share)
                    if size > 0:
                        at = place * share
                        out[at : at + size, :] = quarter[0, first : first + size, :]
                    first += share


def place_quarters(quarters, ranks, row_counts, shares):
    dp_count, held, cols = quarters[0].shape
    return pl.pallas_call(
        functools.partial(quarter_kernel, row_counts, shares),
        grid_spec=pltpu.PrefetchScalarGridSpec(
            num_scalar_prefetch=1,
            grid=(dp_count,),
            in_specs=[pl.BlockSpec((1, held, cols), lambda i, ranks: (i, 0, 0))] * len(quarters),
            out_specs=[
                pl.BlockSpec((rows, cols), lambda i, ranks: (ranks[0] ^ i, 0))
                for rows in row_counts
            ],
        ),
        out_shape=[
            jax.ShapeDtypeStruct((dp_count * rows, cols), quarters[0].dtype)
            for rows in row_counts
        ],
        compiler_params=pltpu.CompilerParams(vmem_limit_bytes=vmem_bytes),
        cost_estimate=pl.CostEstimate(
            flops=0, bytes_accessed=4 * dp_count * sum(row_counts) * cols, transcendentals=0
        ),
    )(ranks, *quarters)


def bits_below(count):
    return [1 << place for place in reversed(range(count.bit_length() - 1))]


class Gather:
    def __init__(self, own, stages):
        self.stages = list(stages)
        self.start(own)

    def start(self, own):
        self.axis, bits = self.stages.pop(0)
        self.masks = [0]
        for bit in reversed(bits):
            self.masks += [mask | bit for mask in self.masks]
        self.held, self.came, self.level = {0: own}, None, 0
        self.send()

    def send(self):
        self.level += 1
        masks = [m for m in self.masks if bin(m).count("1") == self.level]
        if masks:
            self.came = {
                m: swap(self.held[m & (m - 1)], self.axis, m & -m)
                for m in sorted(masks, key=lambda m: (m & -m, m), reverse=True)
            }
        elif self.stages:
            self.start(jnp.stack([self.held[m] for m in self.masks]))

    def step(self):
        if self.came is None:
            return
        self.held.update(self.came)
        self.came = None
        self.send()

    def finish(self):
        while self.came is not None:
            self.came = lax.optimization_barrier(self.came)
            self.step()
        return [self.held[m] for m in self.masks]


def own_shares(weights, ranks):
    seq_count = lax.axis_size("seq")
    shares = [share_of(w.shape[0], seq_count) for w in weights]
    return jnp.concatenate(
        [
            lax.dynamic_slice_in_dim(
                jnp.pad(w, ((0, share * seq_count - w.shape[0]), (0, 0))), ranks[1] * share, share
            )
            for w, share in zip(weights, shares)
        ]
    )


def aligned(rows):
    return rows % 16 == 0 and rows >= 16 * lax.axis_size("seq")


def widen_heads(whole, heads):
    return jnp.pad(
        whole.reshape(-1, heads, HEAD), ((0, 0), (0, 0), (0, LANES - HEAD))
    ).reshape(-1, heads * LANES)


def gather_seq(total, rank):
    return in_order(blocks_of(total, "seq"), rank)


class Scatter:
    def __init__(self, grad, ranks, last=0, shared=True):
        dp_count, seq_count = lax.axis_size("dp"), lax.axis_size("seq")
        self.rows = grad.shape[0] // dp_count
        self.ranks = ranks
        low = grad.astype(jnp.bfloat16).reshape(dp_count, self.rows, -1)
        if shared:
            share = share_of(self.rows, seq_count)
            low = jnp.pad(low, ((0, 0), (0, share * seq_count - self.rows), (0, 0)))
            self.held = low.reshape(dp_count, seq_count, share, -1)
        else:
            self.held = low[:, None]
        over_seq, over_dp = [], []
        bit = 1
        while shared and bit < seq_count:
            over_seq.append(("seq", bit, ranks[1], 1))
            bit *= 2
        bit = 1
        while bit < dp_count:
            over_dp.append(("dp", bit, ranks[0], 0))
            bit *= 2
        first = len(over_seq) - last
        self.todo = over_seq[:first] + over_dp + over_seq[first:]
        self.came = None
        self.send()

    def send(self):
        if not self.todo:
            return
        axis, bit, rank, dim = self.todo.pop(0)
        shape = self.held.shape
        split = self.held.reshape(shape[:dim] + (shape[dim] // 2, 2) + shape[dim + 1 :])
        mine = (rank // bit) % 2
        self.held = lax.dynamic_index_in_dim(split, mine, dim + 1, keepdims=False)
        give = lax.dynamic_index_in_dim(split, 1 - mine, dim + 1, keepdims=False)
        self.came = swap(give, axis, bit)

    def step(self):
        if self.came is None:
            return
        total = self.held.astype(jnp.float32) + self.came.astype(jnp.float32)
        self.held, self.came = total.astype(jnp.bfloat16), None
        self.send()

    def total(self):
        while self.came is not None:
            self.step()
        return self.held.reshape(self.held.shape[2:])

    def finish(self):
        blocks = gather_seq(self.total(), self.ranks[1])
        return jnp.concatenate(blocks, axis=0)[: self.rows].astype(jnp.float32)


def advance(value, scatters):
    active = [s for s in scatters if s.came is not None]
    value, came = lax.optimization_barrier((value, [s.came for s in active]))
    for scatter, arrived in zip(active, came):
        scatter.came = arrived
        scatter.step()
    return value


def shards(
    tokens,
    skip,
    segment_ids,
    grid_widths,
    clip_lengths,
    t5_lengths,
    timestep,
    captions,
    ln_gains,
    ln_biases,
    qk_gains,
    qk_biases,
    w_skip,
    w_mod,
    w_qkv,
    w_out,
    w_cq,
    w_ckv,
    w_co,
    w_up,
    w_down,
    cotangent,
):
    local_tok = tokens.shape[0]
    model_width = tokens.shape[1]
    seq_count = lax.axis_size("seq")
    dp_count = lax.axis_size("dp")
    seq_rank = lax.axis_index("seq")
    dp_rank = lax.axis_index("dp")
    ranks = jnp.stack([dp_rank, seq_rank])
    bucket_len = local_tok * seq_count
    local_heads = HEADS // seq_count
    head_cols = local_heads * HEAD
    wide = w_up.shape[1]
    part = wide // (dp_count * seq_count)
    local_wide = part * dp_count
    row_count = w_mod.shape[0]
    skip_rows = w_skip.shape[0]
    order = seq_rank ^ jnp.arange(seq_count, dtype=jnp.int32)
    seq_range = range(seq_count)

    up_moves = [
        [(r * seq_count * part + j * part, r * part, part) for r in range(dp_count)]
        for j in seq_range
    ]
    qkv_moves = [
        [(kind * model_width + j * head_cols, kind * head_cols, head_cols) for kind in range(3)]
        for j in seq_range
    ]
    own_skip = lax.dynamic_slice_in_dim(w_skip, seq_rank * head_cols, head_cols, axis=1)
    dp_bits, seq_bits = bits_below(dp_count), bits_below(seq_count)
    skip_way = Gather(own_skip, [("dp", dp_bits)]) if aligned(skip_rows) else None
    joined = jnp.concatenate([tokens, skip], axis=1).astype(jnp.float32)
    h_float, pull_skip = jax.vjp(
        layer_norm, joined, ln_gains[0:2].reshape(-1), ln_biases[0:2].reshape(-1)
    )
    h_zero = h_float.astype(jnp.bfloat16)
    own_qkv = pick_columns(w_qkv, ranks, qkv_moves)
    own_square = own_shares([w_out, w_cq, w_co], ranks)
    own_ckv = own_shares([w_ckv], ranks)
    first_ways = [] if skip_way is None else [skip_way]
    h_zero, own_qkv, own_square, own_ckv = advance(
        (h_zero, own_qkv, own_square, own_ckv), first_ways
    )
    own_up = pick_columns(w_up, ranks, up_moves)
    h_way = Gather(h_zero, [("seq", seq_bits)])
    ways = []
    if aligned(row_count):
        qkv_way = Gather(own_qkv, [("dp", dp_bits)])
        square_way = Gather(own_square, [("dp", dp_bits), ("seq", seq_bits)])
        ways = [qkv_way, square_way]
    if aligned(w_ckv.shape[0]):
        ckv_way = Gather(
            own_ckv, [("seq", seq_bits[:-1]), ("dp", dp_bits), ("seq", seq_bits[-1:])]
        )
        ways.append(ckv_way)
    pieces = skip_way.finish() if skip_way else []
    pieces, own_up = advance((pieces, own_up), [h_way] + ways)
    if skip_way:
        part_skip = place_pieces(pieces, ranks)
    else:
        part_skip = lax.all_gather(own_skip, "dp", axis=0, tiled=True)
    h_all = jnp.concatenate(h_way.finish(), axis=0)
    x_cols = matmul(h_all, part_skip).astype(jnp.bfloat16).reshape(seq_count, local_tok, head_cols)
    x_one = jnp.concatenate(
        in_order(exchange([x_cols[k] for k in seq_range], "seq"), seq_rank), axis=1
    ).astype(jnp.float32)

    seg_all = segment_ids[0]
    seg_local, member, _, _ = grid_positions(
        seg_all, grid_widths[0], seq_rank * local_tok, local_tok
    )
    _, _, row_all, col_all = grid_positions(seg_all, grid_widths[0], 0, bucket_len)

    def reorder(values):
        return jnp.take(values.reshape(seq_count, local_tok), order, axis=0).reshape(-1)

    tables = rope_tables(reorder(row_all), reorder(col_all))
    seg_column = reorder(seg_all)[:, None]
    lane_pad = ((0, 0), (0, LANES - HEAD))
    head_gains, head_biases = jnp.pad(qk_gains, lane_pad), jnp.pad(qk_biases, lane_pad)

    cond = silu_gate(timestep[0].astype(jnp.float32)).astype(jnp.bfloat16)
    cond_all = gather_small(cond, "dp")
    cond_rows = lax.dynamic_slice_in_dim(cond_all, dp_rank * row_count, row_count, axis=1)
    shifts = scatter_small(matmul(cond_rows, w_mod), "dp")
    time_shift = jnp.sum(jnp.where(member[:, :, None], shifts[None], 0.0), axis=1)

    keys = -(-CAP // 16) * 16
    caption_rows = jnp.pad(
        captions[0].reshape(IMGS, CAP, -1), ((0, 0), (0, keys - CAP), (0, 0))
    ).reshape(IMGS * keys, -1)
    penalty = caption_penalty(clip_lengths[0], t5_lengths[0], keys)
    x_one, tables, seg_column, caption_rows, penalty, time_shift = advance(
        (x_one, tables, seg_column, caption_rows, penalty, time_shift), ways
    )
    n_float, pull_one = jax.vjp(layer_norm, x_one, ln_gains[2], ln_biases[2])
    n_one = (n_float + time_shift).astype(jnp.bfloat16)
    n_one_blocks, own_up, w_down = advance((blocks_of(n_one, "seq"), own_up, w_down), ways)
    part_up = lax.all_gather(own_up, "dp", axis=0, tiled=True)
    own_down = lax.dynamic_slice_in_dim(w_down, seq_rank * part, part)
    part_down = lax.all_gather(own_down, "dp", axis=0, tiled=True)
    if ways:
        part_qkv = place_pieces(qkv_way.finish(), ranks, 3 * local_heads)
    else:
        part_qkv = widen_heads(lax.all_gather(own_qkv, "dp", axis=0, tiled=True), 3 * local_heads)
    n_one_all = jnp.concatenate(n_one_blocks, axis=0)
    qkv_pre = matmul(n_one_all, part_qkv)
    packed = prep_heads(qkv_pre, tables, seg_column, head_gains, head_biases, local_heads, 256)
    head_out, inverse = self_forward(packed, local_heads, 256)
    head_out = advance(head_out, ways)
    out_blocks = head_out.reshape(seq_count, local_tok, head_cols)
    attn_o = jnp.concatenate(
        in_order(exchange([out_blocks[k] for k in seq_range], "seq"), seq_rank), axis=1
    )
    attn_o, part_up = advance((attn_o, part_up), ways)
    if aligned(w_ckv.shape[0]):
        ckv_rows = w_ckv.shape[0]
        quarters = [q.reshape(dp_count, -1, w_ckv.shape[1]) for q in ckv_way.finish()]
        (full_ckv,) = place_quarters(quarters, ranks, [ckv_rows], [share_of(ckv_rows, seq_count)])
    else:
        full_ckv = lax.all_gather(w_ckv, "dp", axis=0, tiled=True)
    if ways:
        full_out, full_cq, full_co = place_quarters(
            square_way.finish(), ranks, [row_count] * 3, [share_of(row_count, seq_count)] * 3
        )
    else:
        full_out, full_cq, full_co = (
            lax.all_gather(w, "dp", axis=0, tiled=True) for w in (w_out, w_cq, w_co)
        )
    x_two = x_one + matmul(attn_o, full_out)
    n3_float, pull_three = jax.vjp(layer_norm, x_two, ln_gains[3], ln_biases[3])
    n_three = n3_float.astype(jnp.bfloat16)
    n_three, cotangent = lax.optimization_barrier((n_three, cotangent))
    cross_q = matmul(n_three, full_cq).astype(jnp.bfloat16)
    text_kv = matmul(caption_rows, full_ckv).astype(jnp.bfloat16)
    seg_row = seg_local[None]
    span = jnp.stack([seg_local[0], seg_local[-1]])
    cross_o, cross_top, cross_inv = cross_forward(cross_q, text_kv, penalty, seg_row, span)
    cross_o, cot_blocks = lax.optimization_barrier((cross_o, blocks_of(cotangent, "seq")))
    x_three = x_two + matmul(cross_o, full_co)
    n2_float, pull_two = jax.vjp(layer_norm, x_three, ln_gains[4], ln_biases[4])
    n_two = n2_float.astype(jnp.bfloat16)
    n_two_blocks, part_skip, part_down = lax.optimization_barrier(
        (blocks_of(n_two, "seq"), part_skip, part_down)
    )
    n_two_all = jnp.concatenate(n_two_blocks, axis=0)
    cot_all = jnp.concatenate(cot_blocks, axis=0)
    skip_blocks = blocks_of(part_skip, "seq")
    up_proj = matmul(n_two_all, part_up)
    act_float, pull_gelu = jax.vjp(gelu_tanh, up_proj)
    act_low = act_float.astype(jnp.bfloat16)
    down_part = matmul(act_low, part_down).astype(jnp.bfloat16)

    grad_down = matmul(act_low.T, cot_all).astype(jnp.bfloat16)
    total_down = lax.psum_scatter(grad_down, "dp", scatter_dimension=0, tiled=True)
    d_act = matmul(cot_all, part_down.T)
    d_up = pull_gelu(d_act)[0].astype(jnp.bfloat16)
    d_two_part = matmul(d_up, part_up.T).astype(jnp.bfloat16)
    d_two_part, skip_blocks = lax.optimization_barrier((d_two_part, skip_blocks))
    d_two_part = d_two_part.reshape(seq_count, local_tok, model_width)
    grad_up = matmul(n_two_all.T, d_up).astype(jnp.bfloat16)
    total_up = lax.psum_scatter(grad_up, "dp", scatter_dimension=0, tiled=True)
    d_n_two = sum_parts([d_two_part[k] for k in seq_range], "seq", jnp.bfloat16)
    d_n_two, down_part = lax.optimization_barrier((d_n_two, down_part))
    down_part = down_part.reshape(seq_count, local_tok, model_width)
    block_out = (
        x_three + sum_parts([down_part[k] for k in seq_range], "seq", jnp.bfloat16)
    ).astype(jnp.bfloat16)
    back_three_x, gain_four, bias_four = pull_two(d_n_two)
    d_x_three = cotangent.astype(jnp.float32) + back_three_x
    d_co = d_x_three.astype(jnp.bfloat16)
    scatters = [Scatter(matmul(cross_o.T, d_co), ranks, 1)]
    d_cross_o = matmul(d_co, full_co.T).astype(jnp.bfloat16)
    d_cross_q, d_text_kv = cross_backward(
        cross_q, text_kv, penalty, seg_row, span, cross_top, cross_inv, d_cross_o
    )
    d_cross_q = advance(d_cross_q, scatters)
    d_n_three = matmul(d_cross_q, full_cq.T)
    back_two_x, gain_three, bias_three = pull_three(d_n_three)
    d_x_two = d_x_three + back_two_x
    d_attn = d_x_two.astype(jnp.bfloat16)
    d_attn_o = matmul(d_attn, full_out.T).astype(jnp.bfloat16)
    d_turned = in_order(jnp.split(d_attn_o, seq_count, axis=1), seq_rank)
    d_heads = jnp.concatenate(exchange(d_turned, "seq"), axis=0)
    scatters += [
        Scatter(matmul(n_three.T, d_cross_q), ranks, 1),
        Scatter(matmul(caption_rows.T, d_text_kv), ranks),
    ]
    d_heads = advance(d_heads, scatters)
    scatters.append(Scatter(matmul(attn_o.T, d_attn), ranks, 1))
    d_query, d_key, d_value = self_backward(packed, d_heads, inverse, local_heads, 256)
    d_query = advance(d_query, scatters)
    d_qkv, gain_qk, bias_qk = prep_back(
        qkv_pre, d_query, d_key, d_value, tables, head_gains, local_heads, 256
    )
    d_one_part = matmul(d_qkv, part_qkv.T).astype(jnp.bfloat16).reshape(seq_count, local_tok, model_width)
    grad_qkv = matmul(n_one_all.T, d_qkv).astype(jnp.bfloat16)
    total_qkv = lax.psum_scatter(grad_qkv, "dp", scatter_dimension=0, tiled=True)
    d_n_one = sum_parts([d_one_part[k] for k in seq_range], "seq", jnp.bfloat16)
    d_n_one = advance(d_n_one, scatters)
    back_one_x, gain_one, bias_one = pull_one(d_n_one)
    d_x_one = d_x_two + back_one_x
    d_y = d_x_one.astype(jnp.bfloat16)
    y_blocks = in_order(jnp.split(d_y, seq_count, axis=1), seq_rank)
    y_cols = jnp.concatenate(exchange(y_blocks, "seq"), axis=0)
    grad_skip_w = matmul(h_all.T, y_cols).astype(jnp.bfloat16)
    down_blocks, up_blocks = blocks_of(total_down, "seq"), blocks_of(total_up, "seq")
    grad_skip_w, d_n_one, y_blocks, down_blocks, up_blocks = advance(
        (grad_skip_w, d_n_one, y_blocks, down_blocks, up_blocks), scatters
    )
    skip_scatter = Scatter(grad_skip_w, ranks, shared=False)

    d_shift = d_n_one.astype(jnp.bfloat16)
    d_image = matmul(member.astype(jnp.bfloat16).T, d_shift)
    d_image_all = gather_small(sum_all(d_image, "seq"), "dp")
    grad_mod = jnp.dot(
        cond_rows.astype(jnp.float32).T,
        d_image_all,
        precision=lax.Precision.HIGHEST,
        preferred_element_type=jnp.float32,
    )
    d_h_zero = sum(dot_nt(y, w) for y, w in zip(y_blocks, skip_blocks))
    moving = scatters + [skip_scatter]
    d_joined, gain_skip, bias_skip = advance(pull_skip(d_h_zero), moving)
    grad_tokens = d_joined[:, :model_width].astype(jnp.bfloat16)
    grad_skip = d_joined[:, model_width:].astype(jnp.bfloat16)
    qk_cols = 4 * HEAD
    small = jnp.concatenate(
        [
            jnp.stack([gain_skip[:model_width], gain_skip[model_width:]]),
            jnp.stack([gain_one, gain_three, gain_four]),
            jnp.stack([bias_skip[:model_width], bias_skip[model_width:]]),
            jnp.stack([bias_one, bias_three, bias_four]),
            jnp.pad(
                jnp.concatenate([gain_qk[:, :HEAD], bias_qk[:, :HEAD]]).reshape(1, qk_cols),
                ((0, 0), (0, model_width - qk_cols)),
            ),
        ]
    )
    small = sum_all(sum_all(small, "seq"), "dp")
    qk_total = small[10, :qk_cols].reshape(4, HEAD)

    grad_down = jnp.concatenate(in_order(down_blocks, seq_rank), axis=0).astype(jnp.float32)
    grad_up = put_columns(
        up_blocks, ranks, [[(at, first, size) for first, at, size in m] for m in up_moves], wide, jnp.float32
    )
    grad_down, grad_up, grad_mod = advance((grad_down, grad_up, grad_mod), moving)
    grad_co, grad_cq, grad_ckv, grad_out = (s.finish() for s in scatters)
    back_moves = [
        [
            (
                (kind * local_heads + head) * LANES,
                kind * model_width + j * head_cols + head * HEAD,
                HEAD,
            )
            for kind in range(3)
            for head in range(local_heads)
        ]
        for j in seq_range
    ]
    grad_qkv = put_columns(
        blocks_of(total_qkv, "seq"), ranks, back_moves, 3 * model_width, jnp.float32
    )
    skip_moves = [[(0, j * head_cols, head_cols)] for j in seq_range]
    grad_w_skip = put_columns(
        blocks_of(skip_scatter.total(), "seq"), ranks, skip_moves, model_width, jnp.float32
    )
    return (
        block_out,
        grad_tokens,
        grad_skip,
        small[0:5],
        small[5:9],
        small[9],
        qk_total[0:2],
        qk_total[2:4],
        grad_w_skip,
        grad_mod,
        grad_qkv,
        grad_out,
        grad_cq,
        grad_ckv,
        grad_co,
        grad_up,
        grad_down,
    )


def solution(mesh):
    in_specs = (
        P(("dp", "seq"), None),
        P(("dp", "seq"), None),
        P("dp", None),
        P("dp", None),
        P("dp", None),
        P("dp", None),
        P("dp", None, None),
        P("dp", None, None),
        P(),
        P(),
        P(),
        P(),
        P("dp", None),
        P("dp", None),
        P("dp", None),
        P("dp", None),
        P("dp", None),
        P("dp", None),
        P("dp", None),
        P("dp", None),
        P("dp", None),
        P(("dp", "seq"), None),
    )
    out_specs = (
        P(("dp", "seq"), None),
        P(("dp", "seq"), None),
        P(("dp", "seq"), None),
        P(),
        P(),
        P(),
        P(),
        P(),
        P("dp", None),
        P("dp", None),
        P("dp", None),
        P("dp", None),
        P("dp", None),
        P("dp", None),
        P("dp", None),
        P("dp", None),
        P("dp", None),
    )
    return jax.shard_map(shards, mesh=mesh, in_specs=in_specs, out_specs=out_specs, check_vma=False)
```

```python
import functools
import jax
import jax.numpy as jnp
import numpy as np
from jax import lax
from jax.experimental import pallas as pl
from jax.experimental.pallas import tpu as pltpu
from jax.sharding import PartitionSpec as P

HEADS = 16
HEAD = 88
IMGS = 3
CAP = 333
CLIP_TOK = 77
LANES = 128
LOG2E = 1.4426950408889634
eps_norm = 1e-06
masked_score = -1e30
vmem_bytes = 60 * 1024 * 1024


def dot_nt(left, right):
    return lax.dot_general(
        left, right, (((1,), (1,)), ((), ())), preferred_element_type=jnp.float32
    )


def dot_tn(left, right):
    return lax.dot_general(
        left, right, (((0,), (0,)), ((), ())), preferred_element_type=jnp.float32
    )


def matmul(left, right):
    return jnp.dot(left, right, preferred_element_type=jnp.float32)


def widen(value):
    pad = jnp.zeros((value.shape[0], LANES - HEAD), value.dtype)
    return jnp.concatenate([value, pad], axis=1)


def lane_of(shape):
    return lax.broadcasted_iota(jnp.int32, shape, len(shape) - 1)


def head_norm(value):
    mean = jnp.sum(value, axis=1, keepdims=True) * (1.0 / HEAD)
    center = jnp.where(lane_of(value.shape) < HEAD, value - mean, 0.0)
    spread = jnp.sum(center * center, axis=1, keepdims=True) * (1.0 / HEAD)
    factor = lax.rsqrt(spread + eps_norm)
    return center * factor, factor


def turn(value, cos_t, sin_a, sin_b):
    ahead = pltpu.roll(value, LANES - HEAD // 4, 1)
    behind = pltpu.roll(value, HEAD // 4, 1)
    return value * cos_t + ahead * sin_a + behind * sin_b


def turn_back(value, cos_t, sin_a, sin_b):
    return (
        value * cos_t
        + pltpu.roll(value * sin_a, HEAD // 4, 1)
        + pltpu.roll(value * sin_b, LANES - HEAD // 4, 1)
    )


def prep_kernel(heads, pre_ref, cos_ref, sa_ref, sb_ref, seg_ref, gain_ref, bias_ref, out_ref):
    cos_t, sin_a, sin_b = cos_ref[...], sa_ref[...], sb_ref[...]
    seg = seg_ref[...]
    lane = lane_of(cos_t.shape)
    image = lane - HEAD
    own = jnp.where(image == seg, 1.0, 0.0)
    other = jnp.where((image >= 0) & (image < IMGS) & (image != seg), masked_score, 0.0)
    ones = jnp.where(image == 0, 1.0, 0.0)
    for kind in range(3):
        for head in range(heads):
            at = (kind * heads + head) * LANES
            value = pre_ref[:, at : at + LANES]
            if kind < 2:
                normed, _ = head_norm(value)
                value = normed * gain_ref[kind : kind + 1, :] + bias_ref[kind : kind + 1, :]
                value = turn(value, cos_t, sin_a, sin_b) + (own if kind == 0 else other)
            else:
                value = value + ones
            out_ref[:, at : at + LANES] = value.astype(jnp.bfloat16)


def prep_heads(pre, tables, seg, gains, biases, heads, rows):
    count = pre.shape[0]
    cols = 3 * heads * LANES
    wide = pl.BlockSpec((rows, LANES), lambda i: (i, 0))
    return pl.pallas_call(
        functools.partial(prep_kernel, heads),
        grid=(count // rows,),
        in_specs=[
            pl.BlockSpec((rows, pre.shape[1]), lambda i: (i, 0)),
            wide,
            wide,
            wide,
            pl.BlockSpec((rows, 1), lambda i: (i, 0)),
            pl.BlockSpec((2, LANES), lambda i: (0, 0)),
            pl.BlockSpec((2, LANES), lambda i: (0, 0)),
        ],
        out_specs=pl.BlockSpec((rows, cols), lambda i: (i, 0)),
        out_shape=jax.ShapeDtypeStruct((count, cols), jnp.bfloat16),
        compiler_params=pltpu.CompilerParams(vmem_limit_bytes=vmem_bytes),
        cost_estimate=pl.CostEstimate(
            flops=20 * count * cols, bytes_accessed=8 * count * cols, transcendentals=0
        ),
    )(pre, *tables, seg, gains, biases)


score_shift = 10.0


def self_exp(scores):
    return jnp.exp2(scores * (HEAD ** (-0.5) * LOG2E) - score_shift * LOG2E)


def self_forward_kernel(heads, q_ref, k_ref, v_ref, out_ref, inv_ref):
    outs = []
    invs = []
    for head in range(heads):
        cols = slice(head * LANES, (head + 1) * LANES)
        exps = self_exp(dot_nt(k_ref[:, cols], q_ref[:, cols])).astype(jnp.bfloat16)
        total = dot_tn(v_ref[:, cols], exps)
        inverse = 1.0 / total[HEAD : HEAD + 1, :]
        invs.append(inverse)
        outs.append((total * inverse).T[:, :HEAD].astype(jnp.bfloat16))
    out_ref[...] = jnp.concatenate(outs, axis=1)
    for head in range(heads):
        inv_ref[head : head + 1, :] = invs[head]


def self_forward(packed, heads, rows):
    count = packed.shape[0]
    cols = heads * LANES
    return pl.pallas_call(
        functools.partial(self_forward_kernel, heads),
        grid=(count // rows,),
        in_specs=[
            pl.BlockSpec((rows, cols), lambda i: (i, 0)),
            pl.BlockSpec((count, cols), lambda i: (0, 1)),
            pl.BlockSpec((count, cols), lambda i: (0, 2)),
        ],
        out_specs=[
            pl.BlockSpec((rows, heads * HEAD), lambda i: (i, 0)),
            pl.BlockSpec((heads, rows), lambda i: (0, i)),
        ],
        out_shape=[
            jax.ShapeDtypeStruct((count, heads * HEAD), jnp.bfloat16),
            jax.ShapeDtypeStruct((heads, count), jnp.float32),
        ],
        compiler_params=pltpu.CompilerParams(vmem_limit_bytes=vmem_bytes),
        cost_estimate=pl.CostEstimate(
            flops=4 * count * count * cols,
            bytes_accessed=8 * count * cols,
            transcendentals=count * count * heads,
        ),
    )(packed, packed, packed)


def self_backward_kernel(heads, blocks, q_ref, k_ref, v_ref, d_ref, inv_ref, dq_ref, dk_ref, dv_ref, key_sum, value_sum):
    step = pl.program_id(0)

    @pl.when(step == 0)
    def _():
        key_sum[...] = jnp.zeros_like(key_sum)
        value_sum[...] = jnp.zeros_like(value_sum)

    scale = HEAD ** (-0.5)
    for head in range(heads):
        cols = slice(head * LANES, (head + 1) * LANES)
        d_out = widen(d_ref[:, head * HEAD : (head + 1) * HEAD])
        query, key = q_ref[:, cols], k_ref[:, cols]
        probs = self_exp(dot_nt(key, query)) * inv_ref[head : head + 1, :]
        d_probs = dot_nt(v_ref[:, cols], d_out)
        weight = jnp.sum(probs * d_probs, axis=0, keepdims=True)
        d_scores = (probs * (d_probs - weight)).astype(jnp.bfloat16)
        value_sum[:, cols] += matmul(probs.astype(jnp.bfloat16), d_out)
        key_sum[:, cols] += matmul(d_scores, query)
        dq_ref[:, cols] = (dot_tn(d_scores, key) * scale).astype(jnp.bfloat16)

    @pl.when(step == blocks - 1)
    def _():
        dk_ref[...] = (key_sum[...] * scale).astype(jnp.bfloat16)
        dv_ref[...] = value_sum[...].astype(jnp.bfloat16)


def self_backward(packed, d_out, inverse, heads, rows):
    count = packed.shape[0]
    cols = heads * LANES
    blocks = count // rows
    whole = pl.BlockSpec((count, cols), lambda i: (0, 0))
    return pl.pallas_call(
        functools.partial(self_backward_kernel, heads, blocks),
        grid=(blocks,),
        in_specs=[
            pl.BlockSpec((rows, cols), lambda i: (i, 0)),
            pl.BlockSpec((count, cols), lambda i: (0, 1)),
            pl.BlockSpec((count, cols), lambda i: (0, 2)),
            pl.BlockSpec((rows, heads * HEAD), lambda i: (i, 0)),
            pl.BlockSpec((heads, rows), lambda i: (0, i)),
        ],
        out_specs=[pl.BlockSpec((rows, cols), lambda i: (i, 0)), whole, whole],
        out_shape=[jax.ShapeDtypeStruct((count, cols), jnp.bfloat16)] * 3,
        scratch_shapes=[pltpu.VMEM((count, cols), jnp.float32)] * 2,
        compiler_params=pltpu.CompilerParams(vmem_limit_bytes=vmem_bytes),
        cost_estimate=pl.CostEstimate(
            flops=10 * count * count * cols,
            bytes_accessed=14 * count * cols,
            transcendentals=count * count * heads,
        ),
    )(packed, packed, packed, d_out, inverse)


def prep_back_kernel(heads, pre_ref, dq_ref, dk_ref, dv_ref, cos_ref, sa_ref, sb_ref, gain_ref, out_ref, dg_ref, db_ref):
    step = pl.program_id(0)

    @pl.when(step == 0)
    def _():
        dg_ref[...] = jnp.zeros_like(dg_ref)
        db_ref[...] = jnp.zeros_like(db_ref)

    cos_t, sin_a, sin_b = cos_ref[...], sa_ref[...], sb_ref[...]
    live = lane_of(cos_t.shape) < HEAD
    for kind, d_ref in enumerate((dq_ref, dk_ref)):
        gain = gain_ref[kind : kind + 1, :]
        gain_sum = jnp.zeros((1, LANES), jnp.float32)
        bias_sum = jnp.zeros((1, LANES), jnp.float32)
        for head in range(heads):
            at = (kind * heads + head) * LANES
            normed, factor = head_norm(pre_ref[:, at : at + LANES])
            given = jnp.where(live, d_ref[:, head * LANES : (head + 1) * LANES].astype(jnp.float32), 0.0)
            d_normed = turn_back(given, cos_t, sin_a, sin_b)
            gain_sum = gain_sum + jnp.sum(d_normed * normed, axis=0, keepdims=True)
            bias_sum = bias_sum + jnp.sum(d_normed, axis=0, keepdims=True)
            scaled = d_normed * gain
            mean = jnp.sum(scaled, axis=1, keepdims=True) * (1.0 / HEAD)
            slope = jnp.sum(scaled * normed, axis=1, keepdims=True) * (1.0 / HEAD)
            result = jnp.where(live, factor * (scaled - mean - normed * slope), 0.0)
            out_ref[:, at : at + LANES] = result.astype(jnp.bfloat16)
        dg_ref[kind : kind + 1, :] += gain_sum
        db_ref[kind : kind + 1, :] += bias_sum
    out_ref[:, 2 * heads * LANES :] = dv_ref[...]


def prep_back(pre, d_query, d_key, d_value, tables, gains, heads, rows):
    count = pre.shape[0]
    cols = heads * LANES
    wide = pl.BlockSpec((rows, LANES), lambda i: (i, 0))
    headed = pl.BlockSpec((rows, cols), lambda i: (i, 0))
    small = pl.BlockSpec((2, LANES), lambda i: (0, 0))
    return pl.pallas_call(
        functools.partial(prep_back_kernel, heads),
        grid=(count // rows,),
        in_specs=[
            pl.BlockSpec((rows, pre.shape[1]), lambda i: (i, 0)),
            headed,
            headed,
            headed,
            wide,
            wide,
            wide,
            small,
        ],
        out_specs=[pl.BlockSpec((rows, pre.shape[1]), lambda i: (i, 0)), small, small],
        out_shape=[
            jax.ShapeDtypeStruct(pre.shape, jnp.bfloat16),
            jax.ShapeDtypeStruct((2, LANES), jnp.float32),
            jax.ShapeDtypeStruct((2, LANES), jnp.float32),
        ],
        compiler_params=pltpu.CompilerParams(vmem_limit_bytes=vmem_bytes),
        cost_estimate=pl.CostEstimate(
            flops=60 * count * cols, bytes_accessed=30 * count * cols, transcendentals=0
        ),
    )(pre, d_query, d_key, d_value, *tables, gains)


def cross_key(kv_ref, first, head, keys, penalty):
    key = widen(kv_ref[pl.ds(first, keys), head * HEAD : (head + 1) * HEAD])
    return jnp.where(lane_of(key.shape) == HEAD, penalty, key)


def cross_value(kv_ref, first, head, keys, width):
    at = width + head * HEAD
    value = widen(kv_ref[pl.ds(first, keys), at : at + HEAD])
    return jnp.where(lane_of(value.shape) == HEAD, jnp.bfloat16(1), value)


def cross_query(q_ref, head):
    query = widen(q_ref[:, head * HEAD : (head + 1) * HEAD])
    return jnp.where(lane_of(query.shape) == HEAD, jnp.bfloat16(1), query)


cross_factor = HEAD ** (-0.5) * LOG2E


def cross_forward_kernel(heads, keys, span_ref, q_ref, kv_ref, pen_ref, seg_ref, out_ref, top_ref, inv_ref, turned):
    width = heads * HEAD

    def image(index, carry):
        first = pl.multiple_of(index * keys, 16)
        penalty = pen_ref[pl.ds(first, keys), :]
        member = seg_ref[...] == index
        for head in range(heads):
            key = cross_key(kv_ref, first, head, keys, penalty)
            scores = dot_nt(key, cross_query(q_ref, head)) * cross_factor
            top = jnp.max(scores, axis=0, keepdims=True)
            exps = jnp.exp2(scores - top).astype(jnp.bfloat16)
            total = dot_tn(cross_value(kv_ref, first, head, keys, width), exps)
            inverse = 1.0 / total[HEAD : HEAD + 1, :]
            at = slice(head * LANES, (head + 1) * LANES)
            turned[at, :] = jnp.where(member, total * inverse, turned[at, :])
            top_ref[head : head + 1, :] = jnp.where(member, top, top_ref[head : head + 1, :])
            inv_ref[head : head + 1, :] = jnp.where(member, inverse, inv_ref[head : head + 1, :])
        return carry

    lax.fori_loop(span_ref[0], span_ref[1] + 1, image, 0)
    out_ref[...] = jnp.concatenate(
        [
            turned[head * LANES : (head + 1) * LANES, :].T[:, :HEAD].astype(jnp.bfloat16)
            for head in range(heads)
        ],
        axis=1,
    )


def cross_forward(query, text_kv, penalty, seg_row, span):
    count, width = query.shape
    heads = width // HEAD
    keys = text_kv.shape[0] // IMGS
    vmem = pl.BlockSpec(memory_space=pltpu.VMEM)
    return pl.pallas_call(
        functools.partial(cross_forward_kernel, heads, keys),
        in_specs=[pl.BlockSpec(memory_space=pltpu.SMEM)] + [vmem] * 4,
        out_specs=[vmem] * 3,
        out_shape=[
            jax.ShapeDtypeStruct((count, width), jnp.bfloat16),
            jax.ShapeDtypeStruct((heads, count), jnp.float32),
            jax.ShapeDtypeStruct((heads, count), jnp.float32),
        ],
        scratch_shapes=[pltpu.VMEM((heads * LANES, count), jnp.float32)],
        compiler_params=pltpu.CompilerParams(vmem_limit_bytes=vmem_bytes),
        cost_estimate=pl.CostEstimate(
            flops=8 * count * keys * heads * LANES,
            bytes_accessed=2 * text_kv.size + 8 * query.size,
            transcendentals=2 * count * keys * heads,
        ),
    )(span, query, text_kv, penalty, seg_row)


def cross_backward_kernel(heads, keys, span_ref, q_ref, kv_ref, pen_ref, seg_ref, top_ref, inv_ref, d_ref, dq_ref, dkv_ref, turned):
    width = heads * HEAD
    scale = HEAD ** (-0.5)
    turned[...] = jnp.zeros_like(turned)
    dkv_ref[...] = jnp.zeros_like(dkv_ref)

    def image(index, carry):
        first = pl.multiple_of(index * keys, 16)
        penalty = pen_ref[pl.ds(first, keys), :]
        member = seg_ref[...] == index
        d_keys, d_values = [], []
        for head in range(heads):
            key = cross_key(kv_ref, first, head, keys, penalty)
            query = cross_query(q_ref, head)
            d_out = widen(d_ref[:, head * HEAD : (head + 1) * HEAD])
            top = jnp.where(member, top_ref[head : head + 1, :], -masked_score)
            scores = dot_nt(key, query) * cross_factor
            probs = jnp.exp2(scores - top) * inv_ref[head : head + 1, :]
            d_probs = dot_nt(cross_value(kv_ref, first, head, keys, width), d_out)
            weight = jnp.sum(probs * d_probs, axis=0, keepdims=True)
            d_scores = (probs * (d_probs - weight)).astype(jnp.bfloat16)
            d_values.append(matmul(probs.astype(jnp.bfloat16), d_out)[:, :HEAD].astype(jnp.bfloat16))
            d_keys.append((matmul(d_scores, query) * scale)[:, :HEAD].astype(jnp.bfloat16))
            at = slice(head * LANES, (head + 1) * LANES)
            turned[at, :] += dot_tn(key, d_scores)
        dkv_ref[pl.ds(first, keys), :] = jnp.concatenate(d_keys + d_values, axis=1)
        return carry

    lax.fori_loop(span_ref[0], span_ref[1] + 1, image, 0)
    dq_ref[...] = jnp.concatenate(
        [
            (turned[head * LANES : (head + 1) * LANES, :] * scale).T[:, :HEAD].astype(jnp.bfloat16)
            for head in range(heads)
        ],
        axis=1,
    )


def cross_backward(query, text_kv, penalty, seg_row, span, top, inverse, d_out):
    count, width = query.shape
    heads = width // HEAD
    keys = text_kv.shape[0] // IMGS
    vmem = pl.BlockSpec(memory_space=pltpu.VMEM)
    return pl.pallas_call(
        functools.partial(cross_backward_kernel, heads, keys),
        in_specs=[pl.BlockSpec(memory_space=pltpu.SMEM)] + [vmem] * 7,
        out_specs=[vmem] * 2,
        out_shape=[
            jax.ShapeDtypeStruct((count, width), jnp.bfloat16),
            jax.ShapeDtypeStruct(text_kv.shape, jnp.bfloat16),
        ],
        scratch_shapes=[pltpu.VMEM((heads * LANES, count), jnp.float32)],
        compiler_params=pltpu.CompilerParams(vmem_limit_bytes=vmem_bytes),
        cost_estimate=pl.CostEstimate(
            flops=20 * count * keys * heads * LANES,
            bytes_accessed=4 * text_kv.size + 8 * query.size,
            transcendentals=2 * count * keys * heads,
        ),
    )(span, query, text_kv, penalty, seg_row, top, inverse, d_out)


def layer_norm(values, norm_gain, norm_bias):
    center = values - jnp.mean(values, axis=-1, keepdims=True)
    spread = jnp.mean(center * center, axis=-1, keepdims=True)
    return center * lax.rsqrt(spread + eps_norm) * norm_gain + norm_bias


def gelu_tanh(values):
    return (
        0.5
        * values
        * (1.0 + jnp.tanh(0.7978845608028654 * (values + 0.044715 * values * values * values)))
    )


def silu_gate(values):
    return values * jax.nn.sigmoid(values)


def grid_positions(seg_all, widths, first_tok, tok_count):
    images = jnp.arange(IMGS, dtype=jnp.int32)
    starts = jnp.sum((seg_all[None, :] < images[:, None]).astype(jnp.int32), axis=1)
    seg_part = lax.dynamic_slice_in_dim(seg_all, first_tok, tok_count)
    member = seg_part[:, None] == images[None, :]
    start_tok = jnp.sum(jnp.where(member, starts[None, :], 0), axis=1)
    width_tok = jnp.sum(jnp.where(member, widths[None, :], 0), axis=1)
    in_image = first_tok + jnp.arange(tok_count, dtype=jnp.int32) - start_tok
    return (
        seg_part,
        member,
        (in_image // width_tok).astype(jnp.float32),
        (in_image % width_tok).astype(jnp.float32),
    )


def swap(value, axis, mask):
    count = lax.axis_size(axis)
    return lax.ppermute(value, axis, [(rank, rank ^ mask) for rank in range(count)])


def blocks_of(block, axis):
    count = lax.axis_size(axis)
    held = {0: block}
    bit = count // 2
    while bit:
        for mask in list(held):
            held[mask | bit] = swap(held[mask], axis, bit)
        bit //= 2
    return [held[mask] for mask in range(count)]


def sum_parts(parts, axis, kind):
    count = lax.axis_size(axis)
    held = dict(enumerate(parts))
    bit = 1
    while bit < count:
        for mask in [m for m in held if m & bit]:
            came = swap(held.pop(mask).astype(kind), axis, bit)
            held[mask ^ bit] = held[mask ^ bit] + came.astype(jnp.float32)
        bit *= 2
    return held[0]


def gather_small(value, axis):
    bit = 1
    while bit < lax.axis_size(axis):
        value = jnp.concatenate([value, swap(value, axis, bit)])
        bit *= 2
    return value


def scatter_small(value, axis):
    bit = lax.axis_size(axis) // 2
    while bit:
        half = value.shape[0] // 2
        value = value[:half] + swap(value[half:], axis, bit)
        bit //= 2
    return value


def sum_all(value, axis):
    bit = 1
    while bit < lax.axis_size(axis):
        value = value + swap(value, axis, bit)
        bit *= 2
    return value


def exchange(parts, axis):
    return [parts[0]] + [swap(parts[mask], axis, mask) for mask in range(1, len(parts))]


def in_order(blocks, rank):
    stacked = jnp.stack(blocks)
    return [
        lax.dynamic_index_in_dim(stacked, rank ^ place, 0, keepdims=False)
        for place in range(len(blocks))
    ]


def share_of(rows, seq_count):
    if rows >= 16 * seq_count:
        return -(-rows // (16 * seq_count)) * 16
    return -(-rows // seq_count)


def rope_tables(row_pos, col_pos):
    lane = np.arange(LANES)
    half, quarter = HEAD // 2, HEAD // 4
    live = lane < HEAD
    index = lane % half % quarter
    frequency = np.where(live, 10000.0 ** (-(index * 4.0 / HEAD)), 0.0).astype(np.float32)
    front = live & (lane % half < quarter)
    back = live & (lane % half >= quarter)
    angle = jnp.where((lane < half)[None], row_pos[:, None], col_pos[:, None]) * frequency[None]
    sine = jnp.sin(angle)
    return (
        jnp.where(live[None], jnp.cos(angle), 0.0),
        jnp.where(front[None], -sine, 0.0),
        jnp.where(back[None], sine, 0.0),
    )


def caption_penalty(clip_len, t5_len, keys):
    slot = jnp.arange(keys, dtype=jnp.int32)[None]
    clip_live = (slot < CLIP_TOK) & (slot < clip_len[:, None])
    t5_live = (slot >= CLIP_TOK) & (slot < CAP) & (slot - CLIP_TOK < t5_len[:, None])
    return (
        jnp.where(clip_live | t5_live, 0.0, masked_score).astype(jnp.bfloat16).reshape(-1, 1)
    )


def pick_kernel(moves, ranks_ref, source, out):
    if sum(size for _, _, size in moves[0]) < out.shape[1]:
        out[...] = jnp.zeros_like(out)
    for place, moved in enumerate(moves):

        @pl.when(ranks_ref[1] == place)
        def _(moved=moved):
            for first, at, size in moved:
                out[:, at : at + size] = source[:, first : first + size]


def pick_columns(weight, ranks, moves, cols):
    vmem = pl.BlockSpec(memory_space=pltpu.VMEM)
    return pl.pallas_call(
        functools.partial(pick_kernel, moves),
        in_specs=[pl.BlockSpec(memory_space=pltpu.SMEM), vmem],
        out_specs=vmem,
        out_shape=jax.ShapeDtypeStruct((weight.shape[0], cols), weight.dtype),
        compiler_params=pltpu.CompilerParams(vmem_limit_bytes=vmem_bytes),
    )(ranks, weight)


def put_kernel(moves, ranks_ref, *refs):
    out = refs[-1]
    for mask, block in enumerate(refs[:-1]):
        for place, moved in enumerate(moves):

            @pl.when((ranks_ref[1] ^ mask) == place)
            def _(block=block, moved=moved):
                for first, at, size in moved:
                    out[:, at : at + size] = block[:, first : first + size].astype(out.dtype)


def put_columns(blocks, ranks, moves, cols, kind):
    vmem = pl.BlockSpec(memory_space=pltpu.VMEM)
    return pl.pallas_call(
        functools.partial(put_kernel, moves),
        in_specs=[pl.BlockSpec(memory_space=pltpu.SMEM)] + [vmem] * len(blocks),
        out_specs=vmem,
        out_shape=jax.ShapeDtypeStruct((blocks[0].shape[0], cols), kind),
        compiler_params=pltpu.CompilerParams(vmem_limit_bytes=vmem_bytes),
    )(ranks, *blocks)


def quarter_kernel(row_counts, shares, ranks_ref, *refs):
    outs = refs[-len(row_counts) :]
    quarters = refs[: -len(row_counts)]
    seq_count = len(quarters) * (quarters[0].shape[1] // sum(shares))
    for mask in range(seq_count):
        quarter = quarters[mask % len(quarters)]
        base = mask // len(quarters) * sum(shares)
        for place in range(seq_count):

            @pl.when((ranks_ref[1] ^ mask) == place)
            def _(quarter=quarter, place=place, base=base):
                first = base
                for out, rows, share in zip(outs, row_counts, shares):
                    size = min(share, rows - place * share)
                    if size > 0:
                        at = place * share
                        out[at : at + size, :] = quarter[0, first : first + size, :]
                    first += share


def place_quarters(quarters, ranks, row_counts, shares, bits):
    dp_count, held, cols = quarters[0].shape

    def rank_at(i, ranks):
        return ranks[0] ^ sum(bit * ((i >> place) & 1) for place, bit in enumerate(bits))

    return pl.pallas_call(
        functools.partial(quarter_kernel, row_counts, shares),
        grid_spec=pltpu.PrefetchScalarGridSpec(
            num_scalar_prefetch=1,
            grid=(dp_count,),
            in_specs=[pl.BlockSpec((1, held, cols), lambda i, ranks: (i, 0, 0))] * len(quarters),
            out_specs=[
                pl.BlockSpec((rows, cols), lambda i, ranks: (rank_at(i, ranks), 0))
                for rows in row_counts
            ],
        ),
        out_shape=[
            jax.ShapeDtypeStruct((dp_count * rows, cols), quarters[0].dtype)
            for rows in row_counts
        ],
        compiler_params=pltpu.CompilerParams(vmem_limit_bytes=vmem_bytes),
        cost_estimate=pl.CostEstimate(
            flops=0, bytes_accessed=4 * dp_count * sum(row_counts) * cols, transcendentals=0
        ),
    )(ranks, *quarters)


def bits_below(count):
    return [1 << place for place in reversed(range(count.bit_length() - 1))]


class Gather:
    def __init__(self, own, stages):
        self.stages = list(stages)
        self.start(own)

    def start(self, own):
        self.axis, bits, self.joined = self.stages.pop(0)
        self.bits = list(bits)
        self.masks = [0]
        for bit in reversed(bits):
            self.masks += [mask | bit for mask in self.masks]
        self.held, self.came, self.level = own[None] if self.joined else {0: own}, None, 0
        self.send()

    def send(self):
        if self.joined:
            if self.bits:
                self.came = swap(self.held, self.axis, self.bits.pop(0))
            elif self.stages:
                self.start(self.held)
            return
        self.level += 1
        masks = [m for m in self.masks if bin(m).count("1") == self.level]
        if masks:
            self.came = {
                m: swap(self.held[m & (m - 1)], self.axis, m & -m)
                for m in sorted(masks, key=lambda m: (m & -m, m), reverse=True)
            }

    def step(self):
        if self.came is None:
            return
        if self.joined:
            self.held = jnp.concatenate([self.held, self.came])
        else:
            self.held.update(self.came)
        self.came = None
        self.send()

    def finish(self):
        while self.came is not None:
            self.came = lax.optimization_barrier(self.came)
            self.step()
        return [self.held[m] for m in self.masks]


def own_shares(weights, ranks):
    seq_count = lax.axis_size("seq")
    shares = [share_of(w.shape[0], seq_count) for w in weights]
    return jnp.concatenate(
        [
            lax.dynamic_slice_in_dim(
                jnp.pad(w, ((0, share * seq_count - w.shape[0]), (0, 0))), ranks[1] * share, share
            )
            for w, share in zip(weights, shares)
        ]
    )


def aligned(rows):
    return rows % 16 == 0 and rows >= 16 * lax.axis_size("seq")


def split_kernel(ranks_ref, source, *outs):
    width = outs[0].shape[1]
    for mask, out in enumerate(outs):
        for place in range(len(outs)):

            @pl.when((ranks_ref[1] ^ mask) == place)
            def _(out=out, place=place):
                out[...] = source[:, place * width : (place + 1) * width]


def split_columns(value, ranks):
    count = lax.axis_size("seq")
    vmem = pl.BlockSpec(memory_space=pltpu.VMEM)
    block = jax.ShapeDtypeStruct((value.shape[0], value.shape[1] // count), value.dtype)
    return pl.pallas_call(
        split_kernel,
        in_specs=[pl.BlockSpec(memory_space=pltpu.SMEM), vmem],
        out_specs=[vmem] * count,
        out_shape=[block] * count,
        compiler_params=pltpu.CompilerParams(vmem_limit_bytes=vmem_bytes),
    )(ranks, value)


def join_columns(blocks, ranks, kind):
    width = blocks[0].shape[1]
    moves = [[(0, j * width, width)] for j in range(len(blocks))]
    return put_columns(blocks, ranks, moves, len(blocks) * width, kind)


def put_rows_kernel(shares, ranks_ref, *refs):
    outs = refs[-len(shares) :]
    blocks = refs[: -len(shares)]
    for mask, block in enumerate(blocks):
        for place in range(len(blocks)):

            @pl.when((ranks_ref[1] ^ mask) == place)
            def _(block=block, place=place):
                first = 0
                for out, share in zip(outs, shares):
                    size = min(share, out.shape[0] - place * share)
                    width = block.shape[1]
                    for half in range(out.shape[1] // width):
                        if size > 0:
                            out[place * share : place * share + size, half * width : (half + 1) * width] = block[
                                first : first + size, :
                            ].astype(out.dtype)
                        first += share


def put_rows(blocks, ranks, shapes, shares):
    vmem = pl.BlockSpec(memory_space=pltpu.VMEM)
    return pl.pallas_call(
        functools.partial(put_rows_kernel, shares),
        in_specs=[pl.BlockSpec(memory_space=pltpu.SMEM)] + [vmem] * len(blocks),
        out_specs=[vmem] * len(shapes),
        out_shape=[jax.ShapeDtypeStruct(shape, jnp.float32) for shape in shapes],
        compiler_params=pltpu.CompilerParams(vmem_limit_bytes=vmem_bytes),
    )(ranks, *blocks)


def shared_rows(grad, group=1):
    dp_count, seq_count = lax.axis_size("dp"), lax.axis_size("seq")
    low = grad.astype(jnp.bfloat16).reshape(dp_count, -1, grad.shape[1])
    rows = low.shape[1]
    share = share_of(rows, seq_count)
    low = jnp.pad(low, ((0, 0), (0, share * seq_count - rows), (0, 0)))
    low = low.reshape(dp_count, seq_count, share, -1)
    return jnp.concatenate(jnp.split(low, group, axis=3), axis=2)


class Scatter:
    def __init__(self, held, ranks, last=0):
        dp_count, seq_count = lax.axis_size("dp"), lax.axis_size("seq")
        self.held = held
        over_seq, over_dp = [], []
        bit = 1
        while bit < seq_count:
            over_seq.append(("seq", bit, ranks[1], 1))
            bit *= 2
        bit = 1
        while bit < dp_count:
            over_dp.append(("dp", bit, ranks[0], 0))
            bit *= 2
        first = len(over_seq) - last
        self.todo = over_seq[:first] + over_dp + over_seq[first:]
        self.came = None
        self.send()

    def send(self):
        if not self.todo:
            return
        axis, bit, rank, dim = self.todo.pop(0)
        shape = self.held.shape
        split = self.held.reshape(shape[:dim] + (shape[dim] // 2, 2) + shape[dim + 1 :])
        mine = (rank // bit) % 2
        self.held = lax.dynamic_index_in_dim(split, mine, dim + 1, keepdims=False)
        give = lax.dynamic_index_in_dim(split, 1 - mine, dim + 1, keepdims=False)
        self.came = swap(give, axis, bit)

    def step(self):
        if self.came is None:
            return
        total = self.held.astype(jnp.float32) + self.came.astype(jnp.float32)
        self.held, self.came = total.astype(jnp.bfloat16), None
        self.send()

    def total(self):
        while self.came is not None:
            self.step()
        return self.held.reshape(self.held.shape[2:])


def halves_kernel(summed, ranks_ref, *refs):
    if summed:
        keep, came, other, other_came, out, give = refs
        out[...] = (keep[...].astype(jnp.float32) + came[...].astype(jnp.float32)).astype(out.dtype)
        give[...] = (
            other[...].astype(jnp.float32) + other_came[...].astype(jnp.float32)
        ).astype(give.dtype)
    else:
        keep, other, out, give = refs
        out[...] = keep[...]
        give[...] = other[...]


def halves(held, came, ranks, bit):
    count, rows, cols = held.shape

    def mine(i, ranks):
        return (2 * i + (ranks[0] // bit) % 2, 0, 0)

    def others(i, ranks):
        return (2 * i + 1 - (ranks[0] // bit) % 2, 0, 0)

    block = (1, rows, cols)
    specs = [pl.BlockSpec(block, mine)] * (1 if came is None else 2)
    specs += [pl.BlockSpec(block, others)] * (1 if came is None else 2)
    operands = [held] * 2 if came is None else [held, came, held, came]
    out = jax.ShapeDtypeStruct((count // 2, rows, cols), held.dtype)
    return pl.pallas_call(
        functools.partial(halves_kernel, came is not None),
        grid_spec=pltpu.PrefetchScalarGridSpec(
            num_scalar_prefetch=1,
            grid=(count // 2,),
            in_specs=specs,
            out_specs=[pl.BlockSpec(block, lambda i, ranks: (i, 0, 0))] * 2,
        ),
        out_shape=[out, out],
        compiler_params=pltpu.CompilerParams(vmem_limit_bytes=vmem_bytes),
        cost_estimate=pl.CostEstimate(
            flops=0, bytes_accessed=6 * held.size, transcendentals=0
        ),
    )(ranks, *operands)


class PartScatter:
    def __init__(self, grad, ranks):
        count = lax.axis_size("dp")
        self.ranks, self.bit = ranks, 1
        self.held, give = halves(grad.reshape(count, -1, grad.shape[1]), None, ranks, 1)
        self.came = swap(give, "dp", 1)

    def step(self):
        if self.came is None:
            return
        if self.held.shape[0] > 1:
            self.bit *= 2
            self.held, give = halves(self.held, self.came, self.ranks, self.bit)
            self.came = swap(give, "dp", self.bit)
        else:
            total = self.held.astype(jnp.float32) + self.came.astype(jnp.float32)
            self.held, self.came = total.astype(self.held.dtype), None

    def total(self):
        while self.came is not None:
            self.step()
        return self.held[0]


def advance(value, scatters):
    active = [s for s in scatters if s.came is not None]
    value, came = lax.optimization_barrier((value, [s.came for s in active]))
    for scatter, arrived in zip(active, came):
        scatter.came = arrived
        scatter.step()
    return value


def shards(
    tokens,
    skip,
    segment_ids,
    grid_widths,
    clip_lengths,
    t5_lengths,
    timestep,
    captions,
    ln_gains,
    ln_biases,
    qk_gains,
    qk_biases,
    w_skip,
    w_mod,
    w_qkv,
    w_out,
    w_cq,
    w_ckv,
    w_co,
    w_up,
    w_down,
    cotangent,
):
    local_tok = tokens.shape[0]
    model_width = tokens.shape[1]
    seq_count = lax.axis_size("seq")
    dp_count = lax.axis_size("dp")
    seq_rank = lax.axis_index("seq")
    dp_rank = lax.axis_index("dp")
    ranks = jnp.stack([dp_rank, seq_rank])
    bucket_len = local_tok * seq_count
    local_heads = HEADS // seq_count
    head_cols = local_heads * HEAD
    wide = w_up.shape[1]
    part = wide // (dp_count * seq_count)
    local_wide = part * dp_count
    row_count = w_mod.shape[0]
    skip_rows = w_skip.shape[0]
    order = seq_rank ^ jnp.arange(seq_count, dtype=jnp.int32)
    seq_range = range(seq_count)

    up_moves = [
        [(r * seq_count * part + j * part, r * part, part) for r in range(dp_count)]
        for j in seq_range
    ]
    qkv_moves = [
        [
            (
                kind * model_width + j * head_cols + head * HEAD,
                (kind * local_heads + head) * LANES,
                HEAD,
            )
            for kind in range(3)
            for head in range(local_heads)
        ]
        for j in seq_range
    ]
    own_skip = lax.dynamic_slice_in_dim(w_skip, seq_rank * head_cols, head_cols, axis=1)
    part_skip = lax.all_gather(own_skip, "dp", axis=0, tiled=True)
    own_qkv = pick_columns(w_qkv, ranks, qkv_moves, 3 * local_heads * LANES)
    part_qkv = lax.all_gather(own_qkv, "dp", axis=0, tiled=True)
    dp_bits, seq_bits = bits_below(dp_count), bits_below(seq_count)
    joined = jnp.concatenate([tokens, skip], axis=1).astype(jnp.float32)
    h_float, pull_skip = jax.vjp(
        layer_norm, joined, ln_gains[0:2].reshape(-1), ln_biases[0:2].reshape(-1)
    )
    h_zero = h_float.astype(jnp.bfloat16)
    own_square = own_shares([w_out, w_cq, w_co], ranks)
    own_ckv = own_shares([w_ckv], ranks)
    own_up = pick_columns(w_up, ranks, up_moves, local_wide)
    h_zero, own_square, own_ckv, own_qkv = lax.optimization_barrier(
        (h_zero, own_square, own_ckv, own_qkv)
    )
    h_way = Gather(h_zero, [("seq", seq_bits, False)])
    ways = []
    if aligned(row_count):
        square_way = Gather(own_square, [("dp", dp_bits, True), ("seq", seq_bits, False)])
        ways.append(square_way)
    if aligned(w_ckv.shape[0]):
        ckv_way = Gather(
            own_ckv,
            [("seq", seq_bits[:-1], True), ("dp", dp_bits, True), ("seq", seq_bits[-1:], False)],
        )
        ways.append(ckv_way)
    own_up = advance(own_up, [h_way] + ways)
    h_all = jnp.concatenate(h_way.finish(), axis=0)
    x_cols = matmul(h_all, part_skip).astype(jnp.bfloat16).reshape(seq_count, local_tok, head_cols)
    x_one = join_columns(exchange([x_cols[k] for k in seq_range], "seq"), ranks, jnp.float32)

    seg_all = segment_ids[0]
    seg_local, member, _, _ = grid_positions(
        seg_all, grid_widths[0], seq_rank * local_tok, local_tok
    )
    _, _, row_all, col_all = grid_positions(seg_all, grid_widths[0], 0, bucket_len)

    def reorder(values):
        return jnp.take(values.reshape(seq_count, local_tok), order, axis=0).reshape(-1)

    tables = rope_tables(reorder(row_all), reorder(col_all))
    seg_column = reorder(seg_all)[:, None]
    lane_pad = ((0, 0), (0, LANES - HEAD))
    head_gains, head_biases = jnp.pad(qk_gains, lane_pad), jnp.pad(qk_biases, lane_pad)

    cond = silu_gate(timestep[0].astype(jnp.float32)).astype(jnp.bfloat16)
    cond_all = gather_small(cond, "dp")
    cond_rows = lax.dynamic_slice_in_dim(cond_all, dp_rank * row_count, row_count, axis=1)
    shifts = scatter_small(matmul(cond_rows, w_mod), "dp")
    time_shift = jnp.sum(jnp.where(member[:, :, None], shifts[None], 0.0), axis=1)

    keys = -(-CAP // 16) * 16
    caption_rows = jnp.pad(
        captions[0].reshape(IMGS, CAP, -1), ((0, 0), (0, keys - CAP), (0, 0))
    ).reshape(IMGS * keys, -1)
    penalty = caption_penalty(clip_lengths[0], t5_lengths[0], keys)
    x_one, tables, seg_column, caption_rows, penalty, time_shift = advance(
        (x_one, tables, seg_column, caption_rows, penalty, time_shift), ways
    )
    n_float, pull_one = jax.vjp(layer_norm, x_one, ln_gains[2], ln_biases[2])
    n_one = (n_float + time_shift).astype(jnp.bfloat16)
    n_one_blocks, w_down = advance((blocks_of(n_one, "seq"), w_down), ways)
    part_up = lax.all_gather(own_up, "dp", axis=0, tiled=True)
    own_down = lax.dynamic_slice_in_dim(w_down, seq_rank * part, part)
    part_down = lax.all_gather(own_down, "dp", axis=0, tiled=True)
    n_one_all = jnp.concatenate(n_one_blocks, axis=0)
    qkv_pre = matmul(n_one_all, part_qkv)
    packed = prep_heads(qkv_pre, tables, seg_column, head_gains, head_biases, local_heads, 256)
    head_out, inverse = self_forward(packed, local_heads, 256)
    head_out = advance(head_out, ways)
    out_blocks = head_out.reshape(seq_count, local_tok, head_cols)
    attn_o = join_columns(exchange([out_blocks[k] for k in seq_range], "seq"), ranks, jnp.bfloat16)
    attn_o, part_up = advance((attn_o, part_up), ways)
    if aligned(w_ckv.shape[0]):
        ckv_rows = w_ckv.shape[0]
        quarters = [q.reshape(dp_count, -1, w_ckv.shape[1]) for q in ckv_way.finish()]
        (full_ckv,) = place_quarters(
            quarters, ranks, [ckv_rows], [share_of(ckv_rows, seq_count)], dp_bits
        )
    else:
        full_ckv = lax.all_gather(w_ckv, "dp", axis=0, tiled=True)
    if aligned(row_count):
        full_out, full_cq, full_co = place_quarters(
            square_way.finish(),
            ranks,
            [row_count] * 3,
            [share_of(row_count, seq_count)] * 3,
            dp_bits,
        )
    else:
        full_out, full_cq, full_co = (
            lax.all_gather(w, "dp", axis=0, tiled=True) for w in (w_out, w_cq, w_co)
        )
    x_two = x_one + matmul(attn_o, full_out)
    n3_float, pull_three = jax.vjp(layer_norm, x_two, ln_gains[3], ln_biases[3])
    n_three = n3_float.astype(jnp.bfloat16)
    n_three, cotangent = lax.optimization_barrier((n_three, cotangent))
    cross_q = matmul(n_three, full_cq).astype(jnp.bfloat16)
    text_kv = matmul(caption_rows, full_ckv).astype(jnp.bfloat16)
    seg_row = seg_local[None]
    span = jnp.stack([seg_local[0], seg_local[-1]])
    cross_o, cross_top, cross_inv = cross_forward(cross_q, text_kv, penalty, seg_row, span)
    cross_o, cot_blocks = lax.optimization_barrier((cross_o, blocks_of(cotangent, "seq")))
    x_three = x_two + matmul(cross_o, full_co)
    n2_float, pull_two = jax.vjp(layer_norm, x_three, ln_gains[4], ln_biases[4])
    n_two = n2_float.astype(jnp.bfloat16)
    n_two_blocks, part_skip, part_down = lax.optimization_barrier(
        (blocks_of(n_two, "seq"), part_skip, part_down)
    )
    n_two_all = jnp.concatenate(n_two_blocks, axis=0)
    cot_all = jnp.concatenate(cot_blocks, axis=0)
    skip_blocks = blocks_of(part_skip, "seq")
    up_proj = matmul(n_two_all, part_up)
    act_float, pull_gelu = jax.vjp(gelu_tanh, up_proj)
    act_low = act_float.astype(jnp.bfloat16)
    down_part = matmul(act_low, part_down).astype(jnp.bfloat16)

    grad_down = matmul(act_low.T, cot_all).astype(jnp.bfloat16)
    d_act = matmul(cot_all, part_down.T)
    d_up = pull_gelu(d_act)[0].astype(jnp.bfloat16)
    d_two_part = matmul(d_up, part_up.T).astype(jnp.bfloat16)
    total_down = lax.psum_scatter(grad_down, "dp", scatter_dimension=0, tiled=True)
    d_two_part, skip_blocks, _ = lax.optimization_barrier((d_two_part, skip_blocks, grad_down))
    d_two_part = d_two_part.reshape(seq_count, local_tok, model_width)
    grad_up = matmul(n_two_all.T, d_up).astype(jnp.bfloat16)
    d_n_two = sum_parts([d_two_part[k] for k in seq_range], "seq", jnp.bfloat16)
    total_up = lax.psum_scatter(grad_up, "dp", scatter_dimension=0, tiled=True)
    d_n_two, down_part, _ = lax.optimization_barrier((d_n_two, down_part, grad_up))
    down_part = down_part.reshape(seq_count, local_tok, model_width)
    block_out = (
        x_three + sum_parts([down_part[k] for k in seq_range], "seq", jnp.bfloat16)
    ).astype(jnp.bfloat16)
    back_three_x, gain_four, bias_four = pull_two(d_n_two)
    d_x_three = cotangent.astype(jnp.float32) + back_three_x
    d_co = d_x_three.astype(jnp.bfloat16)
    scatters = [Scatter(shared_rows(matmul(cross_o.T, d_co)), ranks, 1)]
    d_cross_o = matmul(d_co, full_co.T).astype(jnp.bfloat16)
    d_cross_q, d_text_kv = cross_backward(
        cross_q, text_kv, penalty, seg_row, span, cross_top, cross_inv, d_cross_o
    )
    d_cross_q = advance(d_cross_q, scatters)
    d_n_three = matmul(d_cross_q, full_cq.T)
    back_two_x, gain_three, bias_three = pull_three(d_n_three)
    d_x_two = d_x_three + back_two_x
    d_attn = d_x_two.astype(jnp.bfloat16)
    d_attn_o = matmul(d_attn, full_out.T).astype(jnp.bfloat16)
    d_turned = split_columns(d_attn_o, ranks)
    d_heads = jnp.concatenate(exchange(d_turned, "seq"), axis=0)
    grad_cross = jnp.concatenate(
        [
            shared_rows(matmul(n_three.T, d_cross_q)),
            shared_rows(matmul(caption_rows.T, d_text_kv), 2),
        ],
        axis=2,
    )
    scatters.append(Scatter(grad_cross, ranks))
    d_heads = advance(d_heads, scatters)
    scatters.append(Scatter(shared_rows(matmul(attn_o.T, d_attn)), ranks, 1))
    d_query, d_key, d_value = self_backward(packed, d_heads, inverse, local_heads, 256)
    d_query = advance(d_query, scatters)
    d_qkv, gain_qk, bias_qk = prep_back(
        qkv_pre, d_query, d_key, d_value, tables, head_gains, local_heads, 256
    )
    d_one_part = matmul(d_qkv, part_qkv.T).astype(jnp.bfloat16).reshape(seq_count, local_tok, model_width)
    grad_qkv = matmul(n_one_all.T, d_qkv).astype(jnp.bfloat16)
    total_qkv = lax.psum_scatter(grad_qkv, "dp", scatter_dimension=0, tiled=True)
    d_n_one = sum_parts([d_one_part[k] for k in seq_range], "seq", jnp.bfloat16)
    d_n_one = advance(d_n_one, scatters)
    back_one_x, gain_one, bias_one = pull_one(d_n_one)
    d_x_one = d_x_two + back_one_x
    d_y = d_x_one.astype(jnp.bfloat16)
    y_blocks = split_columns(d_y, ranks)
    y_cols = jnp.concatenate(exchange(y_blocks, "seq"), axis=0)
    grad_skip_w = matmul(h_all.T, y_cols).astype(jnp.bfloat16)
    grad_skip_w, d_n_one, y_blocks, total_down, total_up = lax.optimization_barrier(
        (grad_skip_w, d_n_one, y_blocks, total_down, total_up)
    )
    moving = scatters
    if aligned(skip_rows):
        skip_scatter = PartScatter(grad_skip_w, ranks)
        moving = [skip_scatter] + scatters
    else:
        total_skip = lax.psum_scatter(grad_skip_w, "dp", scatter_dimension=0, tiled=True)
    down_blocks, up_blocks = blocks_of(total_down, "seq"), blocks_of(total_up, "seq")

    d_shift = d_n_one.astype(jnp.bfloat16)
    d_image = matmul(member.astype(jnp.bfloat16).T, d_shift)
    d_image_all = gather_small(sum_all(d_image, "seq"), "dp")
    grad_mod = jnp.dot(
        cond_rows.astype(jnp.float32).T,
        d_image_all,
        precision=lax.Precision.HIGHEST,
        preferred_element_type=jnp.float32,
    )
    d_h_zero = sum(dot_nt(y, w) for y, w in zip(y_blocks, skip_blocks))
    d_h_zero = advance(d_h_zero, moving)
    d_joined, gain_skip, bias_skip = advance(pull_skip(d_h_zero), moving)
    grad_tokens = d_joined[:, :model_width].astype(jnp.bfloat16)
    grad_skip = d_joined[:, model_width:].astype(jnp.bfloat16)
    qk_cols = 4 * HEAD
    small = jnp.concatenate(
        [
            jnp.stack([gain_skip[:model_width], gain_skip[model_width:]]),
            jnp.stack([gain_one, gain_three, gain_four]),
            jnp.stack([bias_skip[:model_width], bias_skip[model_width:]]),
            jnp.stack([bias_one, bias_three, bias_four]),
            jnp.pad(
                jnp.concatenate([gain_qk[:, :HEAD], bias_qk[:, :HEAD]]).reshape(1, qk_cols),
                ((0, 0), (0, model_width - qk_cols)),
            ),
        ]
    )
    small = sum_all(sum_all(small, "seq"), "dp")
    qk_total = small[10, :qk_cols].reshape(4, HEAD)

    (grad_down,) = put_rows(down_blocks, ranks, [(seq_count * part, model_width)], [part])
    grad_up = put_columns(
        up_blocks,
        ranks,
        [[(at, first, size) for first, at, size in m] for m in up_moves],
        wide,
        jnp.float32,
    )
    grad_down, grad_up, grad_mod = advance((grad_down, grad_up, grad_mod), moving)
    if aligned(skip_rows):
        total_skip = skip_scatter.total()
    share, ckv_share = share_of(row_count, seq_count), share_of(w_ckv.shape[0], seq_count)
    square = (row_count, model_width)
    grad_co, grad_cq, grad_ckv, grad_out = put_rows(
        blocks_of(jnp.concatenate([s.total() for s in scatters]), "seq"),
        ranks,
        [square, square, w_ckv.shape, square],
        [share, share, ckv_share, share],
    )
    grad_qkv = put_columns(
        blocks_of(total_qkv, "seq"),
        ranks,
        [[(at, first, size) for first, at, size in m] for m in qkv_moves],
        3 * model_width,
        jnp.float32,
    )
    grad_w_skip = join_columns(blocks_of(total_skip, "seq"), ranks, jnp.float32)
    return (
        block_out,
        grad_tokens,
        grad_skip,
        small[0:5],
        small[5:9],
        small[9],
        qk_total[0:2],
        qk_total[2:4],
        grad_w_skip,
        grad_mod,
        grad_qkv,
        grad_out,
        grad_cq,
        grad_ckv,
        grad_co,
        grad_up,
        grad_down,
    )


def solution(mesh):
    in_specs = (
        P(("dp", "seq"), None),
        P(("dp", "seq"), None),
        P("dp", None),
        P("dp", None),
        P("dp", None),
        P("dp", None),
        P("dp", None, None),
        P("dp", None, None),
        P(),
        P(),
        P(),
        P(),
        P("dp", None),
        P("dp", None),
        P("dp", None),
        P("dp", None),
        P("dp", None),
        P("dp", None),
        P("dp", None),
        P("dp", None),
        P("dp", None),
        P(("dp", "seq"), None),
    )
    out_specs = (
        P(("dp", "seq"), None),
        P(("dp", "seq"), None),
        P(("dp", "seq"), None),
        P(),
        P(),
        P(),
        P(),
        P(),
        P("dp", None),
        P("dp", None),
        P("dp", None),
        P("dp", None),
        P("dp", None),
        P("dp", None),
        P("dp", None),
        P("dp", None),
        P("dp", None),
    )
    return jax.shard_map(shards, mesh=mesh, in_specs=in_specs, out_specs=out_specs, check_vma=False)
```

```python
import functools
import jax
import jax.numpy as jnp
import numpy as np
from jax import lax
from jax.experimental import pallas as pl
from jax.experimental.pallas import tpu as pltpu
from jax.sharding import PartitionSpec as P

HEADS = 16
HEAD = 88
IMGS = 3
CAP = 333
CLIP_TOK = 77
LANES = 128
LOG2E = 1.4426950408889634
eps_norm = 1e-06
masked_score = -1e30
vmem_bytes = 60 * 1024 * 1024


def dot_nt(left, right):
    return lax.dot_general(
        left, right, (((1,), (1,)), ((), ())), preferred_element_type=jnp.float32
    )


def dot_tn(left, right):
    return lax.dot_general(
        left, right, (((0,), (0,)), ((), ())), preferred_element_type=jnp.float32
    )


def matmul(left, right):
    return jnp.dot(left, right, preferred_element_type=jnp.float32)


def widen(value):
    pad = jnp.zeros((value.shape[0], LANES - HEAD), value.dtype)
    return jnp.concatenate([value, pad], axis=1)


def lane_of(shape):
    return lax.broadcasted_iota(jnp.int32, shape, len(shape) - 1)


def head_norm(value):
    mean = jnp.sum(value, axis=1, keepdims=True) * (1.0 / HEAD)
    center = jnp.where(lane_of(value.shape) < HEAD, value - mean, 0.0)
    spread = jnp.sum(center * center, axis=1, keepdims=True) * (1.0 / HEAD)
    factor = lax.rsqrt(spread + eps_norm)
    return center * factor, factor


def turn(value, cos_t, sin_a, sin_b):
    ahead = pltpu.roll(value, LANES - HEAD // 4, 1)
    behind = pltpu.roll(value, HEAD // 4, 1)
    return value * cos_t + ahead * sin_a + behind * sin_b


def turn_back(value, cos_t, sin_a, sin_b):
    return (
        value * cos_t
        + pltpu.roll(value * sin_a, HEAD // 4, 1)
        + pltpu.roll(value * sin_b, LANES - HEAD // 4, 1)
    )


def prep_kernel(heads, pre_ref, cos_ref, sa_ref, sb_ref, seg_ref, gain_ref, bias_ref, out_ref):
    cos_t, sin_a, sin_b = cos_ref[...], sa_ref[...], sb_ref[...]
    seg = seg_ref[...]
    lane = lane_of(cos_t.shape)
    image = lane - HEAD
    own = jnp.where(image == seg, 1.0, 0.0)
    other = jnp.where((image >= 0) & (image < IMGS) & (image != seg), masked_score, 0.0)
    ones = jnp.where(image == 0, 1.0, 0.0)
    for kind in range(3):
        for head in range(heads):
            at = (kind * heads + head) * LANES
            value = pre_ref[:, at : at + LANES]
            if kind < 2:
                normed, _ = head_norm(value)
                value = normed * gain_ref[kind : kind + 1, :] + bias_ref[kind : kind + 1, :]
                value = turn(value, cos_t, sin_a, sin_b) + (own if kind == 0 else other)
            else:
                value = value + ones
            out_ref[:, at : at + LANES] = value.astype(jnp.bfloat16)


def prep_heads(pre, tables, seg, gains, biases, heads, rows):
    count = pre.shape[0]
    cols = 3 * heads * LANES
    wide = pl.BlockSpec((rows, LANES), lambda i: (i, 0))
    return pl.pallas_call(
        functools.partial(prep_kernel, heads),
        grid=(count // rows,),
        in_specs=[
            pl.BlockSpec((rows, pre.shape[1]), lambda i: (i, 0)),
            wide,
            wide,
            wide,
            pl.BlockSpec((rows, 1), lambda i: (i, 0)),
            pl.BlockSpec((2, LANES), lambda i: (0, 0)),
            pl.BlockSpec((2, LANES), lambda i: (0, 0)),
        ],
        out_specs=pl.BlockSpec((rows, cols), lambda i: (i, 0)),
        out_shape=jax.ShapeDtypeStruct((count, cols), jnp.bfloat16),
        compiler_params=pltpu.CompilerParams(vmem_limit_bytes=vmem_bytes),
        cost_estimate=pl.CostEstimate(
            flops=20 * count * cols, bytes_accessed=8 * count * cols, transcendentals=0
        ),
    )(pre, *tables, seg, gains, biases)


score_shift = 10.0


def self_exp(scores):
    return jnp.exp2(scores * (HEAD ** (-0.5) * LOG2E) - score_shift * LOG2E)


def self_forward_kernel(heads, q_ref, k_ref, v_ref, out_ref, inv_ref):
    outs = []
    invs = []
    for head in range(heads):
        cols = slice(head * LANES, (head + 1) * LANES)
        exps = self_exp(dot_nt(k_ref[:, cols], q_ref[:, cols])).astype(jnp.bfloat16)
        total = dot_tn(v_ref[:, cols], exps)
        inverse = 1.0 / total[HEAD : HEAD + 1, :]
        invs.append(inverse)
        outs.append((total * inverse).T[:, :HEAD].astype(jnp.bfloat16))
    out_ref[...] = jnp.concatenate(outs, axis=1)
    for head in range(heads):
        inv_ref[head : head + 1, :] = invs[head]


def self_forward(packed, heads, rows):
    count = packed.shape[0]
    cols = heads * LANES
    return pl.pallas_call(
        functools.partial(self_forward_kernel, heads),
        grid=(count // rows,),
        in_specs=[
            pl.BlockSpec((rows, cols), lambda i: (i, 0)),
            pl.BlockSpec((count, cols), lambda i: (0, 1)),
            pl.BlockSpec((count, cols), lambda i: (0, 2)),
        ],
        out_specs=[
            pl.BlockSpec((rows, heads * HEAD), lambda i: (i, 0)),
            pl.BlockSpec((heads, rows), lambda i: (0, i)),
        ],
        out_shape=[
            jax.ShapeDtypeStruct((count, heads * HEAD), jnp.bfloat16),
            jax.ShapeDtypeStruct((heads, count), jnp.float32),
        ],
        compiler_params=pltpu.CompilerParams(vmem_limit_bytes=vmem_bytes),
        cost_estimate=pl.CostEstimate(
            flops=4 * count * count * cols,
            bytes_accessed=8 * count * cols,
            transcendentals=count * count * heads,
        ),
    )(packed, packed, packed)


def self_backward_kernel(heads, blocks, q_ref, k_ref, v_ref, d_ref, inv_ref, dq_ref, dk_ref, dv_ref, key_sum, value_sum):
    step = pl.program_id(0)

    @pl.when(step == 0)
    def _():
        key_sum[...] = jnp.zeros_like(key_sum)
        value_sum[...] = jnp.zeros_like(value_sum)

    scale = HEAD ** (-0.5)
    for head in range(heads):
        cols = slice(head * LANES, (head + 1) * LANES)
        d_out = widen(d_ref[:, head * HEAD : (head + 1) * HEAD])
        query, key = q_ref[:, cols], k_ref[:, cols]
        probs = self_exp(dot_nt(key, query)) * inv_ref[head : head + 1, :]
        d_probs = dot_nt(v_ref[:, cols], d_out)
        weight = jnp.sum(probs * d_probs, axis=0, keepdims=True)
        d_scores = (probs * (d_probs - weight)).astype(jnp.bfloat16)
        value_sum[:, cols] += matmul(probs.astype(jnp.bfloat16), d_out)
        key_sum[:, cols] += matmul(d_scores, query)
        dq_ref[:, cols] = (dot_tn(d_scores, key) * scale).astype(jnp.bfloat16)

    @pl.when(step == blocks - 1)
    def _():
        dk_ref[...] = (key_sum[...] * scale).astype(jnp.bfloat16)
        dv_ref[...] = value_sum[...].astype(jnp.bfloat16)


def self_backward(packed, d_out, inverse, heads, rows):
    count = packed.shape[0]
    cols = heads * LANES
    blocks = count // rows
    whole = pl.BlockSpec((count, cols), lambda i: (0, 0))
    return pl.pallas_call(
        functools.partial(self_backward_kernel, heads, blocks),
        grid=(blocks,),
        in_specs=[
            pl.BlockSpec((rows, cols), lambda i: (i, 0)),
            pl.BlockSpec((count, cols), lambda i: (0, 1)),
            pl.BlockSpec((count, cols), lambda i: (0, 2)),
            pl.BlockSpec((rows, heads * HEAD), lambda i: (i, 0)),
            pl.BlockSpec((heads, rows), lambda i: (0, i)),
        ],
        out_specs=[pl.BlockSpec((rows, cols), lambda i: (i, 0)), whole, whole],
        out_shape=[jax.ShapeDtypeStruct((count, cols), jnp.bfloat16)] * 3,
        scratch_shapes=[pltpu.VMEM((count, cols), jnp.float32)] * 2,
        compiler_params=pltpu.CompilerParams(vmem_limit_bytes=vmem_bytes),
        cost_estimate=pl.CostEstimate(
            flops=10 * count * count * cols,
            bytes_accessed=14 * count * cols,
            transcendentals=count * count * heads,
        ),
    )(packed, packed, packed, d_out, inverse)


def prep_back_kernel(heads, pre_ref, dq_ref, dk_ref, dv_ref, cos_ref, sa_ref, sb_ref, gain_ref, out_ref, dg_ref, db_ref):
    step = pl.program_id(0)

    @pl.when(step == 0)
    def _():
        dg_ref[...] = jnp.zeros_like(dg_ref)
        db_ref[...] = jnp.zeros_like(db_ref)

    cos_t, sin_a, sin_b = cos_ref[...], sa_ref[...], sb_ref[...]
    live = lane_of(cos_t.shape) < HEAD
    for kind, d_ref in enumerate((dq_ref, dk_ref)):
        gain = gain_ref[kind : kind + 1, :]
        gain_sum = jnp.zeros((1, LANES), jnp.float32)
        bias_sum = jnp.zeros((1, LANES), jnp.float32)
        for head in range(heads):
            at = (kind * heads + head) * LANES
            normed, factor = head_norm(pre_ref[:, at : at + LANES])
            given = jnp.where(live, d_ref[:, head * LANES : (head + 1) * LANES].astype(jnp.float32), 0.0)
            d_normed = turn_back(given, cos_t, sin_a, sin_b)
            gain_sum = gain_sum + jnp.sum(d_normed * normed, axis=0, keepdims=True)
            bias_sum = bias_sum + jnp.sum(d_normed, axis=0, keepdims=True)
            scaled = d_normed * gain
            mean = jnp.sum(scaled, axis=1, keepdims=True) * (1.0 / HEAD)
            slope = jnp.sum(scaled * normed, axis=1, keepdims=True) * (1.0 / HEAD)
            result = jnp.where(live, factor * (scaled - mean - normed * slope), 0.0)
            out_ref[:, at : at + LANES] = result.astype(jnp.bfloat16)
        dg_ref[kind : kind + 1, :] += gain_sum
        db_ref[kind : kind + 1, :] += bias_sum
    out_ref[:, 2 * heads * LANES :] = dv_ref[...]


def prep_back(pre, d_query, d_key, d_value, tables, gains, heads, rows):
    count = pre.shape[0]
    cols = heads * LANES
    wide = pl.BlockSpec((rows, LANES), lambda i: (i, 0))
    headed = pl.BlockSpec((rows, cols), lambda i: (i, 0))
    small = pl.BlockSpec((2, LANES), lambda i: (0, 0))
    return pl.pallas_call(
        functools.partial(prep_back_kernel, heads),
        grid=(count // rows,),
        in_specs=[
            pl.BlockSpec((rows, pre.shape[1]), lambda i: (i, 0)),
            headed,
            headed,
            headed,
            wide,
            wide,
            wide,
            small,
        ],
        out_specs=[pl.BlockSpec((rows, pre.shape[1]), lambda i: (i, 0)), small, small],
        out_shape=[
            jax.ShapeDtypeStruct(pre.shape, jnp.bfloat16),
            jax.ShapeDtypeStruct((2, LANES), jnp.float32),
            jax.ShapeDtypeStruct((2, LANES), jnp.float32),
        ],
        compiler_params=pltpu.CompilerParams(vmem_limit_bytes=vmem_bytes),
        cost_estimate=pl.CostEstimate(
            flops=60 * count * cols, bytes_accessed=30 * count * cols, transcendentals=0
        ),
    )(pre, d_query, d_key, d_value, *tables, gains)


def cross_key(kv_ref, first, head, keys, penalty):
    key = widen(kv_ref[pl.ds(first, keys), head * HEAD : (head + 1) * HEAD])
    return jnp.where(lane_of(key.shape) == HEAD, penalty, key)


def cross_value(kv_ref, first, head, keys, width):
    at = width + head * HEAD
    value = widen(kv_ref[pl.ds(first, keys), at : at + HEAD])
    return jnp.where(lane_of(value.shape) == HEAD, jnp.bfloat16(1), value)


def cross_query(q_ref, head):
    query = widen(q_ref[:, head * HEAD : (head + 1) * HEAD])
    return jnp.where(lane_of(query.shape) == HEAD, jnp.bfloat16(1), query)


cross_factor = HEAD ** (-0.5) * LOG2E


def cross_forward_kernel(heads, keys, span_ref, q_ref, kv_ref, pen_ref, seg_ref, out_ref, top_ref, inv_ref, turned):
    width = heads * HEAD

    def image(index, carry):
        first = pl.multiple_of(index * keys, 16)
        penalty = pen_ref[pl.ds(first, keys), :]
        member = seg_ref[...] == index
        for head in range(heads):
            key = cross_key(kv_ref, first, head, keys, penalty)
            scores = dot_nt(key, cross_query(q_ref, head)) * cross_factor
            top = jnp.max(scores, axis=0, keepdims=True)
            exps = jnp.exp2(scores - top).astype(jnp.bfloat16)
            total = dot_tn(cross_value(kv_ref, first, head, keys, width), exps)
            inverse = 1.0 / total[HEAD : HEAD + 1, :]
            at = slice(head * LANES, (head + 1) * LANES)
            turned[at, :] = jnp.where(member, total * inverse, turned[at, :])
            top_ref[head : head + 1, :] = jnp.where(member, top, top_ref[head : head + 1, :])
            inv_ref[head : head + 1, :] = jnp.where(member, inverse, inv_ref[head : head + 1, :])
        return carry

    lax.fori_loop(span_ref[0], span_ref[1] + 1, image, 0)
    out_ref[...] = jnp.concatenate(
        [
            turned[head * LANES : (head + 1) * LANES, :].T[:, :HEAD].astype(jnp.bfloat16)
            for head in range(heads)
        ],
        axis=1,
    )


def cross_forward(query, text_kv, penalty, seg_row, span):
    count, width = query.shape
    heads = width // HEAD
    keys = text_kv.shape[0] // IMGS
    vmem = pl.BlockSpec(memory_space=pltpu.VMEM)
    return pl.pallas_call(
        functools.partial(cross_forward_kernel, heads, keys),
        in_specs=[pl.BlockSpec(memory_space=pltpu.SMEM)] + [vmem] * 4,
        out_specs=[vmem] * 3,
        out_shape=[
            jax.ShapeDtypeStruct((count, width), jnp.bfloat16),
            jax.ShapeDtypeStruct((heads, count), jnp.float32),
            jax.ShapeDtypeStruct((heads, count), jnp.float32),
        ],
        scratch_shapes=[pltpu.VMEM((heads * LANES, count), jnp.float32)],
        compiler_params=pltpu.CompilerParams(vmem_limit_bytes=vmem_bytes),
        cost_estimate=pl.CostEstimate(
            flops=8 * count * keys * heads * LANES,
            bytes_accessed=2 * text_kv.size + 8 * query.size,
            transcendentals=2 * count * keys * heads,
        ),
    )(span, query, text_kv, penalty, seg_row)


def cross_backward_kernel(heads, keys, span_ref, q_ref, kv_ref, pen_ref, seg_ref, top_ref, inv_ref, d_ref, dq_ref, dkv_ref, turned):
    width = heads * HEAD
    scale = HEAD ** (-0.5)
    turned[...] = jnp.zeros_like(turned)
    dkv_ref[...] = jnp.zeros_like(dkv_ref)

    def image(index, carry):
        first = pl.multiple_of(index * keys, 16)
        penalty = pen_ref[pl.ds(first, keys), :]
        member = seg_ref[...] == index
        d_keys, d_values = [], []
        for head in range(heads):
            key = cross_key(kv_ref, first, head, keys, penalty)
            query = cross_query(q_ref, head)
            d_out = widen(d_ref[:, head * HEAD : (head + 1) * HEAD])
            top = jnp.where(member, top_ref[head : head + 1, :], -masked_score)
            scores = dot_nt(key, query) * cross_factor
            probs = jnp.exp2(scores - top) * inv_ref[head : head + 1, :]
            d_probs = dot_nt(cross_value(kv_ref, first, head, keys, width), d_out)
            weight = jnp.sum(probs * d_probs, axis=0, keepdims=True)
            d_scores = (probs * (d_probs - weight)).astype(jnp.bfloat16)
            d_values.append(matmul(probs.astype(jnp.bfloat16), d_out)[:, :HEAD].astype(jnp.bfloat16))
            d_keys.append((matmul(d_scores, query) * scale)[:, :HEAD].astype(jnp.bfloat16))
            at = slice(head * LANES, (head + 1) * LANES)
            turned[at, :] += dot_tn(key, d_scores)
        dkv_ref[pl.ds(first, keys), :] = jnp.concatenate(d_keys + d_values, axis=1)
        return carry

    lax.fori_loop(span_ref[0], span_ref[1] + 1, image, 0)
    dq_ref[...] = jnp.concatenate(
        [
            (turned[head * LANES : (head + 1) * LANES, :] * scale).T[:, :HEAD].astype(jnp.bfloat16)
            for head in range(heads)
        ],
        axis=1,
    )


def cross_backward(query, text_kv, penalty, seg_row, span, top, inverse, d_out):
    count, width = query.shape
    heads = width // HEAD
    keys = text_kv.shape[0] // IMGS
    vmem = pl.BlockSpec(memory_space=pltpu.VMEM)
    return pl.pallas_call(
        functools.partial(cross_backward_kernel, heads, keys),
        in_specs=[pl.BlockSpec(memory_space=pltpu.SMEM)] + [vmem] * 7,
        out_specs=[vmem] * 2,
        out_shape=[
            jax.ShapeDtypeStruct((count, width), jnp.bfloat16),
            jax.ShapeDtypeStruct(text_kv.shape, jnp.bfloat16),
        ],
        scratch_shapes=[pltpu.VMEM((heads * LANES, count), jnp.float32)],
        compiler_params=pltpu.CompilerParams(vmem_limit_bytes=vmem_bytes),
        cost_estimate=pl.CostEstimate(
            flops=20 * count * keys * heads * LANES,
            bytes_accessed=4 * text_kv.size + 8 * query.size,
            transcendentals=2 * count * keys * heads,
        ),
    )(span, query, text_kv, penalty, seg_row, top, inverse, d_out)


def layer_norm(values, norm_gain, norm_bias):
    center = values - jnp.mean(values, axis=-1, keepdims=True)
    spread = jnp.mean(center * center, axis=-1, keepdims=True)
    return center * lax.rsqrt(spread + eps_norm) * norm_gain + norm_bias


def gelu_tanh(values):
    return (
        0.5
        * values
        * (1.0 + jnp.tanh(0.7978845608028654 * (values + 0.044715 * values * values * values)))
    )


def silu_gate(values):
    return values * jax.nn.sigmoid(values)


def grid_positions(seg_all, widths, first_tok, tok_count):
    images = jnp.arange(IMGS, dtype=jnp.int32)
    starts = jnp.sum((seg_all[None, :] < images[:, None]).astype(jnp.int32), axis=1)
    seg_part = lax.dynamic_slice_in_dim(seg_all, first_tok, tok_count)
    member = seg_part[:, None] == images[None, :]
    start_tok = jnp.sum(jnp.where(member, starts[None, :], 0), axis=1)
    width_tok = jnp.sum(jnp.where(member, widths[None, :], 0), axis=1)
    in_image = first_tok + jnp.arange(tok_count, dtype=jnp.int32) - start_tok
    return (
        seg_part,
        member,
        (in_image // width_tok).astype(jnp.float32),
        (in_image % width_tok).astype(jnp.float32),
    )


def swap(value, axis, mask):
    count = lax.axis_size(axis)
    return lax.ppermute(value, axis, [(rank, rank ^ mask) for rank in range(count)])


def blocks_of(block, axis):
    count = lax.axis_size(axis)
    held = {0: block}
    bit = count // 2
    while bit:
        for mask in list(held):
            held[mask | bit] = swap(held[mask], axis, bit)
        bit //= 2
    return [held[mask] for mask in range(count)]


def sum_parts(parts, axis, kind):
    count = lax.axis_size(axis)
    held = dict(enumerate(parts))
    bit = 1
    while bit < count:
        for mask in [m for m in held if m & bit]:
            came = swap(held.pop(mask).astype(kind), axis, bit)
            held[mask ^ bit] = held[mask ^ bit] + came.astype(jnp.float32)
        bit *= 2
    return held[0]


def gather_small(value, axis):
    bit = 1
    while bit < lax.axis_size(axis):
        value = jnp.concatenate([value, swap(value, axis, bit)])
        bit *= 2
    return value


def scatter_small(value, axis):
    bit = lax.axis_size(axis) // 2
    while bit:
        half = value.shape[0] // 2
        value = value[:half] + swap(value[half:], axis, bit)
        bit //= 2
    return value


def sum_all(value, axis):
    bit = 1
    while bit < lax.axis_size(axis):
        value = value + swap(value, axis, bit)
        bit *= 2
    return value


def exchange(parts, axis):
    return [parts[0]] + [swap(parts[mask], axis, mask) for mask in range(1, len(parts))]


def in_order(blocks, rank):
    stacked = jnp.stack(blocks)
    return [
        lax.dynamic_index_in_dim(stacked, rank ^ place, 0, keepdims=False)
        for place in range(len(blocks))
    ]


def share_of(rows, seq_count):
    if rows >= 16 * seq_count:
        return -(-rows // (16 * seq_count)) * 16
    return -(-rows // seq_count)


def rope_tables(row_pos, col_pos):
    lane = np.arange(LANES)
    half, quarter = HEAD // 2, HEAD // 4
    live = lane < HEAD
    index = lane % half % quarter
    frequency = np.where(live, 10000.0 ** (-(index * 4.0 / HEAD)), 0.0).astype(np.float32)
    front = live & (lane % half < quarter)
    back = live & (lane % half >= quarter)
    angle = jnp.where((lane < half)[None], row_pos[:, None], col_pos[:, None]) * frequency[None]
    sine = jnp.sin(angle)
    return (
        jnp.where(live[None], jnp.cos(angle), 0.0),
        jnp.where(front[None], -sine, 0.0),
        jnp.where(back[None], sine, 0.0),
    )


def caption_penalty(clip_len, t5_len, keys):
    slot = jnp.arange(keys, dtype=jnp.int32)[None]
    clip_live = (slot < CLIP_TOK) & (slot < clip_len[:, None])
    t5_live = (slot >= CLIP_TOK) & (slot < CAP) & (slot - CLIP_TOK < t5_len[:, None])
    return (
        jnp.where(clip_live | t5_live, 0.0, masked_score).astype(jnp.bfloat16).reshape(-1, 1)
    )


def pick_kernel(moves, ranks_ref, source, out):
    if sum(size for _, _, size in moves[0]) < out.shape[1]:
        out[...] = jnp.zeros_like(out)
    for place, moved in enumerate(moves):

        @pl.when(ranks_ref[1] == place)
        def _(moved=moved):
            for first, at, size in moved:
                out[:, at : at + size] = source[:, first : first + size]


def pick_columns(weight, ranks, moves, cols):
    vmem = pl.BlockSpec(memory_space=pltpu.VMEM)
    return pl.pallas_call(
        functools.partial(pick_kernel, moves),
        in_specs=[pl.BlockSpec(memory_space=pltpu.SMEM), vmem],
        out_specs=vmem,
        out_shape=jax.ShapeDtypeStruct((weight.shape[0], cols), weight.dtype),
        compiler_params=pltpu.CompilerParams(vmem_limit_bytes=vmem_bytes),
    )(ranks, weight)


def put_kernel(moves, ranks_ref, *refs):
    out = refs[-1]
    for mask, block in enumerate(refs[:-1]):
        for place, moved in enumerate(moves):

            @pl.when((ranks_ref[1] ^ mask) == place)
            def _(block=block, moved=moved):
                for first, at, size in moved:
                    out[:, at : at + size] = block[:, first : first + size].astype(out.dtype)


def put_columns(blocks, ranks, moves, cols, kind):
    vmem = pl.BlockSpec(memory_space=pltpu.VMEM)
    return pl.pallas_call(
        functools.partial(put_kernel, moves),
        in_specs=[pl.BlockSpec(memory_space=pltpu.SMEM)] + [vmem] * len(blocks),
        out_specs=vmem,
        out_shape=jax.ShapeDtypeStruct((blocks[0].shape[0], cols), kind),
        compiler_params=pltpu.CompilerParams(vmem_limit_bytes=vmem_bytes),
    )(ranks, *blocks)


def quarter_kernel(row_counts, shares, ranks_ref, *refs):
    outs = refs[-len(row_counts) :]
    quarters = refs[: -len(row_counts)]
    seq_count = len(quarters) * (quarters[0].shape[1] // sum(shares))
    for mask in range(seq_count):
        quarter = quarters[mask % len(quarters)]
        base = mask // len(quarters) * sum(shares)
        for place in range(seq_count):

            @pl.when((ranks_ref[1] ^ mask) == place)
            def _(quarter=quarter, place=place, base=base):
                first = base
                for out, rows, share in zip(outs, row_counts, shares):
                    size = min(share, rows - place * share)
                    if size > 0:
                        at = place * share
                        out[at : at + size, :] = quarter[0, first : first + size, :]
                    first += share


def place_quarters(quarters, ranks, row_counts, shares, bits):
    dp_count, held, cols = quarters[0].shape

    def rank_at(i, ranks):
        return ranks[0] ^ sum(bit * ((i >> place) & 1) for place, bit in enumerate(bits))

    return pl.pallas_call(
        functools.partial(quarter_kernel, row_counts, shares),
        grid_spec=pltpu.PrefetchScalarGridSpec(
            num_scalar_prefetch=1,
            grid=(dp_count,),
            in_specs=[pl.BlockSpec((1, held, cols), lambda i, ranks: (i, 0, 0))] * len(quarters),
            out_specs=[
                pl.BlockSpec((rows, cols), lambda i, ranks: (rank_at(i, ranks), 0))
                for rows in row_counts
            ],
        ),
        out_shape=[
            jax.ShapeDtypeStruct((dp_count * rows, cols), quarters[0].dtype)
            for rows in row_counts
        ],
        compiler_params=pltpu.CompilerParams(vmem_limit_bytes=vmem_bytes),
        cost_estimate=pl.CostEstimate(
            flops=0, bytes_accessed=4 * dp_count * sum(row_counts) * cols, transcendentals=0
        ),
    )(ranks, *quarters)


def bits_below(count):
    return [1 << place for place in reversed(range(count.bit_length() - 1))]


class Gather:
    def __init__(self, own, stages):
        self.stages = list(stages)
        self.start(own)

    def start(self, own):
        self.axis, bits, self.joined = self.stages.pop(0)
        self.bits = list(bits)
        self.masks = [0]
        for bit in reversed(bits):
            self.masks += [mask | bit for mask in self.masks]
        self.held, self.came, self.level = own[None] if self.joined else {0: own}, None, 0
        self.send()

    def send(self):
        if self.joined:
            if self.bits:
                self.came = swap(self.held, self.axis, self.bits.pop(0))
            elif self.stages:
                self.start(self.held)
            return
        self.level += 1
        masks = [m for m in self.masks if bin(m).count("1") == self.level]
        if masks:
            self.came = {
                m: swap(self.held[m & (m - 1)], self.axis, m & -m)
                for m in sorted(masks, key=lambda m: (m & -m, m), reverse=True)
            }

    def step(self):
        if self.came is None:
            return
        if self.joined:
            self.held = jnp.concatenate([self.held, self.came])
        else:
            self.held.update(self.came)
        self.came = None
        self.send()

    def finish(self):
        while self.came is not None:
            self.came = lax.optimization_barrier(self.came)
            self.step()
        return [self.held[m] for m in self.masks]


def own_shares(weights, ranks):
    seq_count = lax.axis_size("seq")
    shares = [share_of(w.shape[0], seq_count) for w in weights]
    return jnp.concatenate(
        [
            lax.dynamic_slice_in_dim(
                jnp.pad(w, ((0, share * seq_count - w.shape[0]), (0, 0))), ranks[1] * share, share
            )
            for w, share in zip(weights, shares)
        ]
    )


def aligned(rows):
    return rows % 16 == 0 and rows >= 16 * lax.axis_size("seq")


def split_kernel(ranks_ref, source, *outs):
    width = outs[0].shape[1]
    for mask, out in enumerate(outs):
        for place in range(len(outs)):

            @pl.when((ranks_ref[1] ^ mask) == place)
            def _(out=out, place=place):
                out[...] = source[:, place * width : (place + 1) * width]


def split_columns(value, ranks):
    count = lax.axis_size("seq")
    vmem = pl.BlockSpec(memory_space=pltpu.VMEM)
    block = jax.ShapeDtypeStruct((value.shape[0], value.shape[1] // count), value.dtype)
    return pl.pallas_call(
        split_kernel,
        in_specs=[pl.BlockSpec(memory_space=pltpu.SMEM), vmem],
        out_specs=[vmem] * count,
        out_shape=[block] * count,
        compiler_params=pltpu.CompilerParams(vmem_limit_bytes=vmem_bytes),
    )(ranks, value)


def join_columns(blocks, ranks, kind):
    width = blocks[0].shape[1]
    moves = [[(0, j * width, width)] for j in range(len(blocks))]
    return put_columns(blocks, ranks, moves, len(blocks) * width, kind)


def put_rows_kernel(shares, ranks_ref, *refs):
    outs = refs[-len(shares) :]
    blocks = refs[: -len(shares)]
    for mask, block in enumerate(blocks):
        for place in range(len(blocks)):

            @pl.when((ranks_ref[1] ^ mask) == place)
            def _(block=block, place=place):
                first = 0
                for out, share in zip(outs, shares):
                    size = min(share, out.shape[0] - place * share)
                    width = block.shape[1]
                    for half in range(out.shape[1] // width):
                        if size > 0:
                            out[place * share : place * share + size, half * width : (half + 1) * width] = block[
                                first : first + size, :
                            ].astype(out.dtype)
                        first += share


def put_rows(blocks, ranks, shapes, shares):
    vmem = pl.BlockSpec(memory_space=pltpu.VMEM)
    return pl.pallas_call(
        functools.partial(put_rows_kernel, shares),
        in_specs=[pl.BlockSpec(memory_space=pltpu.SMEM)] + [vmem] * len(blocks),
        out_specs=[vmem] * len(shapes),
        out_shape=[jax.ShapeDtypeStruct(shape, jnp.float32) for shape in shapes],
        compiler_params=pltpu.CompilerParams(vmem_limit_bytes=vmem_bytes),
    )(ranks, *blocks)


def shared_rows(grad, group=1):
    dp_count, seq_count = lax.axis_size("dp"), lax.axis_size("seq")
    low = grad.astype(jnp.bfloat16).reshape(dp_count, -1, grad.shape[1])
    rows = low.shape[1]
    share = share_of(rows, seq_count)
    low = jnp.pad(low, ((0, 0), (0, share * seq_count - rows), (0, 0)))
    low = low.reshape(dp_count, seq_count, share, -1)
    return jnp.concatenate(jnp.split(low, group, axis=3), axis=2)


class Scatter:
    def __init__(self, held, ranks, last=0):
        dp_count, seq_count = lax.axis_size("dp"), lax.axis_size("seq")
        self.held = held
        over_seq, over_dp = [], []
        bit = 1
        while bit < seq_count:
            over_seq.append(("seq", bit, ranks[1], 1))
            bit *= 2
        bit = 1
        while bit < dp_count:
            over_dp.append(("dp", bit, ranks[0], 0))
            bit *= 2
        first = len(over_seq) - last
        self.todo = over_seq[:first] + over_dp + over_seq[first:]
        self.came = None
        self.send()

    def send(self):
        if not self.todo:
            return
        axis, bit, rank, dim = self.todo.pop(0)
        shape = self.held.shape
        split = self.held.reshape(shape[:dim] + (shape[dim] // 2, 2) + shape[dim + 1 :])
        mine = (rank // bit) % 2
        self.held = lax.dynamic_index_in_dim(split, mine, dim + 1, keepdims=False)
        give = lax.dynamic_index_in_dim(split, 1 - mine, dim + 1, keepdims=False)
        self.came = swap(give, axis, bit)

    def step(self):
        if self.came is None:
            return
        total = self.held.astype(jnp.float32) + self.came.astype(jnp.float32)
        self.held, self.came = total.astype(jnp.bfloat16), None
        self.send()

    def total(self):
        while self.came is not None:
            self.step()
        return self.held.reshape(self.held.shape[2:])


def halves_kernel(summed, ranks_ref, *refs):
    if summed:
        keep, came, other, other_came, out, give = refs
        out[...] = (keep[...].astype(jnp.float32) + came[...].astype(jnp.float32)).astype(out.dtype)
        give[...] = (
            other[...].astype(jnp.float32) + other_came[...].astype(jnp.float32)
        ).astype(give.dtype)
    else:
        keep, other, out, give = refs
        out[...] = keep[...]
        give[...] = other[...]


def halves(held, came, ranks, bit):
    count, rows, cols = held.shape

    def mine(i, ranks):
        return (2 * i + (ranks[0] // bit) % 2, 0, 0)

    def others(i, ranks):
        return (2 * i + 1 - (ranks[0] // bit) % 2, 0, 0)

    block = (1, rows, cols)
    specs = [pl.BlockSpec(block, mine)] * (1 if came is None else 2)
    specs += [pl.BlockSpec(block, others)] * (1 if came is None else 2)
    operands = [held] * 2 if came is None else [held, came, held, came]
    out = jax.ShapeDtypeStruct((count // 2, rows, cols), held.dtype)
    return pl.pallas_call(
        functools.partial(halves_kernel, came is not None),
        grid_spec=pltpu.PrefetchScalarGridSpec(
            num_scalar_prefetch=1,
            grid=(count // 2,),
            in_specs=specs,
            out_specs=[pl.BlockSpec(block, lambda i, ranks: (i, 0, 0))] * 2,
        ),
        out_shape=[out, out],
        compiler_params=pltpu.CompilerParams(vmem_limit_bytes=vmem_bytes),
        cost_estimate=pl.CostEstimate(
            flops=0, bytes_accessed=6 * held.size, transcendentals=0
        ),
    )(ranks, *operands)


class PartScatter:
    def __init__(self, grad, ranks):
        count = lax.axis_size("dp")
        self.ranks, self.bit = ranks, 1
        self.held, give = halves(grad.reshape(count, -1, grad.shape[1]), None, ranks, 1)
        self.came = swap(give, "dp", 1)

    def step(self):
        if self.came is None:
            return
        if self.held.shape[0] > 1:
            self.bit *= 2
            self.held, give = halves(self.held, self.came, self.ranks, self.bit)
            self.came = swap(give, "dp", self.bit)
        else:
            total = self.held.astype(jnp.float32) + self.came.astype(jnp.float32)
            self.held, self.came = total.astype(self.held.dtype), None

    def total(self):
        while self.came is not None:
            self.step()
        return self.held[0]


class SumWay:
    def __init__(self, parts, axis):
        self.held, self.axis, self.bit = dict(enumerate(parts)), axis, 1
        self.came = None
        self.send()

    def send(self):
        if self.bit < lax.axis_size(self.axis):
            self.came = {
                mask ^ self.bit: swap(self.held.pop(mask).astype(jnp.bfloat16), self.axis, self.bit)
                for mask in sorted(self.held)
                if mask & self.bit
            }
            self.bit *= 2

    def step(self):
        if self.came is None:
            return
        for mask, arrived in self.came.items():
            self.held[mask] = self.held[mask].astype(jnp.float32) + arrived.astype(jnp.float32)
        self.came = None
        self.send()

    def total(self):
        while self.came is not None:
            self.step()
        return self.held[0]


def advance(value, scatters):
    active = [s for s in scatters if s.came is not None]
    value, came = lax.optimization_barrier((value, [s.came for s in active]))
    for scatter, arrived in zip(active, came):
        scatter.came = arrived
        scatter.step()
    return value


def shards(
    tokens,
    skip,
    segment_ids,
    grid_widths,
    clip_lengths,
    t5_lengths,
    timestep,
    captions,
    ln_gains,
    ln_biases,
    qk_gains,
    qk_biases,
    w_skip,
    w_mod,
    w_qkv,
    w_out,
    w_cq,
    w_ckv,
    w_co,
    w_up,
    w_down,
    cotangent,
):
    local_tok = tokens.shape[0]
    model_width = tokens.shape[1]
    seq_count = lax.axis_size("seq")
    dp_count = lax.axis_size("dp")
    seq_rank = lax.axis_index("seq")
    dp_rank = lax.axis_index("dp")
    ranks = jnp.stack([dp_rank, seq_rank])
    bucket_len = local_tok * seq_count
    local_heads = HEADS // seq_count
    head_cols = local_heads * HEAD
    wide = w_up.shape[1]
    part = wide // (dp_count * seq_count)
    local_wide = part * dp_count
    row_count = w_mod.shape[0]
    skip_rows = w_skip.shape[0]
    order = seq_rank ^ jnp.arange(seq_count, dtype=jnp.int32)
    seq_range = range(seq_count)

    up_moves = [
        [(r * seq_count * part + j * part, r * part, part) for r in range(dp_count)]
        for j in seq_range
    ]
    qkv_moves = [
        [
            (
                kind * model_width + j * head_cols + head * HEAD,
                (kind * local_heads + head) * LANES,
                HEAD,
            )
            for kind in range(3)
            for head in range(local_heads)
        ]
        for j in seq_range
    ]
    own_skip = lax.dynamic_slice_in_dim(w_skip, seq_rank * head_cols, head_cols, axis=1)
    part_skip = lax.all_gather(own_skip, "dp", axis=0, tiled=True)
    own_qkv = pick_columns(w_qkv, ranks, qkv_moves, 3 * local_heads * LANES)
    part_qkv = lax.all_gather(own_qkv, "dp", axis=0, tiled=True)
    dp_bits, seq_bits = bits_below(dp_count), bits_below(seq_count)
    joined = jnp.concatenate([tokens, skip], axis=1).astype(jnp.float32)
    h_float, pull_skip = jax.vjp(
        layer_norm, joined, ln_gains[0:2].reshape(-1), ln_biases[0:2].reshape(-1)
    )
    h_zero = h_float.astype(jnp.bfloat16)
    own_square = own_shares([w_out, w_cq, w_co], ranks)
    own_ckv = own_shares([w_ckv], ranks)
    own_up = pick_columns(w_up, ranks, up_moves, local_wide)
    h_zero, own_square, own_ckv, own_qkv = lax.optimization_barrier(
        (h_zero, own_square, own_ckv, own_qkv)
    )
    h_way = Gather(h_zero, [("seq", seq_bits, False)])
    ways = []
    if aligned(row_count):
        square_way = Gather(own_square, [("dp", dp_bits, True), ("seq", seq_bits, False)])
        ways.append(square_way)
    if aligned(w_ckv.shape[0]):
        ckv_way = Gather(
            own_ckv,
            [("seq", seq_bits[:-1], True), ("dp", dp_bits, True), ("seq", seq_bits[-1:], False)],
        )
        ways.append(ckv_way)
    own_up = advance(own_up, [h_way] + ways)
    h_all = jnp.concatenate(h_way.finish(), axis=0)
    x_cols = matmul(h_all, part_skip).astype(jnp.bfloat16).reshape(seq_count, local_tok, head_cols)
    x_one = join_columns(exchange([x_cols[k] for k in seq_range], "seq"), ranks, jnp.float32)

    seg_all = segment_ids[0]
    seg_local, member, _, _ = grid_positions(
        seg_all, grid_widths[0], seq_rank * local_tok, local_tok
    )
    _, _, row_all, col_all = grid_positions(seg_all, grid_widths[0], 0, bucket_len)

    def reorder(values):
        return jnp.take(values.reshape(seq_count, local_tok), order, axis=0).reshape(-1)

    tables = rope_tables(reorder(row_all), reorder(col_all))
    seg_column = reorder(seg_all)[:, None]
    lane_pad = ((0, 0), (0, LANES - HEAD))
    head_gains, head_biases = jnp.pad(qk_gains, lane_pad), jnp.pad(qk_biases, lane_pad)

    cond = silu_gate(timestep[0].astype(jnp.float32)).astype(jnp.bfloat16)
    cond_all = gather_small(cond, "dp")
    xor_order = dp_rank ^ jnp.arange(dp_count, dtype=jnp.int32)
    cond_ranked = jnp.take(cond_all.reshape(dp_count, IMGS, model_width), xor_order, axis=0).reshape(
        dp_count * IMGS, model_width
    )
    cond_rows = lax.dynamic_slice_in_dim(cond_all, dp_rank * row_count, row_count, axis=1)
    shifts = scatter_small(matmul(cond_rows, w_mod), "dp")
    time_shift = jnp.sum(jnp.where(member[:, :, None], shifts[None], 0.0), axis=1)

    keys = -(-CAP // 16) * 16
    caption_rows = jnp.pad(
        captions[0].reshape(IMGS, CAP, -1), ((0, 0), (0, keys - CAP), (0, 0))
    ).reshape(IMGS * keys, -1)
    penalty = caption_penalty(clip_lengths[0], t5_lengths[0], keys)
    x_one, tables, seg_column, caption_rows, penalty, time_shift = advance(
        (x_one, tables, seg_column, caption_rows, penalty, time_shift), ways
    )
    n_float, pull_one = jax.vjp(layer_norm, x_one, ln_gains[2], ln_biases[2])
    n_one = (n_float + time_shift).astype(jnp.bfloat16)
    n_one_blocks, w_down = advance((blocks_of(n_one, "seq"), w_down), ways)
    own_down = lax.dynamic_slice_in_dim(w_down, seq_rank * part, part)
    part_down = lax.all_gather(own_down, "dp", axis=0, tiled=True)
    n_one_all = jnp.concatenate(n_one_blocks, axis=0)
    qkv_pre = matmul(n_one_all, part_qkv)
    packed = prep_heads(qkv_pre, tables, seg_column, head_gains, head_biases, local_heads, 256)
    head_out, inverse = self_forward(packed, local_heads, 256)
    head_out, own_up = advance((head_out, own_up), ways)
    part_up = lax.all_gather(own_up, "dp", axis=0, tiled=True)
    out_blocks = head_out.reshape(seq_count, local_tok, head_cols)
    attn_o = join_columns(exchange([out_blocks[k] for k in seq_range], "seq"), ranks, jnp.bfloat16)
    attn_o = advance(attn_o, ways)
    if aligned(w_ckv.shape[0]):
        ckv_rows = w_ckv.shape[0]
        quarters = [q.reshape(dp_count, -1, w_ckv.shape[1]) for q in ckv_way.finish()]
        (full_ckv,) = place_quarters(
            quarters, ranks, [ckv_rows], [share_of(ckv_rows, seq_count)], dp_bits
        )
    else:
        full_ckv = lax.all_gather(w_ckv, "dp", axis=0, tiled=True)
    if aligned(row_count):
        full_out, full_cq, full_co = place_quarters(
            square_way.finish(),
            ranks,
            [row_count] * 3,
            [share_of(row_count, seq_count)] * 3,
            dp_bits,
        )
    else:
        full_out, full_cq, full_co = (
            lax.all_gather(w, "dp", axis=0, tiled=True) for w in (w_out, w_cq, w_co)
        )
    x_two = x_one + matmul(attn_o, full_out)
    n3_float, pull_three = jax.vjp(layer_norm, x_two, ln_gains[3], ln_biases[3])
    n_three = n3_float.astype(jnp.bfloat16)
    n_three, cotangent = lax.optimization_barrier((n_three, cotangent))
    cross_q = matmul(n_three, full_cq).astype(jnp.bfloat16)
    text_kv = matmul(caption_rows, full_ckv).astype(jnp.bfloat16)
    seg_row = seg_local[None]
    span = jnp.stack([seg_local[0], seg_local[-1]])
    cross_o, cross_top, cross_inv = cross_forward(cross_q, text_kv, penalty, seg_row, span)
    cross_o, cot_blocks, part_up = lax.optimization_barrier(
        (cross_o, blocks_of(cotangent, "seq"), part_up)
    )
    cot_all = jnp.concatenate(cot_blocks, axis=0)
    x_three = x_two + matmul(cross_o, full_co)
    n2_float, pull_two = jax.vjp(layer_norm, x_three, ln_gains[4], ln_biases[4])
    n_two = n2_float.astype(jnp.bfloat16)
    n_two_blocks, part_skip, part_down, cot_all = lax.optimization_barrier(
        (blocks_of(n_two, "seq"), part_skip, part_down, cot_all)
    )
    n_two_all = jnp.concatenate(n_two_blocks, axis=0)
    skip_blocks = blocks_of(part_skip, "seq")
    up_proj = matmul(n_two_all, part_up)
    act_float, pull_gelu = jax.vjp(gelu_tanh, up_proj)
    act_low = act_float.astype(jnp.bfloat16)
    down_part = matmul(act_low, part_down).astype(jnp.bfloat16)

    grad_down = matmul(act_low.T, cot_all).astype(jnp.bfloat16)
    d_act = matmul(cot_all, part_down.T)
    d_up = pull_gelu(d_act)[0].astype(jnp.bfloat16)
    d_two_part = matmul(d_up, part_up.T).astype(jnp.bfloat16)
    total_down = lax.psum_scatter(grad_down, "dp", scatter_dimension=0, tiled=True)
    d_two_part, skip_blocks = lax.optimization_barrier((d_two_part, skip_blocks))
    d_two_part = d_two_part.reshape(seq_count, local_tok, model_width)
    grad_up = matmul(n_two_all.T, d_up).astype(jnp.bfloat16)
    d_n_two = sum_parts([d_two_part[k] for k in seq_range], "seq", jnp.bfloat16)
    total_up = lax.psum_scatter(grad_up, "dp", scatter_dimension=0, tiled=True)
    d_n_two, _, _ = lax.optimization_barrier((d_n_two, grad_up, grad_down))
    back_three_x, gain_four, bias_four = pull_two(d_n_two)
    d_x_three = cotangent.astype(jnp.float32) + back_three_x
    d_co = d_x_three.astype(jnp.bfloat16)
    scatters = [Scatter(shared_rows(matmul(cross_o.T, d_co)), ranks, 1)]
    d_cross_o = matmul(d_co, full_co.T).astype(jnp.bfloat16)
    d_cross_q, d_text_kv = cross_backward(
        cross_q, text_kv, penalty, seg_row, span, cross_top, cross_inv, d_cross_o
    )
    d_cross_q = advance(d_cross_q, scatters)
    d_n_three = matmul(d_cross_q, full_cq.T)
    back_two_x, gain_three, bias_three = pull_three(d_n_three)
    d_x_two = d_x_three + back_two_x
    d_attn = d_x_two.astype(jnp.bfloat16)
    d_attn_o = matmul(d_attn, full_out.T).astype(jnp.bfloat16)
    d_turned = split_columns(d_attn_o, ranks)
    d_heads = jnp.concatenate(exchange(d_turned, "seq"), axis=0)
    grad_cross = jnp.concatenate(
        [
            shared_rows(matmul(n_three.T, d_cross_q)),
            shared_rows(matmul(caption_rows.T, d_text_kv), 2),
        ],
        axis=2,
    )
    scatters.append(Scatter(grad_cross, ranks))
    d_heads, down_part = advance((d_heads, down_part), scatters)
    down_part = down_part.reshape(seq_count, local_tok, model_width)
    block_way = SumWay([down_part[k] for k in seq_range], "seq")
    scatters.append(Scatter(shared_rows(matmul(attn_o.T, d_attn)), ranks, 1))
    d_query, d_key, d_value = self_backward(packed, d_heads, inverse, local_heads, 256)
    d_query, total_up = advance((d_query, total_up), scatters + [block_way])
    up_way = Gather(total_up, [("seq", seq_bits, False)])
    d_qkv, gain_qk, bias_qk = prep_back(
        qkv_pre, d_query, d_key, d_value, tables, head_gains, local_heads, 256
    )
    d_one_part = matmul(d_qkv, part_qkv.T).astype(jnp.bfloat16).reshape(seq_count, local_tok, model_width)
    grad_qkv = matmul(n_one_all.T, d_qkv).astype(jnp.bfloat16)
    total_qkv = lax.psum_scatter(grad_qkv, "dp", scatter_dimension=0, tiled=True)
    d_n_one = sum_parts([d_one_part[k] for k in seq_range], "seq", jnp.bfloat16)
    d_n_one, total_down = advance(
        (d_n_one, total_down), [scatters[0], scatters[2], block_way, up_way]
    )
    block_out = (x_three + block_way.total()).astype(jnp.bfloat16)
    down_way = Gather(total_down, [("seq", seq_bits, False)])
    back_one_x, gain_one, bias_one = pull_one(d_n_one)
    d_x_one = d_x_two + back_one_x
    d_y = d_x_one.astype(jnp.bfloat16)
    y_blocks = split_columns(d_y, ranks)
    y_cols = jnp.concatenate(exchange(y_blocks, "seq"), axis=0)
    grad_skip_w = matmul(h_all.T, y_cols).astype(jnp.bfloat16)
    grad_skip_w, d_n_one, y_blocks = lax.optimization_barrier((grad_skip_w, d_n_one, y_blocks))
    moving = scatters + [up_way, down_way]
    if aligned(skip_rows):
        skip_scatter = PartScatter(grad_skip_w, ranks)
        moving = [skip_scatter] + moving
    else:
        total_skip = lax.psum_scatter(grad_skip_w, "dp", scatter_dimension=0, tiled=True)

    d_shift = d_n_one.astype(jnp.bfloat16)
    d_image = matmul(member.astype(jnp.bfloat16).T, d_shift)
    d_h_zero = sum(dot_nt(y, w) for y, w in zip(y_blocks, skip_blocks))
    d_h_zero = advance(d_h_zero, moving)
    d_joined, gain_skip, bias_skip = advance(pull_skip(d_h_zero), moving)
    grad_tokens = d_joined[:, :model_width].astype(jnp.bfloat16)
    grad_skip = d_joined[:, model_width:].astype(jnp.bfloat16)
    qk_cols = 4 * HEAD
    mine = lax.broadcasted_iota(jnp.int32, (dp_count, 1, 1), 0) == dp_rank
    d_images = jnp.where(mine, d_image[None], 0.0).reshape(dp_count * IMGS, model_width)
    small = jnp.concatenate(
        [
            d_images,
            jnp.stack([gain_skip[:model_width], gain_skip[model_width:]]),
            jnp.stack([gain_one, gain_three, gain_four]),
            jnp.stack([bias_skip[:model_width], bias_skip[model_width:]]),
            jnp.stack([bias_one, bias_three, bias_four]),
            jnp.pad(
                jnp.concatenate([gain_qk[:, :HEAD], bias_qk[:, :HEAD]]).reshape(1, qk_cols),
                ((0, 0), (0, model_width - qk_cols)),
            ),
        ]
    )
    small = sum_all(sum_all(small, "dp"), "seq")
    cond_abs = lax.dynamic_slice_in_dim(
        cond_ranked, dp_rank * row_count, row_count, axis=1
    ).astype(jnp.float32)
    grad_mod = jnp.dot(
        cond_abs.T,
        small[: dp_count * IMGS],
        precision=lax.Precision.HIGHEST,
        preferred_element_type=jnp.float32,
    )
    d_image_all, small = small[: dp_count * IMGS], small[dp_count * IMGS :]
    qk_total = small[10, :qk_cols].reshape(4, HEAD)

    (grad_down,) = put_rows(down_way.finish(), ranks, [(seq_count * part, model_width)], [part])
    grad_up = put_columns(
        up_way.finish(),
        ranks,
        [[(at, first, size) for first, at, size in m] for m in up_moves],
        wide,
        jnp.float32,
    )
    grad_down, grad_up = advance((grad_down, grad_up), moving)
    if aligned(skip_rows):
        total_skip = skip_scatter.total()
    share, ckv_share = share_of(row_count, seq_count), share_of(w_ckv.shape[0], seq_count)
    square = (row_count, model_width)
    grad_co, grad_cq, grad_ckv, grad_out = put_rows(
        blocks_of(jnp.concatenate([s.total() for s in scatters]), "seq"),
        ranks,
        [square, square, w_ckv.shape, square],
        [share, share, ckv_share, share],
    )
    grad_qkv = put_columns(
        blocks_of(total_qkv, "seq"),
        ranks,
        [[(at, first, size) for first, at, size in m] for m in qkv_moves],
        3 * model_width,
        jnp.float32,
    )
    grad_w_skip = join_columns(blocks_of(total_skip, "seq"), ranks, jnp.float32)
    return (
        block_out,
        grad_tokens,
        grad_skip,
        small[0:5],
        small[5:9],
        small[9],
        qk_total[0:2],
        qk_total[2:4],
        grad_w_skip,
        grad_mod,
        grad_qkv,
        grad_out,
        grad_cq,
        grad_ckv,
        grad_co,
        grad_up,
        grad_down,
    )


def solution(mesh):
    in_specs = (
        P(("dp", "seq"), None),
        P(("dp", "seq"), None),
        P("dp", None),
        P("dp", None),
        P("dp", None),
        P("dp", None),
        P("dp", None, None),
        P("dp", None, None),
        P(),
        P(),
        P(),
        P(),
        P("dp", None),
        P("dp", None),
        P("dp", None),
        P("dp", None),
        P("dp", None),
        P("dp", None),
        P("dp", None),
        P("dp", None),
        P("dp", None),
        P(("dp", "seq"), None),
    )
    out_specs = (
        P(("dp", "seq"), None),
        P(("dp", "seq"), None),
        P(("dp", "seq"), None),
        P(),
        P(),
        P(),
        P(),
        P(),
        P("dp", None),
        P("dp", None),
        P("dp", None),
        P("dp", None),
        P("dp", None),
        P("dp", None),
        P("dp", None),
        P("dp", None),
        P("dp", None),
    )
    return jax.shard_map(shards, mesh=mesh, in_specs=in_specs, out_specs=out_specs, check_vma=False)
```

```python
import functools
import jax
import jax.numpy as jnp
import numpy as np
from jax import lax
from jax.experimental import pallas as pl
from jax.experimental.pallas import tpu as pltpu
from jax.sharding import PartitionSpec as P

HEADS = 16
HEAD = 88
IMGS = 3
CAP = 333
CLIP_TOK = 77
LANES = 128
LOG2E = 1.4426950408889634
eps_norm = 1e-06
masked_score = -1e30
vmem_bytes = 60 * 1024 * 1024


def dot_nt(left, right):
    return lax.dot_general(
        left, right, (((1,), (1,)), ((), ())), preferred_element_type=jnp.float32
    )


def dot_tn(left, right):
    return lax.dot_general(
        left, right, (((0,), (0,)), ((), ())), preferred_element_type=jnp.float32
    )


def matmul(left, right):
    return jnp.dot(left, right, preferred_element_type=jnp.float32)


def widen(value):
    pad = jnp.zeros((value.shape[0], LANES - HEAD), value.dtype)
    return jnp.concatenate([value, pad], axis=1)


def lane_of(shape):
    return lax.broadcasted_iota(jnp.int32, shape, len(shape) - 1)


def head_norm(value):
    mean = jnp.sum(value, axis=1, keepdims=True) * (1.0 / HEAD)
    center = jnp.where(lane_of(value.shape) < HEAD, value - mean, 0.0)
    spread = jnp.sum(center * center, axis=1, keepdims=True) * (1.0 / HEAD)
    factor = lax.rsqrt(spread + eps_norm)
    return center * factor, factor


def turn(value, cos_t, sin_a, sin_b):
    ahead = pltpu.roll(value, LANES - HEAD // 4, 1)
    behind = pltpu.roll(value, HEAD // 4, 1)
    return value * cos_t + ahead * sin_a + behind * sin_b


def turn_back(value, cos_t, sin_a, sin_b):
    return (
        value * cos_t
        + pltpu.roll(value * sin_a, HEAD // 4, 1)
        + pltpu.roll(value * sin_b, LANES - HEAD // 4, 1)
    )


def prep_kernel(heads, pre_ref, cos_ref, sa_ref, sb_ref, seg_ref, gain_ref, bias_ref, out_ref):
    cos_t, sin_a, sin_b = cos_ref[...], sa_ref[...], sb_ref[...]
    seg = seg_ref[...]
    lane = lane_of(cos_t.shape)
    image = lane - HEAD
    own = jnp.where(image == seg, 1.0, 0.0)
    other = jnp.where((image >= 0) & (image < IMGS) & (image != seg), masked_score, 0.0)
    ones = jnp.where(image == 0, 1.0, 0.0)
    for kind in range(3):
        for head in range(heads):
            at = (kind * heads + head) * LANES
            value = pre_ref[:, at : at + LANES]
            if kind < 2:
                normed, _ = head_norm(value)
                value = normed * gain_ref[kind : kind + 1, :] + bias_ref[kind : kind + 1, :]
                value = turn(value, cos_t, sin_a, sin_b) + (own if kind == 0 else other)
            else:
                value = value + ones
            out_ref[:, at : at + LANES] = value.astype(jnp.bfloat16)


def prep_heads(pre, tables, seg, gains, biases, heads, rows):
    count = pre.shape[0]
    cols = 3 * heads * LANES
    wide = pl.BlockSpec((rows, LANES), lambda i: (i, 0))
    return pl.pallas_call(
        functools.partial(prep_kernel, heads),
        grid=(count // rows,),
        in_specs=[
            pl.BlockSpec((rows, pre.shape[1]), lambda i: (i, 0)),
            wide,
            wide,
            wide,
            pl.BlockSpec((rows, 1), lambda i: (i, 0)),
            pl.BlockSpec((2, LANES), lambda i: (0, 0)),
            pl.BlockSpec((2, LANES), lambda i: (0, 0)),
        ],
        out_specs=pl.BlockSpec((rows, cols), lambda i: (i, 0)),
        out_shape=jax.ShapeDtypeStruct((count, cols), jnp.bfloat16),
        compiler_params=pltpu.CompilerParams(vmem_limit_bytes=vmem_bytes),
        cost_estimate=pl.CostEstimate(
            flops=20 * count * cols, bytes_accessed=8 * count * cols, transcendentals=0
        ),
    )(pre, *tables, seg, gains, biases)


score_shift = 10.0


def self_exp(scores):
    return jnp.exp2(scores * (HEAD ** (-0.5) * LOG2E) - score_shift * LOG2E)


def self_forward_kernel(heads, q_ref, k_ref, v_ref, out_ref, inv_ref):
    outs = []
    invs = []
    for head in range(heads):
        cols = slice(head * LANES, (head + 1) * LANES)
        exps = self_exp(dot_nt(k_ref[:, cols], q_ref[:, cols])).astype(jnp.bfloat16)
        total = dot_tn(v_ref[:, cols], exps)
        inverse = 1.0 / total[HEAD : HEAD + 1, :]
        invs.append(inverse)
        outs.append((total * inverse).T[:, :HEAD].astype(jnp.bfloat16))
    out_ref[...] = jnp.concatenate(outs, axis=1)
    for head in range(heads):
        inv_ref[head : head + 1, :] = invs[head]


def self_forward(packed, heads, rows):
    count = packed.shape[0]
    cols = heads * LANES
    return pl.pallas_call(
        functools.partial(self_forward_kernel, heads),
        grid=(count // rows,),
        in_specs=[
            pl.BlockSpec((rows, cols), lambda i: (i, 0)),
            pl.BlockSpec((count, cols), lambda i: (0, 1)),
            pl.BlockSpec((count, cols), lambda i: (0, 2)),
        ],
        out_specs=[
            pl.BlockSpec((rows, heads * HEAD), lambda i: (i, 0)),
            pl.BlockSpec((heads, rows), lambda i: (0, i)),
        ],
        out_shape=[
            jax.ShapeDtypeStruct((count, heads * HEAD), jnp.bfloat16),
            jax.ShapeDtypeStruct((heads, count), jnp.float32),
        ],
        compiler_params=pltpu.CompilerParams(vmem_limit_bytes=vmem_bytes),
        cost_estimate=pl.CostEstimate(
            flops=4 * count * count * cols,
            bytes_accessed=8 * count * cols,
            transcendentals=count * count * heads,
        ),
    )(packed, packed, packed)


def self_backward_kernel(heads, blocks, q_ref, k_ref, v_ref, d_ref, inv_ref, dq_ref, dk_ref, dv_ref, key_sum, value_sum):
    step = pl.program_id(0)

    @pl.when(step == 0)
    def _():
        key_sum[...] = jnp.zeros_like(key_sum)
        value_sum[...] = jnp.zeros_like(value_sum)

    scale = HEAD ** (-0.5)
    for head in range(heads):
        cols = slice(head * LANES, (head + 1) * LANES)
        d_out = widen(d_ref[:, head * HEAD : (head + 1) * HEAD])
        query, key = q_ref[:, cols], k_ref[:, cols]
        probs = self_exp(dot_nt(key, query)) * inv_ref[head : head + 1, :]
        d_probs = dot_nt(v_ref[:, cols], d_out)
        weight = jnp.sum(probs * d_probs, axis=0, keepdims=True)
        d_scores = (probs * (d_probs - weight)).astype(jnp.bfloat16)
        value_sum[:, cols] += matmul(probs.astype(jnp.bfloat16), d_out)
        key_sum[:, cols] += matmul(d_scores, query)
        dq_ref[:, cols] = (dot_tn(d_scores, key) * scale).astype(jnp.bfloat16)

    @pl.when(step == blocks - 1)
    def _():
        dk_ref[...] = (key_sum[...] * scale).astype(jnp.bfloat16)
        dv_ref[...] = value_sum[...].astype(jnp.bfloat16)


def self_backward(packed, d_out, inverse, heads, rows):
    count = packed.shape[0]
    cols = heads * LANES
    blocks = count // rows
    whole = pl.BlockSpec((count, cols), lambda i: (0, 0))
    return pl.pallas_call(
        functools.partial(self_backward_kernel, heads, blocks),
        grid=(blocks,),
        in_specs=[
            pl.BlockSpec((rows, cols), lambda i: (i, 0)),
            pl.BlockSpec((count, cols), lambda i: (0, 1)),
            pl.BlockSpec((count, cols), lambda i: (0, 2)),
            pl.BlockSpec((rows, heads * HEAD), lambda i: (i, 0)),
            pl.BlockSpec((heads, rows), lambda i: (0, i)),
        ],
        out_specs=[pl.BlockSpec((rows, cols), lambda i: (i, 0)), whole, whole],
        out_shape=[jax.ShapeDtypeStruct((count, cols), jnp.bfloat16)] * 3,
        scratch_shapes=[pltpu.VMEM((count, cols), jnp.float32)] * 2,
        compiler_params=pltpu.CompilerParams(vmem_limit_bytes=vmem_bytes),
        cost_estimate=pl.CostEstimate(
            flops=10 * count * count * cols,
            bytes_accessed=14 * count * cols,
            transcendentals=count * count * heads,
        ),
    )(packed, packed, packed, d_out, inverse)


def prep_back_kernel(heads, pre_ref, dq_ref, dk_ref, dv_ref, cos_ref, sa_ref, sb_ref, gain_ref, out_ref, dg_ref, db_ref):
    step = pl.program_id(0)

    @pl.when(step == 0)
    def _():
        dg_ref[...] = jnp.zeros_like(dg_ref)
        db_ref[...] = jnp.zeros_like(db_ref)

    cos_t, sin_a, sin_b = cos_ref[...], sa_ref[...], sb_ref[...]
    live = lane_of(cos_t.shape) < HEAD
    for kind, d_ref in enumerate((dq_ref, dk_ref)):
        gain = gain_ref[kind : kind + 1, :]
        gain_sum = jnp.zeros((1, LANES), jnp.float32)
        bias_sum = jnp.zeros((1, LANES), jnp.float32)
        for head in range(heads):
            at = (kind * heads + head) * LANES
            normed, factor = head_norm(pre_ref[:, at : at + LANES])
            given = jnp.where(live, d_ref[:, head * LANES : (head + 1) * LANES].astype(jnp.float32), 0.0)
            d_normed = turn_back(given, cos_t, sin_a, sin_b)
            gain_sum = gain_sum + jnp.sum(d_normed * normed, axis=0, keepdims=True)
            bias_sum = bias_sum + jnp.sum(d_normed, axis=0, keepdims=True)
            scaled = d_normed * gain
            mean = jnp.sum(scaled, axis=1, keepdims=True) * (1.0 / HEAD)
            slope = jnp.sum(scaled * normed, axis=1, keepdims=True) * (1.0 / HEAD)
            result = jnp.where(live, factor * (scaled - mean - normed * slope), 0.0)
            out_ref[:, at : at + LANES] = result.astype(jnp.bfloat16)
        dg_ref[kind : kind + 1, :] += gain_sum
        db_ref[kind : kind + 1, :] += bias_sum
    out_ref[:, 2 * heads * LANES :] = dv_ref[...]


def prep_back(pre, d_query, d_key, d_value, tables, gains, heads, rows):
    count = pre.shape[0]
    cols = heads * LANES
    wide = pl.BlockSpec((rows, LANES), lambda i: (i, 0))
    headed = pl.BlockSpec((rows, cols), lambda i: (i, 0))
    small = pl.BlockSpec((2, LANES), lambda i: (0, 0))
    return pl.pallas_call(
        functools.partial(prep_back_kernel, heads),
        grid=(count // rows,),
        in_specs=[
            pl.BlockSpec((rows, pre.shape[1]), lambda i: (i, 0)),
            headed,
            headed,
            headed,
            wide,
            wide,
            wide,
            small,
        ],
        out_specs=[pl.BlockSpec((rows, pre.shape[1]), lambda i: (i, 0)), small, small],
        out_shape=[
            jax.ShapeDtypeStruct(pre.shape, jnp.bfloat16),
            jax.ShapeDtypeStruct((2, LANES), jnp.float32),
            jax.ShapeDtypeStruct((2, LANES), jnp.float32),
        ],
        compiler_params=pltpu.CompilerParams(vmem_limit_bytes=vmem_bytes),
        cost_estimate=pl.CostEstimate(
            flops=60 * count * cols, bytes_accessed=30 * count * cols, transcendentals=0
        ),
    )(pre, d_query, d_key, d_value, *tables, gains)


def cross_key(kv_ref, first, head, keys, penalty):
    key = widen(kv_ref[pl.ds(first, keys), head * HEAD : (head + 1) * HEAD])
    return jnp.where(lane_of(key.shape) == HEAD, penalty, key)


def cross_value(kv_ref, first, head, keys, width):
    at = width + head * HEAD
    value = widen(kv_ref[pl.ds(first, keys), at : at + HEAD])
    return jnp.where(lane_of(value.shape) == HEAD, jnp.bfloat16(1), value)


def cross_query(q_ref, head):
    query = widen(q_ref[:, head * HEAD : (head + 1) * HEAD])
    return jnp.where(lane_of(query.shape) == HEAD, jnp.bfloat16(1), query)


cross_factor = HEAD ** (-0.5) * LOG2E


def cross_forward_kernel(heads, keys, span_ref, q_ref, kv_ref, pen_ref, seg_ref, out_ref, top_ref, inv_ref, turned):
    width = heads * HEAD

    def image(index, carry):
        first = pl.multiple_of(index * keys, 16)
        penalty = pen_ref[pl.ds(first, keys), :]
        member = seg_ref[...] == index
        for head in range(heads):
            key = cross_key(kv_ref, first, head, keys, penalty)
            scores = dot_nt(key, cross_query(q_ref, head)) * cross_factor
            top = jnp.max(scores, axis=0, keepdims=True)
            exps = jnp.exp2(scores - top).astype(jnp.bfloat16)
            total = dot_tn(cross_value(kv_ref, first, head, keys, width), exps)
            inverse = 1.0 / total[HEAD : HEAD + 1, :]
            at = slice(head * LANES, (head + 1) * LANES)
            turned[at, :] = jnp.where(member, total * inverse, turned[at, :])
            top_ref[head : head + 1, :] = jnp.where(member, top, top_ref[head : head + 1, :])
            inv_ref[head : head + 1, :] = jnp.where(member, inverse, inv_ref[head : head + 1, :])
        return carry

    lax.fori_loop(span_ref[0], span_ref[1] + 1, image, 0)
    out_ref[...] = jnp.concatenate(
        [
            turned[head * LANES : (head + 1) * LANES, :].T[:, :HEAD].astype(jnp.bfloat16)
            for head in range(heads)
        ],
        axis=1,
    )


def cross_forward(query, text_kv, penalty, seg_row, span):
    count, width = query.shape
    heads = width // HEAD
    keys = text_kv.shape[0] // IMGS
    vmem = pl.BlockSpec(memory_space=pltpu.VMEM)
    return pl.pallas_call(
        functools.partial(cross_forward_kernel, heads, keys),
        in_specs=[pl.BlockSpec(memory_space=pltpu.SMEM)] + [vmem] * 4,
        out_specs=[vmem] * 3,
        out_shape=[
            jax.ShapeDtypeStruct((count, width), jnp.bfloat16),
            jax.ShapeDtypeStruct((heads, count), jnp.float32),
            jax.ShapeDtypeStruct((heads, count), jnp.float32),
        ],
        scratch_shapes=[pltpu.VMEM((heads * LANES, count), jnp.float32)],
        compiler_params=pltpu.CompilerParams(vmem_limit_bytes=vmem_bytes),
        cost_estimate=pl.CostEstimate(
            flops=8 * count * keys * heads * LANES,
            bytes_accessed=2 * text_kv.size + 8 * query.size,
            transcendentals=2 * count * keys * heads,
        ),
    )(span, query, text_kv, penalty, seg_row)


def cross_backward_kernel(heads, keys, span_ref, q_ref, kv_ref, pen_ref, seg_ref, top_ref, inv_ref, d_ref, dq_ref, dkv_ref, turned):
    width = heads * HEAD
    scale = HEAD ** (-0.5)
    turned[...] = jnp.zeros_like(turned)
    dkv_ref[...] = jnp.zeros_like(dkv_ref)

    def image(index, carry):
        first = pl.multiple_of(index * keys, 16)
        penalty = pen_ref[pl.ds(first, keys), :]
        member = seg_ref[...] == index
        d_keys, d_values = [], []
        for head in range(heads):
            key = cross_key(kv_ref, first, head, keys, penalty)
            query = cross_query(q_ref, head)
            d_out = widen(d_ref[:, head * HEAD : (head + 1) * HEAD])
            top = jnp.where(member, top_ref[head : head + 1, :], -masked_score)
            scores = dot_nt(key, query) * cross_factor
            probs = jnp.exp2(scores - top) * inv_ref[head : head + 1, :]
            d_probs = dot_nt(cross_value(kv_ref, first, head, keys, width), d_out)
            weight = jnp.sum(probs * d_probs, axis=0, keepdims=True)
            d_scores = (probs * (d_probs - weight)).astype(jnp.bfloat16)
            d_values.append(matmul(probs.astype(jnp.bfloat16), d_out)[:, :HEAD].astype(jnp.bfloat16))
            d_keys.append((matmul(d_scores, query) * scale)[:, :HEAD].astype(jnp.bfloat16))
            at = slice(head * LANES, (head + 1) * LANES)
            turned[at, :] += dot_tn(key, d_scores)
        dkv_ref[pl.ds(first, keys), :] = jnp.concatenate(d_keys + d_values, axis=1)
        return carry

    lax.fori_loop(span_ref[0], span_ref[1] + 1, image, 0)
    dq_ref[...] = jnp.concatenate(
        [
            (turned[head * LANES : (head + 1) * LANES, :] * scale).T[:, :HEAD].astype(jnp.bfloat16)
            for head in range(heads)
        ],
        axis=1,
    )


def cross_backward(query, text_kv, penalty, seg_row, span, top, inverse, d_out):
    count, width = query.shape
    heads = width // HEAD
    keys = text_kv.shape[0] // IMGS
    vmem = pl.BlockSpec(memory_space=pltpu.VMEM)
    return pl.pallas_call(
        functools.partial(cross_backward_kernel, heads, keys),
        in_specs=[pl.BlockSpec(memory_space=pltpu.SMEM)] + [vmem] * 7,
        out_specs=[vmem] * 2,
        out_shape=[
            jax.ShapeDtypeStruct((count, width), jnp.bfloat16),
            jax.ShapeDtypeStruct(text_kv.shape, jnp.bfloat16),
        ],
        scratch_shapes=[pltpu.VMEM((heads * LANES, count), jnp.float32)],
        compiler_params=pltpu.CompilerParams(vmem_limit_bytes=vmem_bytes),
        cost_estimate=pl.CostEstimate(
            flops=20 * count * keys * heads * LANES,
            bytes_accessed=4 * text_kv.size + 8 * query.size,
            transcendentals=2 * count * keys * heads,
        ),
    )(span, query, text_kv, penalty, seg_row, top, inverse, d_out)


def layer_norm(values, norm_gain, norm_bias):
    center = values - jnp.mean(values, axis=-1, keepdims=True)
    spread = jnp.mean(center * center, axis=-1, keepdims=True)
    return center * lax.rsqrt(spread + eps_norm) * norm_gain + norm_bias


def gelu_tanh(values):
    return (
        0.5
        * values
        * (1.0 + jnp.tanh(0.7978845608028654 * (values + 0.044715 * values * values * values)))
    )


def silu_gate(values):
    return values * jax.nn.sigmoid(values)


def grid_positions(seg_all, widths, first_tok, tok_count):
    images = jnp.arange(IMGS, dtype=jnp.int32)
    starts = jnp.sum((seg_all[None, :] < images[:, None]).astype(jnp.int32), axis=1)
    seg_part = lax.dynamic_slice_in_dim(seg_all, first_tok, tok_count)
    member = seg_part[:, None] == images[None, :]
    start_tok = jnp.sum(jnp.where(member, starts[None, :], 0), axis=1)
    width_tok = jnp.sum(jnp.where(member, widths[None, :], 0), axis=1)
    in_image = first_tok + jnp.arange(tok_count, dtype=jnp.int32) - start_tok
    return (
        seg_part,
        member,
        (in_image // width_tok).astype(jnp.float32),
        (in_image % width_tok).astype(jnp.float32),
    )


def swap(value, axis, mask):
    count = lax.axis_size(axis)
    return lax.ppermute(value, axis, [(rank, rank ^ mask) for rank in range(count)])


def blocks_of(block, axis):
    count = lax.axis_size(axis)
    held = {0: block}
    bit = count // 2
    while bit:
        for mask in list(held):
            held[mask | bit] = swap(held[mask], axis, bit)
        bit //= 2
    return [held[mask] for mask in range(count)]


def sum_parts(parts, axis, kind):
    count = lax.axis_size(axis)
    held = dict(enumerate(parts))
    bit = 1
    while bit < count:
        for mask in [m for m in held if m & bit]:
            came = swap(held.pop(mask).astype(kind), axis, bit)
            held[mask ^ bit] = held[mask ^ bit] + came.astype(jnp.float32)
        bit *= 2
    return held[0]


def gather_small(value, axis):
    bit = 1
    while bit < lax.axis_size(axis):
        value = jnp.concatenate([value, swap(value, axis, bit)])
        bit *= 2
    return value


def scatter_small(value, axis):
    bit = lax.axis_size(axis) // 2
    while bit:
        half = value.shape[0] // 2
        value = value[:half] + swap(value[half:], axis, bit)
        bit //= 2
    return value


def sum_all(value, axis):
    bit = 1
    while bit < lax.axis_size(axis):
        value = value + swap(value, axis, bit)
        bit *= 2
    return value


def exchange(parts, axis):
    return [parts[0]] + [swap(parts[mask], axis, mask) for mask in range(1, len(parts))]


def in_order(blocks, rank):
    stacked = jnp.stack(blocks)
    return [
        lax.dynamic_index_in_dim(stacked, rank ^ place, 0, keepdims=False)
        for place in range(len(blocks))
    ]


def share_of(rows, seq_count):
    if rows >= 16 * seq_count:
        return -(-rows // (16 * seq_count)) * 16
    return -(-rows // seq_count)


def rope_tables(row_pos, col_pos):
    lane = np.arange(LANES)
    half, quarter = HEAD // 2, HEAD // 4
    live = lane < HEAD
    index = lane % half % quarter
    frequency = np.where(live, 10000.0 ** (-(index * 4.0 / HEAD)), 0.0).astype(np.float32)
    front = live & (lane % half < quarter)
    back = live & (lane % half >= quarter)
    angle = jnp.where((lane < half)[None], row_pos[:, None], col_pos[:, None]) * frequency[None]
    sine = jnp.sin(angle)
    return (
        jnp.where(live[None], jnp.cos(angle), 0.0),
        jnp.where(front[None], -sine, 0.0),
        jnp.where(back[None], sine, 0.0),
    )


def caption_penalty(clip_len, t5_len, keys):
    slot = jnp.arange(keys, dtype=jnp.int32)[None]
    clip_live = (slot < CLIP_TOK) & (slot < clip_len[:, None])
    t5_live = (slot >= CLIP_TOK) & (slot < CAP) & (slot - CLIP_TOK < t5_len[:, None])
    return (
        jnp.where(clip_live | t5_live, 0.0, masked_score).astype(jnp.bfloat16).reshape(-1, 1)
    )


def pick_kernel(moves, ranks_ref, source, out):
    if sum(size for _, _, size in moves[0]) < out.shape[1]:
        out[...] = jnp.zeros_like(out)
    for place, moved in enumerate(moves):

        @pl.when(ranks_ref[1] == place)
        def _(moved=moved):
            for first, at, size in moved:
                out[:, at : at + size] = source[:, first : first + size]


def pick_columns(weight, ranks, moves, cols):
    vmem = pl.BlockSpec(memory_space=pltpu.VMEM)
    return pl.pallas_call(
        functools.partial(pick_kernel, moves),
        in_specs=[pl.BlockSpec(memory_space=pltpu.SMEM), vmem],
        out_specs=vmem,
        out_shape=jax.ShapeDtypeStruct((weight.shape[0], cols), weight.dtype),
        compiler_params=pltpu.CompilerParams(vmem_limit_bytes=vmem_bytes),
    )(ranks, weight)


def put_kernel(moves, ranks_ref, *refs):
    out = refs[-1]
    for mask, block in enumerate(refs[:-1]):
        for place, moved in enumerate(moves):

            @pl.when((ranks_ref[1] ^ mask) == place)
            def _(block=block, moved=moved):
                for first, at, size in moved:
                    out[:, at : at + size] = block[:, first : first + size].astype(out.dtype)


def put_columns(blocks, ranks, moves, cols, kind):
    vmem = pl.BlockSpec(memory_space=pltpu.VMEM)
    return pl.pallas_call(
        functools.partial(put_kernel, moves),
        in_specs=[pl.BlockSpec(memory_space=pltpu.SMEM)] + [vmem] * len(blocks),
        out_specs=vmem,
        out_shape=jax.ShapeDtypeStruct((blocks[0].shape[0], cols), kind),
        compiler_params=pltpu.CompilerParams(vmem_limit_bytes=vmem_bytes),
    )(ranks, *blocks)


def quarter_kernel(row_counts, shares, ranks_ref, *refs):
    outs = refs[-len(row_counts) :]
    quarters = refs[: -len(row_counts)]
    seq_count = len(quarters) * (quarters[0].shape[1] // sum(shares))
    for mask in range(seq_count):
        quarter = quarters[mask % len(quarters)]
        base = mask // len(quarters) * sum(shares)
        for place in range(seq_count):

            @pl.when((ranks_ref[1] ^ mask) == place)
            def _(quarter=quarter, place=place, base=base):
                first = base
                for out, rows, share in zip(outs, row_counts, shares):
                    size = min(share, rows - place * share)
                    if size > 0:
                        at = place * share
                        out[at : at + size, :] = quarter[0, first : first + size, :]
                    first += share


def place_quarters(quarters, ranks, row_counts, shares, bits):
    dp_count, held, cols = quarters[0].shape

    def rank_at(i, ranks):
        return ranks[0] ^ sum(bit * ((i >> place) & 1) for place, bit in enumerate(bits))

    return pl.pallas_call(
        functools.partial(quarter_kernel, row_counts, shares),
        grid_spec=pltpu.PrefetchScalarGridSpec(
            num_scalar_prefetch=1,
            grid=(dp_count,),
            in_specs=[pl.BlockSpec((1, held, cols), lambda i, ranks: (i, 0, 0))] * len(quarters),
            out_specs=[
                pl.BlockSpec((rows, cols), lambda i, ranks: (rank_at(i, ranks), 0))
                for rows in row_counts
            ],
        ),
        out_shape=[
            jax.ShapeDtypeStruct((dp_count * rows, cols), quarters[0].dtype)
            for rows in row_counts
        ],
        compiler_params=pltpu.CompilerParams(vmem_limit_bytes=vmem_bytes),
        cost_estimate=pl.CostEstimate(
            flops=0, bytes_accessed=4 * dp_count * sum(row_counts) * cols, transcendentals=0
        ),
    )(ranks, *quarters)


def bits_below(count):
    return [1 << place for place in reversed(range(count.bit_length() - 1))]


class Gather:
    def __init__(self, own, stages):
        self.stages = list(stages)
        self.start(own)

    def start(self, own):
        self.axis, bits, self.joined = self.stages.pop(0)
        self.bits = list(bits)
        self.masks = [0]
        for bit in reversed(bits):
            self.masks += [mask | bit for mask in self.masks]
        self.held, self.came, self.level = own[None] if self.joined else {0: own}, None, 0
        self.send()

    def send(self):
        if self.joined:
            if self.bits:
                self.came = swap(self.held, self.axis, self.bits.pop(0))
            elif self.stages:
                self.start(self.held)
            return
        self.level += 1
        masks = [m for m in self.masks if bin(m).count("1") == self.level]
        if masks:
            self.came = {
                m: swap(self.held[m & (m - 1)], self.axis, m & -m)
                for m in sorted(masks, key=lambda m: (m & -m, m), reverse=True)
            }

    def step(self):
        if self.came is None:
            return
        if self.joined:
            self.held = jnp.concatenate([self.held, self.came])
        else:
            self.held.update(self.came)
        self.came = None
        self.send()

    def finish(self):
        while self.came is not None:
            self.came = lax.optimization_barrier(self.came)
            self.step()
        return [self.held[m] for m in self.masks]


def own_shares(weights, ranks):
    seq_count = lax.axis_size("seq")
    shares = [share_of(w.shape[0], seq_count) for w in weights]
    return jnp.concatenate(
        [
            lax.dynamic_slice_in_dim(
                jnp.pad(w, ((0, share * seq_count - w.shape[0]), (0, 0))), ranks[1] * share, share
            )
            for w, share in zip(weights, shares)
        ]
    )


def aligned(rows):
    return rows % 16 == 0 and rows >= 16 * lax.axis_size("seq")


def split_kernel(ranks_ref, source, *outs):
    width = outs[0].shape[1]
    for mask, out in enumerate(outs):
        for place in range(len(outs)):

            @pl.when((ranks_ref[1] ^ mask) == place)
            def _(out=out, place=place):
                out[...] = source[:, place * width : (place + 1) * width]


def split_columns(value, ranks):
    count = lax.axis_size("seq")
    vmem = pl.BlockSpec(memory_space=pltpu.VMEM)
    block = jax.ShapeDtypeStruct((value.shape[0], value.shape[1] // count), value.dtype)
    return pl.pallas_call(
        split_kernel,
        in_specs=[pl.BlockSpec(memory_space=pltpu.SMEM), vmem],
        out_specs=[vmem] * count,
        out_shape=[block] * count,
        compiler_params=pltpu.CompilerParams(vmem_limit_bytes=vmem_bytes),
    )(ranks, value)


def join_columns(blocks, ranks, kind):
    width = blocks[0].shape[1]
    moves = [[(0, j * width, width)] for j in range(len(blocks))]
    return put_columns(blocks, ranks, moves, len(blocks) * width, kind)


def put_rows_kernel(shares, ranks_ref, *refs):
    outs = refs[-len(shares) :]
    blocks = refs[: -len(shares)]
    for mask, block in enumerate(blocks):
        for place in range(len(blocks)):

            @pl.when((ranks_ref[1] ^ mask) == place)
            def _(block=block, place=place):
                first = 0
                for out, share in zip(outs, shares):
                    size = min(share, out.shape[0] - place * share)
                    width = block.shape[1]
                    for half in range(out.shape[1] // width):
                        if size > 0:
                            out[place * share : place * share + size, half * width : (half + 1) * width] = block[
                                first : first + size, :
                            ].astype(out.dtype)
                        first += share


def put_rows(blocks, ranks, shapes, shares):
    vmem = pl.BlockSpec(memory_space=pltpu.VMEM)
    return pl.pallas_call(
        functools.partial(put_rows_kernel, shares),
        in_specs=[pl.BlockSpec(memory_space=pltpu.SMEM)] + [vmem] * len(blocks),
        out_specs=[vmem] * len(shapes),
        out_shape=[jax.ShapeDtypeStruct(shape, jnp.float32) for shape in shapes],
        compiler_params=pltpu.CompilerParams(vmem_limit_bytes=vmem_bytes),
    )(ranks, *blocks)


def shared_rows(grad, group=1):
    dp_count, seq_count = lax.axis_size("dp"), lax.axis_size("seq")
    low = grad.astype(jnp.bfloat16).reshape(dp_count, -1, grad.shape[1])
    rows = low.shape[1]
    share = share_of(rows, seq_count)
    low = jnp.pad(low, ((0, 0), (0, share * seq_count - rows), (0, 0)))
    low = low.reshape(dp_count, seq_count, share, -1)
    return jnp.concatenate(jnp.split(low, group, axis=3), axis=2)


class Scatter:
    def __init__(self, held, ranks, last=0):
        dp_count, seq_count = lax.axis_size("dp"), lax.axis_size("seq")
        self.held = held
        over_seq, over_dp = [], []
        bit = 1
        while bit < seq_count:
            over_seq.append(("seq", bit, ranks[1], 1))
            bit *= 2
        bit = 1
        while bit < dp_count:
            over_dp.append(("dp", bit, ranks[0], 0))
            bit *= 2
        first = len(over_seq) - last
        self.todo = over_seq[:first] + over_dp + over_seq[first:]
        self.came = None
        self.send()

    def send(self):
        if not self.todo:
            return
        axis, bit, rank, dim = self.todo.pop(0)
        shape = self.held.shape
        split = self.held.reshape(shape[:dim] + (shape[dim] // 2, 2) + shape[dim + 1 :])
        mine = (rank // bit) % 2
        self.held = lax.dynamic_index_in_dim(split, mine, dim + 1, keepdims=False)
        give = lax.dynamic_index_in_dim(split, 1 - mine, dim + 1, keepdims=False)
        self.came = swap(give, axis, bit)

    def step(self):
        if self.came is None:
            return
        total = self.held.astype(jnp.float32) + self.came.astype(jnp.float32)
        self.held, self.came = total.astype(jnp.bfloat16), None
        self.send()

    def total(self):
        while self.came is not None:
            self.step()
        return self.held.reshape(self.held.shape[2:])


def halves_kernel(summed, ranks_ref, *refs):
    if summed:
        keep, came, other, other_came, out, give = refs
        out[...] = (keep[...].astype(jnp.float32) + came[...].astype(jnp.float32)).astype(out.dtype)
        give[...] = (
            other[...].astype(jnp.float32) + other_came[...].astype(jnp.float32)
        ).astype(give.dtype)
    else:
        keep, other, out, give = refs
        out[...] = keep[...]
        give[...] = other[...]


def halves(held, came, ranks, bit):
    count, rows, cols = held.shape

    def mine(i, ranks):
        return (2 * i + (ranks[0] // bit) % 2, 0, 0)

    def others(i, ranks):
        return (2 * i + 1 - (ranks[0] // bit) % 2, 0, 0)

    block = (1, rows, cols)
    specs = [pl.BlockSpec(block, mine)] * (1 if came is None else 2)
    specs += [pl.BlockSpec(block, others)] * (1 if came is None else 2)
    operands = [held] * 2 if came is None else [held, came, held, came]
    out = jax.ShapeDtypeStruct((count // 2, rows, cols), held.dtype)
    return pl.pallas_call(
        functools.partial(halves_kernel, came is not None),
        grid_spec=pltpu.PrefetchScalarGridSpec(
            num_scalar_prefetch=1,
            grid=(count // 2,),
            in_specs=specs,
            out_specs=[pl.BlockSpec(block, lambda i, ranks: (i, 0, 0))] * 2,
        ),
        out_shape=[out, out],
        compiler_params=pltpu.CompilerParams(vmem_limit_bytes=vmem_bytes),
        cost_estimate=pl.CostEstimate(
            flops=0, bytes_accessed=6 * held.size, transcendentals=0
        ),
    )(ranks, *operands)


class PartScatter:
    def __init__(self, grad, ranks):
        count = lax.axis_size("dp")
        self.ranks, self.bit = ranks, 1
        self.held, give = halves(grad.reshape(count, -1, grad.shape[1]), None, ranks, 1)
        self.came = swap(give, "dp", 1)

    def step(self):
        if self.came is None:
            return
        if self.held.shape[0] > 1:
            self.bit *= 2
            self.held, give = halves(self.held, self.came, self.ranks, self.bit)
            self.came = swap(give, "dp", self.bit)
        else:
            total = self.held.astype(jnp.float32) + self.came.astype(jnp.float32)
            self.held, self.came = total.astype(self.held.dtype), None

    def total(self):
        while self.came is not None:
            self.step()
        return self.held[0]


class SumWay:
    def __init__(self, parts, axis):
        self.held, self.axis, self.bit = dict(enumerate(parts)), axis, 1
        self.came = None
        self.send()

    def send(self):
        if self.bit < lax.axis_size(self.axis):
            self.came = {
                mask ^ self.bit: swap(self.held.pop(mask).astype(jnp.bfloat16), self.axis, self.bit)
                for mask in sorted(self.held)
                if mask & self.bit
            }
            self.bit *= 2

    def step(self):
        if self.came is None:
            return
        for mask, arrived in self.came.items():
            self.held[mask] = self.held[mask].astype(jnp.float32) + arrived.astype(jnp.float32)
        self.came = None
        self.send()

    def total(self):
        while self.came is not None:
            self.step()
        return self.held[0]


def advance(value, scatters):
    active = [s for s in scatters if s.came is not None]
    value, came = lax.optimization_barrier((value, [s.came for s in active]))
    for scatter, arrived in zip(active, came):
        scatter.came = arrived
        scatter.step()
    return value


def shards(
    tokens,
    skip,
    segment_ids,
    grid_widths,
    clip_lengths,
    t5_lengths,
    timestep,
    captions,
    ln_gains,
    ln_biases,
    qk_gains,
    qk_biases,
    w_skip,
    w_mod,
    w_qkv,
    w_out,
    w_cq,
    w_ckv,
    w_co,
    w_up,
    w_down,
    cotangent,
):
    local_tok = tokens.shape[0]
    model_width = tokens.shape[1]
    seq_count = lax.axis_size("seq")
    dp_count = lax.axis_size("dp")
    seq_rank = lax.axis_index("seq")
    dp_rank = lax.axis_index("dp")
    ranks = jnp.stack([dp_rank, seq_rank])
    bucket_len = local_tok * seq_count
    local_heads = HEADS // seq_count
    head_cols = local_heads * HEAD
    wide = w_up.shape[1]
    part = wide // (dp_count * seq_count)
    local_wide = part * dp_count
    row_count = w_mod.shape[0]
    skip_rows = w_skip.shape[0]
    order = seq_rank ^ jnp.arange(seq_count, dtype=jnp.int32)
    seq_range = range(seq_count)

    up_moves = [
        [(r * seq_count * part + j * part, r * part, part) for r in range(dp_count)]
        for j in seq_range
    ]
    qkv_moves = [
        [
            (
                kind * model_width + j * head_cols + head * HEAD,
                (kind * local_heads + head) * LANES,
                HEAD,
            )
            for kind in range(3)
            for head in range(local_heads)
        ]
        for j in seq_range
    ]
    own_skip = lax.dynamic_slice_in_dim(w_skip, seq_rank * head_cols, head_cols, axis=1)
    part_skip = lax.all_gather(own_skip, "dp", axis=0, tiled=True)
    own_qkv = pick_columns(w_qkv, ranks, qkv_moves, 3 * local_heads * LANES)
    part_qkv = lax.all_gather(own_qkv, "dp", axis=0, tiled=True)
    dp_bits, seq_bits = bits_below(dp_count), bits_below(seq_count)
    joined = jnp.concatenate([tokens, skip], axis=1).astype(jnp.float32)
    h_float, pull_skip = jax.vjp(
        layer_norm, joined, ln_gains[0:2].reshape(-1), ln_biases[0:2].reshape(-1)
    )
    h_zero = h_float.astype(jnp.bfloat16)
    own_square = own_shares([w_out, w_cq, w_co], ranks)
    own_ckv = own_shares([w_ckv], ranks)
    own_up = pick_columns(w_up, ranks, up_moves, local_wide)
    h_zero, own_square, own_ckv, own_qkv = lax.optimization_barrier(
        (h_zero, own_square, own_ckv, own_qkv)
    )
    h_way = Gather(h_zero, [("seq", seq_bits, False)])
    ways = []
    if aligned(row_count):
        square_way = Gather(own_square, [("dp", dp_bits, True), ("seq", seq_bits, False)])
        ways.append(square_way)
    if aligned(w_ckv.shape[0]):
        ckv_way = Gather(
            own_ckv,
            [("seq", seq_bits[:-1], True), ("dp", dp_bits, True), ("seq", seq_bits[-1:], False)],
        )
        ways.append(ckv_way)
    seg_all = segment_ids[0]
    seg_local, member, _, _ = grid_positions(
        seg_all, grid_widths[0], seq_rank * local_tok, local_tok
    )
    _, _, row_all, col_all = grid_positions(seg_all, grid_widths[0], 0, bucket_len)

    def reorder(values):
        return jnp.take(values.reshape(seq_count, local_tok), order, axis=0).reshape(-1)

    tables = rope_tables(reorder(row_all), reorder(col_all))
    seg_column = reorder(seg_all)[:, None]
    lane_pad = ((0, 0), (0, LANES - HEAD))
    head_gains, head_biases = jnp.pad(qk_gains, lane_pad), jnp.pad(qk_biases, lane_pad)

    keys = -(-CAP // 16) * 16
    caption_rows = jnp.pad(
        captions[0].reshape(IMGS, CAP, -1), ((0, 0), (0, keys - CAP), (0, 0))
    ).reshape(IMGS * keys, -1)
    penalty = caption_penalty(clip_lengths[0], t5_lengths[0], keys)
    own_up, tables, seg_column, caption_rows, penalty = advance(
        (own_up, tables, seg_column, caption_rows, penalty), [h_way] + ways
    )
    h_all = jnp.concatenate(h_way.finish(), axis=0)
    x_cols = matmul(h_all, part_skip).astype(jnp.bfloat16).reshape(seq_count, local_tok, head_cols)
    x_one = join_columns(exchange([x_cols[k] for k in seq_range], "seq"), ranks, jnp.float32)

    cond = silu_gate(timestep[0].astype(jnp.float32)).astype(jnp.bfloat16)
    cond_all = gather_small(cond, "dp")
    xor_order = dp_rank ^ jnp.arange(dp_count, dtype=jnp.int32)
    cond_ranked = jnp.take(cond_all.reshape(dp_count, IMGS, model_width), xor_order, axis=0).reshape(
        dp_count * IMGS, model_width
    )
    cond_rows = lax.dynamic_slice_in_dim(cond_all, dp_rank * row_count, row_count, axis=1)
    shifts = scatter_small(matmul(cond_rows, w_mod), "dp")
    time_shift = jnp.sum(jnp.where(member[:, :, None], shifts[None], 0.0), axis=1)

    x_one, time_shift = advance((x_one, time_shift), ways[:1])
    n_float, pull_one = jax.vjp(layer_norm, x_one, ln_gains[2], ln_biases[2])
    n_one = (n_float + time_shift).astype(jnp.bfloat16)
    n_one_blocks, w_down = advance((blocks_of(n_one, "seq"), w_down), ways)
    own_down = lax.dynamic_slice_in_dim(w_down, seq_rank * part, part)
    part_down = lax.all_gather(own_down, "dp", axis=0, tiled=True)
    n_one_all = jnp.concatenate(n_one_blocks, axis=0)
    qkv_pre = matmul(n_one_all, part_qkv)
    packed = prep_heads(qkv_pre, tables, seg_column, head_gains, head_biases, local_heads, 256)
    head_out, inverse = self_forward(packed, local_heads, 256)
    head_out, own_up = advance((head_out, own_up), ways)
    part_up = lax.all_gather(own_up, "dp", axis=0, tiled=True)
    out_blocks = head_out.reshape(seq_count, local_tok, head_cols)
    attn_o = join_columns(exchange([out_blocks[k] for k in seq_range], "seq"), ranks, jnp.bfloat16)
    attn_o = advance(attn_o, ways)
    if aligned(row_count):
        full_out, full_cq, full_co = place_quarters(
            square_way.finish(),
            ranks,
            [row_count] * 3,
            [share_of(row_count, seq_count)] * 3,
            dp_bits,
        )
    else:
        full_out, full_cq, full_co = (
            lax.all_gather(w, "dp", axis=0, tiled=True) for w in (w_out, w_cq, w_co)
        )
    x_two = x_one + matmul(attn_o, full_out)
    n3_float, pull_three = jax.vjp(layer_norm, x_two, ln_gains[3], ln_biases[3])
    n_three = n3_float.astype(jnp.bfloat16)
    n_three, cotangent = advance((n_three, cotangent), ways)
    cross_q = matmul(n_three, full_cq).astype(jnp.bfloat16)
    if aligned(w_ckv.shape[0]):
        ckv_rows = w_ckv.shape[0]
        quarters = [q.reshape(dp_count, -1, w_ckv.shape[1]) for q in ckv_way.finish()]
        (full_ckv,) = place_quarters(
            quarters, ranks, [ckv_rows], [share_of(ckv_rows, seq_count)], dp_bits
        )
    else:
        full_ckv = lax.all_gather(w_ckv, "dp", axis=0, tiled=True)
    text_kv = matmul(caption_rows, full_ckv).astype(jnp.bfloat16)
    seg_row = seg_local[None]
    span = jnp.stack([seg_local[0], seg_local[-1]])
    cross_o, cross_top, cross_inv = cross_forward(cross_q, text_kv, penalty, seg_row, span)
    cross_o, cot_blocks, part_up = lax.optimization_barrier(
        (cross_o, blocks_of(cotangent, "seq"), part_up)
    )
    cot_all = jnp.concatenate(cot_blocks, axis=0)
    x_three = x_two + matmul(cross_o, full_co)
    n2_float, pull_two = jax.vjp(layer_norm, x_three, ln_gains[4], ln_biases[4])
    n_two = n2_float.astype(jnp.bfloat16)
    n_two_blocks, part_skip, part_down, cot_all = lax.optimization_barrier(
        (blocks_of(n_two, "seq"), part_skip, part_down, cot_all)
    )
    n_two_all = jnp.concatenate(n_two_blocks, axis=0)
    skip_blocks = blocks_of(part_skip, "seq")
    up_proj = matmul(n_two_all, part_up)
    act_float, pull_gelu = jax.vjp(gelu_tanh, up_proj)
    act_low = act_float.astype(jnp.bfloat16)
    down_part = matmul(act_low, part_down).astype(jnp.bfloat16)

    grad_down = matmul(act_low.T, cot_all).astype(jnp.bfloat16)
    d_act = matmul(cot_all, part_down.T)
    d_up = pull_gelu(d_act)[0].astype(jnp.bfloat16)
    d_two_part = matmul(d_up, part_up.T).astype(jnp.bfloat16)
    total_down = lax.psum_scatter(grad_down, "dp", scatter_dimension=0, tiled=True)
    d_two_part, skip_blocks = lax.optimization_barrier((d_two_part, skip_blocks))
    d_two_part = d_two_part.reshape(seq_count, local_tok, model_width)
    grad_up = matmul(n_two_all.T, d_up).astype(jnp.bfloat16)
    d_n_two = sum_parts([d_two_part[k] for k in seq_range], "seq", jnp.bfloat16)
    total_up = lax.psum_scatter(grad_up, "dp", scatter_dimension=0, tiled=True)
    d_n_two, _, _ = lax.optimization_barrier((d_n_two, grad_up, grad_down))
    back_three_x, gain_four, bias_four = pull_two(d_n_two)
    d_x_three = cotangent.astype(jnp.float32) + back_three_x
    d_co = d_x_three.astype(jnp.bfloat16)
    scatters = [Scatter(shared_rows(matmul(cross_o.T, d_co)), ranks, 1)]
    d_cross_o = matmul(d_co, full_co.T).astype(jnp.bfloat16)
    d_cross_q, d_text_kv = cross_backward(
        cross_q, text_kv, penalty, seg_row, span, cross_top, cross_inv, d_cross_o
    )
    d_cross_q = advance(d_cross_q, scatters)
    d_n_three = matmul(d_cross_q, full_cq.T)
    back_two_x, gain_three, bias_three = pull_three(d_n_three)
    d_x_two = d_x_three + back_two_x
    d_attn = d_x_two.astype(jnp.bfloat16)
    d_attn_o = matmul(d_attn, full_out.T).astype(jnp.bfloat16)
    d_turned = split_columns(d_attn_o, ranks)
    d_heads = jnp.concatenate(exchange(d_turned, "seq"), axis=0)
    grad_cross = jnp.concatenate(
        [
            shared_rows(matmul(n_three.T, d_cross_q)),
            shared_rows(matmul(caption_rows.T, d_text_kv), 2),
        ],
        axis=2,
    )
    scatters.append(Scatter(grad_cross, ranks))
    d_heads, down_part = advance((d_heads, down_part), scatters)
    down_part = down_part.reshape(seq_count, local_tok, model_width)
    block_way = SumWay([down_part[k] for k in seq_range], "seq")
    scatters.append(Scatter(shared_rows(matmul(attn_o.T, d_attn)), ranks, 1))
    d_query, d_key, d_value = self_backward(packed, d_heads, inverse, local_heads, 256)
    d_query, total_up = advance((d_query, total_up), scatters + [block_way])
    up_way = Gather(total_up, [("seq", seq_bits, False)])
    d_qkv, gain_qk, bias_qk = prep_back(
        qkv_pre, d_query, d_key, d_value, tables, head_gains, local_heads, 256
    )
    d_one_part = matmul(d_qkv, part_qkv.T).astype(jnp.bfloat16).reshape(seq_count, local_tok, model_width)
    grad_qkv = matmul(n_one_all.T, d_qkv).astype(jnp.bfloat16)
    total_qkv = lax.psum_scatter(grad_qkv, "dp", scatter_dimension=0, tiled=True)
    d_n_one = sum_parts([d_one_part[k] for k in seq_range], "seq", jnp.bfloat16)
    d_n_one, total_down = advance(
        (d_n_one, total_down), [block_way, up_way]
    )
    block_out = (x_three + block_way.total()).astype(jnp.bfloat16)
    down_way = Gather(total_down, [("seq", seq_bits, False)])
    back_one_x, gain_one, bias_one = pull_one(d_n_one)
    d_x_one = d_x_two + back_one_x
    d_y = d_x_one.astype(jnp.bfloat16)
    y_blocks = split_columns(d_y, ranks)
    y_cols = jnp.concatenate(exchange(y_blocks, "seq"), axis=0)
    grad_skip_w = matmul(h_all.T, y_cols).astype(jnp.bfloat16)
    grad_skip_w, d_n_one, y_blocks = lax.optimization_barrier((grad_skip_w, d_n_one, y_blocks))
    moving = scatters + [up_way, down_way]
    first_moving = moving
    if aligned(skip_rows):
        skip_scatter = PartScatter(grad_skip_w, ranks)
        y_blocks = advance(y_blocks, moving)
        first_moving, moving = [skip_scatter], [skip_scatter] + moving
    else:
        total_skip = lax.psum_scatter(grad_skip_w, "dp", scatter_dimension=0, tiled=True)

    d_shift = d_n_one.astype(jnp.bfloat16)
    d_image = matmul(member.astype(jnp.bfloat16).T, d_shift)
    d_h_zero = sum(dot_nt(y, w) for y, w in zip(y_blocks, skip_blocks))
    d_h_zero = advance(d_h_zero, first_moving)
    d_joined, gain_skip, bias_skip = advance(pull_skip(d_h_zero), moving)
    grad_tokens = d_joined[:, :model_width].astype(jnp.bfloat16)
    grad_skip = d_joined[:, model_width:].astype(jnp.bfloat16)
    qk_cols = 4 * HEAD
    mine = lax.broadcasted_iota(jnp.int32, (dp_count, 1, 1), 0) == dp_rank
    d_images = jnp.where(mine, d_image[None], 0.0).reshape(dp_count * IMGS, model_width)
    small = jnp.concatenate(
        [
            d_images,
            jnp.stack([gain_skip[:model_width], gain_skip[model_width:]]),
            jnp.stack([gain_one, gain_three, gain_four]),
            jnp.stack([bias_skip[:model_width], bias_skip[model_width:]]),
            jnp.stack([bias_one, bias_three, bias_four]),
            jnp.pad(
                jnp.concatenate([gain_qk[:, :HEAD], bias_qk[:, :HEAD]]).reshape(1, qk_cols),
                ((0, 0), (0, model_width - qk_cols)),
            ),
        ]
    )
    small = sum_all(sum_all(small, "dp"), "seq")
    cond_abs = lax.dynamic_slice_in_dim(
        cond_ranked, dp_rank * row_count, row_count, axis=1
    ).astype(jnp.float32)
    grad_mod = jnp.dot(
        cond_abs.T,
        small[: dp_count * IMGS],
        precision=lax.Precision.HIGHEST,
        preferred_element_type=jnp.float32,
    )
    d_image_all, small = small[: dp_count * IMGS], small[dp_count * IMGS :]
    qk_total = small[10, :qk_cols].reshape(4, HEAD)

    (grad_down,) = put_rows(down_way.finish(), ranks, [(seq_count * part, model_width)], [part])
    grad_up = put_columns(
        up_way.finish(),
        ranks,
        [[(at, first, size) for first, at, size in m] for m in up_moves],
        wide,
        jnp.float32,
    )
    grad_down, grad_up = advance((grad_down, grad_up), moving)
    if aligned(skip_rows):
        total_skip = skip_scatter.total()
    share, ckv_share = share_of(row_count, seq_count), share_of(w_ckv.shape[0], seq_count)
    square = (row_count, model_width)
    grad_co, grad_cq, grad_ckv, grad_out = put_rows(
        blocks_of(jnp.concatenate([s.total() for s in scatters]), "seq"),
        ranks,
        [square, square, w_ckv.shape, square],
        [share, share, ckv_share, share],
    )
    grad_qkv = put_columns(
        blocks_of(total_qkv, "seq"),
        ranks,
        [[(at, first, size) for first, at, size in m] for m in qkv_moves],
        3 * model_width,
        jnp.float32,
    )
    grad_w_skip = join_columns(blocks_of(total_skip, "seq"), ranks, jnp.float32)
    return (
        block_out,
        grad_tokens,
        grad_skip,
        small[0:5],
        small[5:9],
        small[9],
        qk_total[0:2],
        qk_total[2:4],
        grad_w_skip,
        grad_mod,
        grad_qkv,
        grad_out,
        grad_cq,
        grad_ckv,
        grad_co,
        grad_up,
        grad_down,
    )


def solution(mesh):
    in_specs = (
        P(("dp", "seq"), None),
        P(("dp", "seq"), None),
        P("dp", None),
        P("dp", None),
        P("dp", None),
        P("dp", None),
        P("dp", None, None),
        P("dp", None, None),
        P(),
        P(),
        P(),
        P(),
        P("dp", None),
        P("dp", None),
        P("dp", None),
        P("dp", None),
        P("dp", None),
        P("dp", None),
        P("dp", None),
        P("dp", None),
        P("dp", None),
        P(("dp", "seq"), None),
    )
    out_specs = (
        P(("dp", "seq"), None),
        P(("dp", "seq"), None),
        P(("dp", "seq"), None),
        P(),
        P(),
        P(),
        P(),
        P(),
        P("dp", None),
        P("dp", None),
        P("dp", None),
        P("dp", None),
        P("dp", None),
        P("dp", None),
        P("dp", None),
        P("dp", None),
        P("dp", None),
    )
    return jax.shard_map(shards, mesh=mesh, in_specs=in_specs, out_specs=out_specs, check_vma=False)
```

```python
import functools
import jax
import jax.numpy as jnp
import numpy as np
from jax import lax
from jax.experimental import pallas as pl
from jax.experimental.pallas import tpu as pltpu
from jax.sharding import PartitionSpec as P

HEADS = 16
HEAD = 88
IMGS = 3
CAP = 333
CLIP_TOK = 77
LANES = 128
LOG2E = 1.4426950408889634
eps_norm = 1e-06
masked_score = -1e30
vmem_bytes = 60 * 1024 * 1024


def dot_nt(left, right):
    return lax.dot_general(
        left, right, (((1,), (1,)), ((), ())), preferred_element_type=jnp.float32
    )


def dot_tn(left, right):
    return lax.dot_general(
        left, right, (((0,), (0,)), ((), ())), preferred_element_type=jnp.float32
    )


def matmul(left, right):
    return jnp.dot(left, right, preferred_element_type=jnp.float32)


def widen(value):
    pad = jnp.zeros((value.shape[0], LANES - HEAD), value.dtype)
    return jnp.concatenate([value, pad], axis=1)


def lane_of(shape):
    return lax.broadcasted_iota(jnp.int32, shape, len(shape) - 1)


def head_norm(value):
    mean = jnp.sum(value, axis=1, keepdims=True) * (1.0 / HEAD)
    center = jnp.where(lane_of(value.shape) < HEAD, value - mean, 0.0)
    spread = jnp.sum(center * center, axis=1, keepdims=True) * (1.0 / HEAD)
    factor = lax.rsqrt(spread + eps_norm)
    return center * factor, factor


def turn(value, cos_t, sin_a, sin_b):
    ahead = pltpu.roll(value, LANES - HEAD // 4, 1)
    behind = pltpu.roll(value, HEAD // 4, 1)
    return value * cos_t + ahead * sin_a + behind * sin_b


def turn_back(value, cos_t, sin_a, sin_b):
    return (
        value * cos_t
        + pltpu.roll(value * sin_a, HEAD // 4, 1)
        + pltpu.roll(value * sin_b, LANES - HEAD // 4, 1)
    )


def prep_kernel(heads, pre_ref, cos_ref, sa_ref, sb_ref, seg_ref, gain_ref, bias_ref, out_ref):
    cos_t, sin_a, sin_b = cos_ref[...], sa_ref[...], sb_ref[...]
    seg = seg_ref[...]
    lane = lane_of(cos_t.shape)
    image = lane - HEAD
    own = jnp.where(image == seg, 1.0, 0.0)
    other = jnp.where((image >= 0) & (image < IMGS) & (image != seg), masked_score, 0.0)
    ones = jnp.where(image == 0, 1.0, 0.0)
    for kind in range(3):
        for head in range(heads):
            at = (kind * heads + head) * LANES
            value = pre_ref[:, at : at + LANES]
            if kind < 2:
                normed, _ = head_norm(value)
                value = normed * gain_ref[kind : kind + 1, :] + bias_ref[kind : kind + 1, :]
                value = turn(value, cos_t, sin_a, sin_b) + (own if kind == 0 else other)
            else:
                value = value + ones
            out_ref[:, at : at + LANES] = value.astype(jnp.bfloat16)


def prep_heads(pre, tables, seg, gains, biases, heads, rows):
    count = pre.shape[0]
    cols = 3 * heads * LANES
    wide = pl.BlockSpec((rows, LANES), lambda i: (i, 0))
    return pl.pallas_call(
        functools.partial(prep_kernel, heads),
        grid=(count // rows,),
        in_specs=[
            pl.BlockSpec((rows, pre.shape[1]), lambda i: (i, 0)),
            wide,
            wide,
            wide,
            pl.BlockSpec((rows, 1), lambda i: (i, 0)),
            pl.BlockSpec((2, LANES), lambda i: (0, 0)),
            pl.BlockSpec((2, LANES), lambda i: (0, 0)),
        ],
        out_specs=pl.BlockSpec((rows, cols), lambda i: (i, 0)),
        out_shape=jax.ShapeDtypeStruct((count, cols), jnp.bfloat16),
        compiler_params=pltpu.CompilerParams(vmem_limit_bytes=vmem_bytes),
        cost_estimate=pl.CostEstimate(
            flops=20 * count * cols, bytes_accessed=8 * count * cols, transcendentals=0
        ),
    )(pre, *tables, seg, gains, biases)


score_shift = 10.0


def self_exp(scores):
    return jnp.exp2(scores * (HEAD ** (-0.5) * LOG2E) - score_shift * LOG2E)


def self_forward_kernel(heads, q_ref, k_ref, v_ref, out_ref, inv_ref):
    outs = []
    invs = []
    for head in range(heads):
        cols = slice(head * LANES, (head + 1) * LANES)
        exps = self_exp(dot_nt(k_ref[:, cols], q_ref[:, cols])).astype(jnp.bfloat16)
        total = dot_tn(v_ref[:, cols], exps)
        inverse = 1.0 / total[HEAD : HEAD + 1, :]
        invs.append(inverse)
        outs.append((total * inverse).T[:, :HEAD].astype(jnp.bfloat16))
    out_ref[...] = jnp.concatenate(outs, axis=1)
    for head in range(heads):
        inv_ref[head : head + 1, :] = invs[head]


def self_forward(packed, heads, rows):
    count = packed.shape[0]
    cols = heads * LANES
    return pl.pallas_call(
        functools.partial(self_forward_kernel, heads),
        grid=(count // rows,),
        in_specs=[
            pl.BlockSpec((rows, cols), lambda i: (i, 0)),
            pl.BlockSpec((count, cols), lambda i: (0, 1)),
            pl.BlockSpec((count, cols), lambda i: (0, 2)),
        ],
        out_specs=[
            pl.BlockSpec((rows, heads * HEAD), lambda i: (i, 0)),
            pl.BlockSpec((heads, rows), lambda i: (0, i)),
        ],
        out_shape=[
            jax.ShapeDtypeStruct((count, heads * HEAD), jnp.bfloat16),
            jax.ShapeDtypeStruct((heads, count), jnp.float32),
        ],
        compiler_params=pltpu.CompilerParams(vmem_limit_bytes=vmem_bytes),
        cost_estimate=pl.CostEstimate(
            flops=4 * count * count * cols,
            bytes_accessed=8 * count * cols,
            transcendentals=count * count * heads,
        ),
    )(packed, packed, packed)


def self_backward_kernel(heads, blocks, q_ref, k_ref, v_ref, d_ref, inv_ref, dq_ref, dk_ref, dv_ref, key_sum, value_sum):
    step = pl.program_id(0)

    @pl.when(step == 0)
    def _():
        key_sum[...] = jnp.zeros_like(key_sum)
        value_sum[...] = jnp.zeros_like(value_sum)

    scale = HEAD ** (-0.5)
    for head in range(heads):
        cols = slice(head * LANES, (head + 1) * LANES)
        d_out = widen(d_ref[:, head * HEAD : (head + 1) * HEAD])
        query, key = q_ref[:, cols], k_ref[:, cols]
        probs = self_exp(dot_nt(key, query)) * inv_ref[head : head + 1, :]
        d_probs = dot_nt(v_ref[:, cols], d_out)
        weight = jnp.sum(probs * d_probs, axis=0, keepdims=True)
        d_scores = (probs * (d_probs - weight)).astype(jnp.bfloat16)
        value_sum[:, cols] += matmul(probs.astype(jnp.bfloat16), d_out)
        key_sum[:, cols] += matmul(d_scores, query)
        dq_ref[:, cols] = (dot_tn(d_scores, key) * scale).astype(jnp.bfloat16)

    @pl.when(step == blocks - 1)
    def _():
        dk_ref[...] = (key_sum[...] * scale).astype(jnp.bfloat16)
        dv_ref[...] = value_sum[...].astype(jnp.bfloat16)


def self_backward(packed, d_out, inverse, heads, rows):
    count = packed.shape[0]
    cols = heads * LANES
    blocks = count // rows
    whole = pl.BlockSpec((count, cols), lambda i: (0, 0))
    return pl.pallas_call(
        functools.partial(self_backward_kernel, heads, blocks),
        grid=(blocks,),
        in_specs=[
            pl.BlockSpec((rows, cols), lambda i: (i, 0)),
            pl.BlockSpec((count, cols), lambda i: (0, 1)),
            pl.BlockSpec((count, cols), lambda i: (0, 2)),
            pl.BlockSpec((rows, heads * HEAD), lambda i: (i, 0)),
            pl.BlockSpec((heads, rows), lambda i: (0, i)),
        ],
        out_specs=[pl.BlockSpec((rows, cols), lambda i: (i, 0)), whole, whole],
        out_shape=[jax.ShapeDtypeStruct((count, cols), jnp.bfloat16)] * 3,
        scratch_shapes=[pltpu.VMEM((count, cols), jnp.float32)] * 2,
        compiler_params=pltpu.CompilerParams(vmem_limit_bytes=vmem_bytes),
        cost_estimate=pl.CostEstimate(
            flops=10 * count * count * cols,
            bytes_accessed=14 * count * cols,
            transcendentals=count * count * heads,
        ),
    )(packed, packed, packed, d_out, inverse)


def prep_back_kernel(heads, pre_ref, dq_ref, dk_ref, dv_ref, cos_ref, sa_ref, sb_ref, gain_ref, out_ref, dg_ref, db_ref):
    step = pl.program_id(0)

    @pl.when(step == 0)
    def _():
        dg_ref[...] = jnp.zeros_like(dg_ref)
        db_ref[...] = jnp.zeros_like(db_ref)

    cos_t, sin_a, sin_b = cos_ref[...], sa_ref[...], sb_ref[...]
    live = lane_of(cos_t.shape) < HEAD
    for kind, d_ref in enumerate((dq_ref, dk_ref)):
        gain = gain_ref[kind : kind + 1, :]
        gain_sum = jnp.zeros((1, LANES), jnp.float32)
        bias_sum = jnp.zeros((1, LANES), jnp.float32)
        for head in range(heads):
            at = (kind * heads + head) * LANES
            normed, factor = head_norm(pre_ref[:, at : at + LANES])
            given = jnp.where(live, d_ref[:, head * LANES : (head + 1) * LANES].astype(jnp.float32), 0.0)
            d_normed = turn_back(given, cos_t, sin_a, sin_b)
            gain_sum = gain_sum + jnp.sum(d_normed * normed, axis=0, keepdims=True)
            bias_sum = bias_sum + jnp.sum(d_normed, axis=0, keepdims=True)
            scaled = d_normed * gain
            mean = jnp.sum(scaled, axis=1, keepdims=True) * (1.0 / HEAD)
            slope = jnp.sum(scaled * normed, axis=1, keepdims=True) * (1.0 / HEAD)
            result = jnp.where(live, factor * (scaled - mean - normed * slope), 0.0)
            out_ref[:, at : at + LANES] = result.astype(jnp.bfloat16)
        dg_ref[kind : kind + 1, :] += gain_sum
        db_ref[kind : kind + 1, :] += bias_sum
    out_ref[:, 2 * heads * LANES :] = dv_ref[...]


def prep_back(pre, d_query, d_key, d_value, tables, gains, heads, rows):
    count = pre.shape[0]
    cols = heads * LANES
    wide = pl.BlockSpec((rows, LANES), lambda i: (i, 0))
    headed = pl.BlockSpec((rows, cols), lambda i: (i, 0))
    small = pl.BlockSpec((2, LANES), lambda i: (0, 0))
    return pl.pallas_call(
        functools.partial(prep_back_kernel, heads),
        grid=(count // rows,),
        in_specs=[
            pl.BlockSpec((rows, pre.shape[1]), lambda i: (i, 0)),
            headed,
            headed,
            headed,
            wide,
            wide,
            wide,
            small,
        ],
        out_specs=[pl.BlockSpec((rows, pre.shape[1]), lambda i: (i, 0)), small, small],
        out_shape=[
            jax.ShapeDtypeStruct(pre.shape, jnp.bfloat16),
            jax.ShapeDtypeStruct((2, LANES), jnp.float32),
            jax.ShapeDtypeStruct((2, LANES), jnp.float32),
        ],
        compiler_params=pltpu.CompilerParams(vmem_limit_bytes=vmem_bytes),
        cost_estimate=pl.CostEstimate(
            flops=60 * count * cols, bytes_accessed=30 * count * cols, transcendentals=0
        ),
    )(pre, d_query, d_key, d_value, *tables, gains)


def cross_key(kv_ref, first, head, keys, penalty):
    key = widen(kv_ref[pl.ds(first, keys), head * HEAD : (head + 1) * HEAD])
    return jnp.where(lane_of(key.shape) == HEAD, penalty, key)


def cross_value(kv_ref, first, head, keys, width):
    at = width + head * HEAD
    value = widen(kv_ref[pl.ds(first, keys), at : at + HEAD])
    return jnp.where(lane_of(value.shape) == HEAD, jnp.bfloat16(1), value)


def cross_query(q_ref, head):
    query = widen(q_ref[:, head * HEAD : (head + 1) * HEAD])
    return jnp.where(lane_of(query.shape) == HEAD, jnp.bfloat16(1), query)


cross_factor = HEAD ** (-0.5) * LOG2E


def cross_forward_kernel(heads, keys, span_ref, q_ref, kv_ref, pen_ref, seg_ref, out_ref, top_ref, inv_ref, turned):
    width = heads * HEAD

    def image(index, carry):
        first = pl.multiple_of(index * keys, 16)
        penalty = pen_ref[pl.ds(first, keys), :]
        member = seg_ref[...] == index
        for head in range(heads):
            key = cross_key(kv_ref, first, head, keys, penalty)
            scores = dot_nt(key, cross_query(q_ref, head)) * cross_factor
            top = jnp.max(scores, axis=0, keepdims=True)
            exps = jnp.exp2(scores - top).astype(jnp.bfloat16)
            total = dot_tn(cross_value(kv_ref, first, head, keys, width), exps)
            inverse = 1.0 / total[HEAD : HEAD + 1, :]
            at = slice(head * LANES, (head + 1) * LANES)
            turned[at, :] = jnp.where(member, total * inverse, turned[at, :])
            top_ref[head : head + 1, :] = jnp.where(member, top, top_ref[head : head + 1, :])
            inv_ref[head : head + 1, :] = jnp.where(member, inverse, inv_ref[head : head + 1, :])
        return carry

    lax.fori_loop(span_ref[0], span_ref[1] + 1, image, 0)
    out_ref[...] = jnp.concatenate(
        [
            turned[head * LANES : (head + 1) * LANES, :].T[:, :HEAD].astype(jnp.bfloat16)
            for head in range(heads)
        ],
        axis=1,
    )


def cross_forward(query, text_kv, penalty, seg_row, span):
    count, width = query.shape
    heads = width // HEAD
    keys = text_kv.shape[0] // IMGS
    vmem = pl.BlockSpec(memory_space=pltpu.VMEM)
    return pl.pallas_call(
        functools.partial(cross_forward_kernel, heads, keys),
        in_specs=[pl.BlockSpec(memory_space=pltpu.SMEM)] + [vmem] * 4,
        out_specs=[vmem] * 3,
        out_shape=[
            jax.ShapeDtypeStruct((count, width), jnp.bfloat16),
            jax.ShapeDtypeStruct((heads, count), jnp.float32),
            jax.ShapeDtypeStruct((heads, count), jnp.float32),
        ],
        scratch_shapes=[pltpu.VMEM((heads * LANES, count), jnp.float32)],
        compiler_params=pltpu.CompilerParams(vmem_limit_bytes=vmem_bytes),
        cost_estimate=pl.CostEstimate(
            flops=8 * count * keys * heads * LANES,
            bytes_accessed=2 * text_kv.size + 8 * query.size,
            transcendentals=2 * count * keys * heads,
        ),
    )(span, query, text_kv, penalty, seg_row)


def cross_backward_kernel(heads, keys, span_ref, q_ref, kv_ref, pen_ref, seg_ref, top_ref, inv_ref, d_ref, dq_ref, dkv_ref, turned):
    width = heads * HEAD
    scale = HEAD ** (-0.5)
    turned[...] = jnp.zeros_like(turned)
    dkv_ref[...] = jnp.zeros_like(dkv_ref)

    def image(index, carry):
        first = pl.multiple_of(index * keys, 16)
        penalty = pen_ref[pl.ds(first, keys), :]
        member = seg_ref[...] == index
        d_keys, d_values = [], []
        for head in range(heads):
            key = cross_key(kv_ref, first, head, keys, penalty)
            query = cross_query(q_ref, head)
            d_out = widen(d_ref[:, head * HEAD : (head + 1) * HEAD])
            top = jnp.where(member, top_ref[head : head + 1, :], -masked_score)
            scores = dot_nt(key, query) * cross_factor
            probs = jnp.exp2(scores - top) * inv_ref[head : head + 1, :]
            d_probs = dot_nt(cross_value(kv_ref, first, head, keys, width), d_out)
            weight = jnp.sum(probs * d_probs, axis=0, keepdims=True)
            d_scores = (probs * (d_probs - weight)).astype(jnp.bfloat16)
            d_values.append(matmul(probs.astype(jnp.bfloat16), d_out)[:, :HEAD].astype(jnp.bfloat16))
            d_keys.append((matmul(d_scores, query) * scale)[:, :HEAD].astype(jnp.bfloat16))
            at = slice(head * LANES, (head + 1) * LANES)
            turned[at, :] += dot_tn(key, d_scores)
        dkv_ref[pl.ds(first, keys), :] = jnp.concatenate(d_keys + d_values, axis=1)
        return carry

    lax.fori_loop(span_ref[0], span_ref[1] + 1, image, 0)
    dq_ref[...] = jnp.concatenate(
        [
            (turned[head * LANES : (head + 1) * LANES, :] * scale).T[:, :HEAD].astype(jnp.bfloat16)
            for head in range(heads)
        ],
        axis=1,
    )


def cross_backward(query, text_kv, penalty, seg_row, span, top, inverse, d_out):
    count, width = query.shape
    heads = width // HEAD
    keys = text_kv.shape[0] // IMGS
    vmem = pl.BlockSpec(memory_space=pltpu.VMEM)
    return pl.pallas_call(
        functools.partial(cross_backward_kernel, heads, keys),
        in_specs=[pl.BlockSpec(memory_space=pltpu.SMEM)] + [vmem] * 7,
        out_specs=[vmem] * 2,
        out_shape=[
            jax.ShapeDtypeStruct((count, width), jnp.bfloat16),
            jax.ShapeDtypeStruct(text_kv.shape, jnp.bfloat16),
        ],
        scratch_shapes=[pltpu.VMEM((heads * LANES, count), jnp.float32)],
        compiler_params=pltpu.CompilerParams(vmem_limit_bytes=vmem_bytes),
        cost_estimate=pl.CostEstimate(
            flops=20 * count * keys * heads * LANES,
            bytes_accessed=4 * text_kv.size + 8 * query.size,
            transcendentals=2 * count * keys * heads,
        ),
    )(span, query, text_kv, penalty, seg_row, top, inverse, d_out)


def layer_norm(values, norm_gain, norm_bias):
    center = values - jnp.mean(values, axis=-1, keepdims=True)
    spread = jnp.mean(center * center, axis=-1, keepdims=True)
    return center * lax.rsqrt(spread + eps_norm) * norm_gain + norm_bias


def gelu_tanh(values):
    return (
        0.5
        * values
        * (1.0 + jnp.tanh(0.7978845608028654 * (values + 0.044715 * values * values * values)))
    )


def silu_gate(values):
    return values * jax.nn.sigmoid(values)


def grid_positions(seg_all, widths, first_tok, tok_count):
    images = jnp.arange(IMGS, dtype=jnp.int32)
    starts = jnp.sum((seg_all[None, :] < images[:, None]).astype(jnp.int32), axis=1)
    seg_part = lax.dynamic_slice_in_dim(seg_all, first_tok, tok_count)
    member = seg_part[:, None] == images[None, :]
    start_tok = jnp.sum(jnp.where(member, starts[None, :], 0), axis=1)
    width_tok = jnp.sum(jnp.where(member, widths[None, :], 0), axis=1)
    in_image = first_tok + jnp.arange(tok_count, dtype=jnp.int32) - start_tok
    return (
        seg_part,
        member,
        (in_image // width_tok).astype(jnp.float32),
        (in_image % width_tok).astype(jnp.float32),
    )


def swap(value, axis, mask):
    count = lax.axis_size(axis)
    return lax.ppermute(value, axis, [(rank, rank ^ mask) for rank in range(count)])


def blocks_of(block, axis):
    count = lax.axis_size(axis)
    held = {0: block}
    bit = count // 2
    while bit:
        for mask in list(held):
            held[mask | bit] = swap(held[mask], axis, bit)
        bit //= 2
    return [held[mask] for mask in range(count)]


def sum_parts(parts, axis, kind):
    count = lax.axis_size(axis)
    held = dict(enumerate(parts))
    bit = 1
    while bit < count:
        for mask in [m for m in held if m & bit]:
            came = swap(held.pop(mask).astype(kind), axis, bit)
            held[mask ^ bit] = held[mask ^ bit] + came.astype(jnp.float32)
        bit *= 2
    return held[0]


def gather_small(value, axis):
    bit = 1
    while bit < lax.axis_size(axis):
        value = jnp.concatenate([value, swap(value, axis, bit)])
        bit *= 2
    return value


def scatter_small(value, axis):
    bit = lax.axis_size(axis) // 2
    while bit:
        half = value.shape[0] // 2
        value = value[:half] + swap(value[half:], axis, bit)
        bit //= 2
    return value


def sum_all(value, axis):
    bit = 1
    while bit < lax.axis_size(axis):
        value = value + swap(value, axis, bit)
        bit *= 2
    return value


def exchange(parts, axis):
    return [parts[0]] + [swap(parts[mask], axis, mask) for mask in range(1, len(parts))]


def in_order(blocks, rank):
    stacked = jnp.stack(blocks)
    return [
        lax.dynamic_index_in_dim(stacked, rank ^ place, 0, keepdims=False)
        for place in range(len(blocks))
    ]


def share_of(rows, seq_count):
    if rows >= 16 * seq_count:
        return -(-rows // (16 * seq_count)) * 16
    return -(-rows // seq_count)


def rope_tables(row_pos, col_pos):
    lane = np.arange(LANES)
    half, quarter = HEAD // 2, HEAD // 4
    live = lane < HEAD
    index = lane % half % quarter
    frequency = np.where(live, 10000.0 ** (-(index * 4.0 / HEAD)), 0.0).astype(np.float32)
    front = live & (lane % half < quarter)
    back = live & (lane % half >= quarter)
    angle = jnp.where((lane < half)[None], row_pos[:, None], col_pos[:, None]) * frequency[None]
    sine = jnp.sin(angle)
    return (
        jnp.where(live[None], jnp.cos(angle), 0.0),
        jnp.where(front[None], -sine, 0.0),
        jnp.where(back[None], sine, 0.0),
    )


def caption_penalty(clip_len, t5_len, keys):
    slot = jnp.arange(keys, dtype=jnp.int32)[None]
    clip_live = (slot < CLIP_TOK) & (slot < clip_len[:, None])
    t5_live = (slot >= CLIP_TOK) & (slot < CAP) & (slot - CLIP_TOK < t5_len[:, None])
    return (
        jnp.where(clip_live | t5_live, 0.0, masked_score).astype(jnp.bfloat16).reshape(-1, 1)
    )


def pick_kernel(moves, ranks_ref, source, out):
    if sum(size for _, _, size in moves[0]) < out.shape[1]:
        out[...] = jnp.zeros_like(out)
    for place, moved in enumerate(moves):

        @pl.when(ranks_ref[1] == place)
        def _(moved=moved):
            for first, at, size in moved:
                out[:, at : at + size] = source[:, first : first + size]


def pick_columns(weight, ranks, moves, cols):
    vmem = pl.BlockSpec(memory_space=pltpu.VMEM)
    return pl.pallas_call(
        functools.partial(pick_kernel, moves),
        in_specs=[pl.BlockSpec(memory_space=pltpu.SMEM), vmem],
        out_specs=vmem,
        out_shape=jax.ShapeDtypeStruct((weight.shape[0], cols), weight.dtype),
        compiler_params=pltpu.CompilerParams(vmem_limit_bytes=vmem_bytes),
    )(ranks, weight)


def put_kernel(moves, ranks_ref, *refs):
    out = refs[-1]
    for mask, block in enumerate(refs[:-1]):
        for place, moved in enumerate(moves):

            @pl.when((ranks_ref[1] ^ mask) == place)
            def _(block=block, moved=moved):
                for first, at, size in moved:
                    out[:, at : at + size] = block[:, first : first + size].astype(out.dtype)


def put_columns(blocks, ranks, moves, cols, kind):
    vmem = pl.BlockSpec(memory_space=pltpu.VMEM)
    return pl.pallas_call(
        functools.partial(put_kernel, moves),
        in_specs=[pl.BlockSpec(memory_space=pltpu.SMEM)] + [vmem] * len(blocks),
        out_specs=vmem,
        out_shape=jax.ShapeDtypeStruct((blocks[0].shape[0], cols), kind),
        compiler_params=pltpu.CompilerParams(vmem_limit_bytes=vmem_bytes),
    )(ranks, *blocks)


def quarter_kernel(row_counts, shares, ranks_ref, *refs):
    outs = refs[-len(row_counts) :]
    quarters = refs[: -len(row_counts)]
    seq_count = len(quarters) * (quarters[0].shape[1] // sum(shares))
    for mask in range(seq_count):
        quarter = quarters[mask % len(quarters)]
        base = mask // len(quarters) * sum(shares)
        for place in range(seq_count):

            @pl.when((ranks_ref[1] ^ mask) == place)
            def _(quarter=quarter, place=place, base=base):
                first = base
                for out, rows, share in zip(outs, row_counts, shares):
                    size = min(share, rows - place * share)
                    if size > 0:
                        at = place * share
                        out[at : at + size, :] = quarter[0, first : first + size, :]
                    first += share


def place_quarters(quarters, ranks, row_counts, shares, bits):
    dp_count, held, cols = quarters[0].shape

    def rank_at(i, ranks):
        return ranks[0] ^ sum(bit * ((i >> place) & 1) for place, bit in enumerate(bits))

    return pl.pallas_call(
        functools.partial(quarter_kernel, row_counts, shares),
        grid_spec=pltpu.PrefetchScalarGridSpec(
            num_scalar_prefetch=1,
            grid=(dp_count,),
            in_specs=[pl.BlockSpec((1, held, cols), lambda i, ranks: (i, 0, 0))] * len(quarters),
            out_specs=[
                pl.BlockSpec((rows, cols), lambda i, ranks: (rank_at(i, ranks), 0))
                for rows in row_counts
            ],
        ),
        out_shape=[
            jax.ShapeDtypeStruct((dp_count * rows, cols), quarters[0].dtype)
            for rows in row_counts
        ],
        compiler_params=pltpu.CompilerParams(vmem_limit_bytes=vmem_bytes),
        cost_estimate=pl.CostEstimate(
            flops=0, bytes_accessed=4 * dp_count * sum(row_counts) * cols, transcendentals=0
        ),
    )(ranks, *quarters)


def bits_below(count):
    return [1 << place for place in reversed(range(count.bit_length() - 1))]


class Gather:
    def __init__(self, own, stages):
        self.stages = list(stages)
        self.start(own)

    def start(self, own):
        self.axis, bits, self.joined = self.stages.pop(0)
        self.bits = list(bits)
        self.masks = [0]
        for bit in reversed(bits):
            self.masks += [mask | bit for mask in self.masks]
        self.held, self.came, self.level = own[None] if self.joined else {0: own}, None, 0
        self.send()

    def send(self):
        if self.joined:
            if self.bits:
                self.came = swap(self.held, self.axis, self.bits.pop(0))
            elif self.stages:
                self.start(self.held)
            return
        self.level += 1
        masks = [m for m in self.masks if bin(m).count("1") == self.level]
        if masks:
            self.came = {
                m: swap(self.held[m & (m - 1)], self.axis, m & -m)
                for m in sorted(masks, key=lambda m: (m & -m, m), reverse=True)
            }

    def step(self):
        if self.came is None:
            return
        if self.joined:
            self.held = jnp.concatenate([self.held, self.came])
        else:
            self.held.update(self.came)
        self.came = None
        self.send()

    def finish(self):
        while self.came is not None:
            self.came = lax.optimization_barrier(self.came)
            self.step()
        return [self.held[m] for m in self.masks]


def own_shares(weights, ranks):
    seq_count = lax.axis_size("seq")
    shares = [share_of(w.shape[0], seq_count) for w in weights]
    return jnp.concatenate(
        [
            lax.dynamic_slice_in_dim(
                jnp.pad(w, ((0, share * seq_count - w.shape[0]), (0, 0))), ranks[1] * share, share
            )
            for w, share in zip(weights, shares)
        ]
    )


def aligned(rows):
    return rows % 16 == 0 and rows >= 16 * lax.axis_size("seq")


def split_kernel(ranks_ref, source, *outs):
    width = outs[0].shape[1]
    for mask, out in enumerate(outs):
        for place in range(len(outs)):

            @pl.when((ranks_ref[1] ^ mask) == place)
            def _(out=out, place=place):
                out[...] = source[:, place * width : (place + 1) * width]


def split_columns(value, ranks):
    count = lax.axis_size("seq")
    vmem = pl.BlockSpec(memory_space=pltpu.VMEM)
    block = jax.ShapeDtypeStruct((value.shape[0], value.shape[1] // count), value.dtype)
    return pl.pallas_call(
        split_kernel,
        in_specs=[pl.BlockSpec(memory_space=pltpu.SMEM), vmem],
        out_specs=[vmem] * count,
        out_shape=[block] * count,
        compiler_params=pltpu.CompilerParams(vmem_limit_bytes=vmem_bytes),
    )(ranks, value)


def join_columns(blocks, ranks, kind):
    width = blocks[0].shape[1]
    moves = [[(0, j * width, width)] for j in range(len(blocks))]
    return put_columns(blocks, ranks, moves, len(blocks) * width, kind)


def put_rows_kernel(shares, ranks_ref, *refs):
    outs = refs[-len(shares) :]
    blocks = refs[: -len(shares)]
    for mask, block in enumerate(blocks):
        for place in range(len(blocks)):

            @pl.when((ranks_ref[1] ^ mask) == place)
            def _(block=block, place=place):
                first = 0
                for out, share in zip(outs, shares):
                    size = min(share, out.shape[0] - place * share)
                    width = block.shape[1]
                    for half in range(out.shape[1] // width):
                        if size > 0:
                            out[place * share : place * share + size, half * width : (half + 1) * width] = block[
                                first : first + size, :
                            ].astype(out.dtype)
                        first += share


def put_rows(blocks, ranks, shapes, shares):
    vmem = pl.BlockSpec(memory_space=pltpu.VMEM)
    return pl.pallas_call(
        functools.partial(put_rows_kernel, shares),
        in_specs=[pl.BlockSpec(memory_space=pltpu.SMEM)] + [vmem] * len(blocks),
        out_specs=[vmem] * len(shapes),
        out_shape=[jax.ShapeDtypeStruct(shape, jnp.float32) for shape in shapes],
        compiler_params=pltpu.CompilerParams(vmem_limit_bytes=vmem_bytes),
    )(ranks, *blocks)


def shared_rows(grad, group=1):
    dp_count, seq_count = lax.axis_size("dp"), lax.axis_size("seq")
    low = grad.astype(jnp.bfloat16).reshape(dp_count, -1, grad.shape[1])
    rows = low.shape[1]
    share = share_of(rows, seq_count)
    low = jnp.pad(low, ((0, 0), (0, share * seq_count - rows), (0, 0)))
    low = low.reshape(dp_count, seq_count, share, -1)
    return jnp.concatenate(jnp.split(low, group, axis=3), axis=2)


class Scatter:
    def __init__(self, held, ranks, last=0):
        dp_count, seq_count = lax.axis_size("dp"), lax.axis_size("seq")
        self.held = held
        over_seq, over_dp = [], []
        bit = 1
        while bit < seq_count:
            over_seq.append(("seq", bit, ranks[1], 1))
            bit *= 2
        bit = 1
        while bit < dp_count:
            over_dp.append(("dp", bit, ranks[0], 0))
            bit *= 2
        first = len(over_seq) - last
        self.todo = over_seq[:first] + over_dp + over_seq[first:]
        self.came = None
        self.send()

    def send(self):
        if not self.todo:
            return
        axis, bit, rank, dim = self.todo.pop(0)
        shape = self.held.shape
        split = self.held.reshape(shape[:dim] + (shape[dim] // 2, 2) + shape[dim + 1 :])
        mine = (rank // bit) % 2
        self.held = lax.dynamic_index_in_dim(split, mine, dim + 1, keepdims=False)
        give = lax.dynamic_index_in_dim(split, 1 - mine, dim + 1, keepdims=False)
        self.came = swap(give, axis, bit)

    def step(self):
        if self.came is None:
            return
        total = self.held.astype(jnp.float32) + self.came.astype(jnp.float32)
        self.held, self.came = total.astype(jnp.bfloat16), None
        self.send()

    def total(self):
        while self.came is not None:
            self.step()
        return self.held.reshape(self.held.shape[2:])


def halves_kernel(summed, ranks_ref, *refs):
    if summed:
        keep, came, other, other_came, out, give = refs
        out[...] = (keep[...].astype(jnp.float32) + came[...].astype(jnp.float32)).astype(out.dtype)
        give[...] = (
            other[...].astype(jnp.float32) + other_came[...].astype(jnp.float32)
        ).astype(give.dtype)
    else:
        keep, other, out, give = refs
        out[...] = keep[...]
        give[...] = other[...]


def halves(held, came, ranks, bit):
    count, rows, cols = held.shape

    def mine(i, ranks):
        return (2 * i + (ranks[0] // bit) % 2, 0, 0)

    def others(i, ranks):
        return (2 * i + 1 - (ranks[0] // bit) % 2, 0, 0)

    block = (1, rows, cols)
    specs = [pl.BlockSpec(block, mine)] * (1 if came is None else 2)
    specs += [pl.BlockSpec(block, others)] * (1 if came is None else 2)
    operands = [held] * 2 if came is None else [held, came, held, came]
    out = jax.ShapeDtypeStruct((count // 2, rows, cols), held.dtype)
    return pl.pallas_call(
        functools.partial(halves_kernel, came is not None),
        grid_spec=pltpu.PrefetchScalarGridSpec(
            num_scalar_prefetch=1,
            grid=(count // 2,),
            in_specs=specs,
            out_specs=[pl.BlockSpec(block, lambda i, ranks: (i, 0, 0))] * 2,
        ),
        out_shape=[out, out],
        compiler_params=pltpu.CompilerParams(vmem_limit_bytes=vmem_bytes),
        cost_estimate=pl.CostEstimate(
            flops=0, bytes_accessed=6 * held.size, transcendentals=0
        ),
    )(ranks, *operands)


class PartScatter:
    def __init__(self, grad, ranks):
        count = lax.axis_size("dp")
        self.ranks, self.bit = ranks, 1
        self.held, give = halves(grad.reshape(count, -1, grad.shape[1]), None, ranks, 1)
        self.came = swap(give, "dp", 1)

    def step(self):
        if self.came is None:
            return
        if self.held.shape[0] > 1:
            self.bit *= 2
            self.held, give = halves(self.held, self.came, self.ranks, self.bit)
            self.came = swap(give, "dp", self.bit)
        else:
            total = self.held.astype(jnp.float32) + self.came.astype(jnp.float32)
            self.held, self.came = total.astype(self.held.dtype), None

    def total(self):
        while self.came is not None:
            self.step()
        return self.held[0]


class SumWay:
    def __init__(self, parts, axis):
        self.held, self.axis, self.bit = dict(enumerate(parts)), axis, 1
        self.came = None
        self.send()

    def send(self):
        if self.bit < lax.axis_size(self.axis):
            self.came = {
                mask ^ self.bit: swap(self.held.pop(mask).astype(jnp.bfloat16), self.axis, self.bit)
                for mask in sorted(self.held)
                if mask & self.bit
            }
            self.bit *= 2

    def step(self):
        if self.came is None:
            return
        for mask, arrived in self.came.items():
            self.held[mask] = self.held[mask].astype(jnp.float32) + arrived.astype(jnp.float32)
        self.came = None
        self.send()

    def total(self):
        while self.came is not None:
            self.step()
        return self.held[0]


def advance(value, scatters):
    active = [s for s in scatters if s.came is not None]
    value, came = lax.optimization_barrier((value, [s.came for s in active]))
    for scatter, arrived in zip(active, came):
        scatter.came = arrived
        scatter.step()
    return value


def shards(
    tokens,
    skip,
    segment_ids,
    grid_widths,
    clip_lengths,
    t5_lengths,
    timestep,
    captions,
    ln_gains,
    ln_biases,
    qk_gains,
    qk_biases,
    w_skip,
    w_mod,
    w_qkv,
    w_out,
    w_cq,
    w_ckv,
    w_co,
    w_up,
    w_down,
    cotangent,
):
    local_tok = tokens.shape[0]
    model_width = tokens.shape[1]
    seq_count = lax.axis_size("seq")
    dp_count = lax.axis_size("dp")
    seq_rank = lax.axis_index("seq")
    dp_rank = lax.axis_index("dp")
    ranks = jnp.stack([dp_rank, seq_rank])
    bucket_len = local_tok * seq_count
    local_heads = HEADS // seq_count
    head_cols = local_heads * HEAD
    wide = w_up.shape[1]
    part = wide // (dp_count * seq_count)
    local_wide = part * dp_count
    row_count = w_mod.shape[0]
    skip_rows = w_skip.shape[0]
    order = seq_rank ^ jnp.arange(seq_count, dtype=jnp.int32)
    seq_range = range(seq_count)

    up_moves = [
        [(r * seq_count * part + j * part, r * part, part) for r in range(dp_count)]
        for j in seq_range
    ]
    qkv_moves = [
        [
            (
                kind * model_width + j * head_cols + head * HEAD,
                (kind * local_heads + head) * LANES,
                HEAD,
            )
            for kind in range(3)
            for head in range(local_heads)
        ]
        for j in seq_range
    ]
    own_skip = lax.dynamic_slice_in_dim(w_skip, seq_rank * head_cols, head_cols, axis=1)
    part_skip = lax.all_gather(own_skip, "dp", axis=0, tiled=True)
    own_qkv = pick_columns(w_qkv, ranks, qkv_moves, 3 * local_heads * LANES)
    part_qkv = lax.all_gather(own_qkv, "dp", axis=0, tiled=True)
    dp_bits, seq_bits = bits_below(dp_count), bits_below(seq_count)
    joined = jnp.concatenate([tokens, skip], axis=1).astype(jnp.float32)
    h_float, pull_skip = jax.vjp(
        layer_norm, joined, ln_gains[0:2].reshape(-1), ln_biases[0:2].reshape(-1)
    )
    h_zero = h_float.astype(jnp.bfloat16)
    own_square = own_shares([w_out, w_cq, w_co], ranks)
    own_ckv = own_shares([w_ckv], ranks)
    own_up = pick_columns(w_up, ranks, up_moves, local_wide)
    h_zero, own_square, own_ckv, own_qkv = lax.optimization_barrier(
        (h_zero, own_square, own_ckv, own_qkv)
    )
    h_way = Gather(h_zero, [("seq", seq_bits, False)])
    ways = []
    if aligned(row_count):
        square_way = Gather(own_square, [("dp", dp_bits, True), ("seq", seq_bits, False)])
        ways.append(square_way)
    if aligned(w_ckv.shape[0]):
        ckv_way = Gather(
            own_ckv,
            [("seq", seq_bits[:-1], True), ("dp", dp_bits, True), ("seq", seq_bits[-1:], False)],
        )
        ways.append(ckv_way)
    seg_all = segment_ids[0]
    seg_local, member, _, _ = grid_positions(
        seg_all, grid_widths[0], seq_rank * local_tok, local_tok
    )
    _, _, row_all, col_all = grid_positions(seg_all, grid_widths[0], 0, bucket_len)

    def reorder(values):
        return jnp.take(values.reshape(seq_count, local_tok), order, axis=0).reshape(-1)

    tables = rope_tables(reorder(row_all), reorder(col_all))
    seg_column = reorder(seg_all)[:, None]
    lane_pad = ((0, 0), (0, LANES - HEAD))
    head_gains, head_biases = jnp.pad(qk_gains, lane_pad), jnp.pad(qk_biases, lane_pad)

    keys = -(-CAP // 16) * 16
    caption_rows = jnp.pad(
        captions[0].reshape(IMGS, CAP, -1), ((0, 0), (0, keys - CAP), (0, 0))
    ).reshape(IMGS * keys, -1)
    penalty = caption_penalty(clip_lengths[0], t5_lengths[0], keys)
    own_up, tables, seg_column, caption_rows, penalty = advance(
        (own_up, tables, seg_column, caption_rows, penalty), [h_way] + ways
    )
    h_all = jnp.concatenate(h_way.finish(), axis=0)
    x_cols = matmul(h_all, part_skip).astype(jnp.bfloat16).reshape(seq_count, local_tok, head_cols)
    x_one = join_columns(exchange([x_cols[k] for k in seq_range], "seq"), ranks, jnp.float32)

    cond = silu_gate(timestep[0].astype(jnp.float32)).astype(jnp.bfloat16)
    cond_all = gather_small(cond, "dp")
    xor_order = dp_rank ^ jnp.arange(dp_count, dtype=jnp.int32)
    cond_ranked = jnp.take(cond_all.reshape(dp_count, IMGS, model_width), xor_order, axis=0).reshape(
        dp_count * IMGS, model_width
    )
    cond_rows = lax.dynamic_slice_in_dim(cond_all, dp_rank * row_count, row_count, axis=1)
    shifts = scatter_small(matmul(cond_rows, w_mod), "dp")
    time_shift = jnp.sum(jnp.where(member[:, :, None], shifts[None], 0.0), axis=1)

    x_one, time_shift = advance((x_one, time_shift), ways)
    n_float, pull_one = jax.vjp(layer_norm, x_one, ln_gains[2], ln_biases[2])
    n_one = (n_float + time_shift).astype(jnp.bfloat16)
    n_one_blocks, w_down = advance((blocks_of(n_one, "seq"), w_down), ways)
    own_down = lax.dynamic_slice_in_dim(w_down, seq_rank * part, part)
    part_down = lax.all_gather(own_down, "dp", axis=0, tiled=True)
    n_one_all = jnp.concatenate(n_one_blocks, axis=0)
    qkv_pre = matmul(n_one_all, part_qkv)
    packed = prep_heads(qkv_pre, tables, seg_column, head_gains, head_biases, local_heads, 256)
    head_out, inverse = self_forward(packed, local_heads, 256)
    head_out, own_up = advance((head_out, own_up), ways)
    part_up = lax.all_gather(own_up, "dp", axis=0, tiled=True)
    out_blocks = head_out.reshape(seq_count, local_tok, head_cols)
    attn_o = join_columns(exchange([out_blocks[k] for k in seq_range], "seq"), ranks, jnp.bfloat16)
    attn_o = advance(attn_o, ways)
    if aligned(w_ckv.shape[0]):
        ckv_rows = w_ckv.shape[0]
        quarters = [q.reshape(dp_count, -1, w_ckv.shape[1]) for q in ckv_way.finish()]
        (full_ckv,) = place_quarters(
            quarters, ranks, [ckv_rows], [share_of(ckv_rows, seq_count)], dp_bits
        )
    else:
        full_ckv = lax.all_gather(w_ckv, "dp", axis=0, tiled=True)
    if aligned(row_count):
        full_out, full_cq, full_co = place_quarters(
            square_way.finish(),
            ranks,
            [row_count] * 3,
            [share_of(row_count, seq_count)] * 3,
            dp_bits,
        )
    else:
        full_out, full_cq, full_co = (
            lax.all_gather(w, "dp", axis=0, tiled=True) for w in (w_out, w_cq, w_co)
        )
    x_two = x_one + matmul(attn_o, full_out)
    n3_float, pull_three = jax.vjp(layer_norm, x_two, ln_gains[3], ln_biases[3])
    n_three = n3_float.astype(jnp.bfloat16)
    n_three, cotangent = lax.optimization_barrier((n_three, cotangent))
    cross_q = matmul(n_three, full_cq).astype(jnp.bfloat16)
    text_kv = matmul(caption_rows, full_ckv).astype(jnp.bfloat16)
    seg_row = seg_local[None]
    span = jnp.stack([seg_local[0], seg_local[-1]])
    cross_o, cross_top, cross_inv = cross_forward(cross_q, text_kv, penalty, seg_row, span)
    cross_o, cot_blocks, part_up = lax.optimization_barrier(
        (cross_o, blocks_of(cotangent, "seq"), part_up)
    )
    cot_all = jnp.concatenate(cot_blocks, axis=0)
    x_three = x_two + matmul(cross_o, full_co)
    n2_float, pull_two = jax.vjp(layer_norm, x_three, ln_gains[4], ln_biases[4])
    n_two = n2_float.astype(jnp.bfloat16)
    n_two_way = Gather(n_two, [("seq", seq_bits, False)])
    cot_all, part_down = advance((cot_all, part_down), [n_two_way])
    n_two_blocks, part_skip = lax.optimization_barrier((n_two_way.finish(), part_skip))
    n_two_all = jnp.concatenate(n_two_blocks, axis=0)
    skip_blocks = blocks_of(part_skip, "seq")
    up_proj = matmul(n_two_all, part_up)
    act_float, pull_gelu = jax.vjp(gelu_tanh, up_proj)
    act_low = act_float.astype(jnp.bfloat16)
    down_part = matmul(act_low, part_down).astype(jnp.bfloat16)

    grad_down = matmul(act_low.T, cot_all).astype(jnp.bfloat16)
    d_act = matmul(cot_all, part_down.T)
    d_up = pull_gelu(d_act)[0].astype(jnp.bfloat16)
    d_two_part = matmul(d_up, part_up.T).astype(jnp.bfloat16)
    total_down = lax.psum_scatter(grad_down, "dp", scatter_dimension=0, tiled=True)
    d_two_part, skip_blocks = lax.optimization_barrier((d_two_part, skip_blocks))
    d_two_part = d_two_part.reshape(seq_count, local_tok, model_width)
    grad_up = matmul(n_two_all.T, d_up).astype(jnp.bfloat16)
    d_n_two = sum_parts([d_two_part[k] for k in seq_range], "seq", jnp.bfloat16)
    total_up = lax.psum_scatter(grad_up, "dp", scatter_dimension=0, tiled=True)
    d_n_two, _, _ = lax.optimization_barrier((d_n_two, grad_up, grad_down))
    back_three_x, gain_four, bias_four = pull_two(d_n_two)
    d_x_three = cotangent.astype(jnp.float32) + back_three_x
    d_co = d_x_three.astype(jnp.bfloat16)
    scatters = [Scatter(shared_rows(matmul(cross_o.T, d_co)), ranks, 1)]
    d_cross_o = matmul(d_co, full_co.T).astype(jnp.bfloat16)
    d_cross_q, d_text_kv = cross_backward(
        cross_q, text_kv, penalty, seg_row, span, cross_top, cross_inv, d_cross_o
    )
    d_cross_q = advance(d_cross_q, scatters)
    d_n_three = matmul(d_cross_q, full_cq.T)
    back_two_x, gain_three, bias_three = pull_three(d_n_three)
    d_x_two = d_x_three + back_two_x
    d_attn = d_x_two.astype(jnp.bfloat16)
    d_attn_o = matmul(d_attn, full_out.T).astype(jnp.bfloat16)
    d_turned = split_columns(d_attn_o, ranks)
    d_heads = jnp.concatenate(exchange(d_turned, "seq"), axis=0)
    grad_cross = jnp.concatenate(
        [
            shared_rows(matmul(n_three.T, d_cross_q)),
            shared_rows(matmul(caption_rows.T, d_text_kv), 2),
        ],
        axis=2,
    )
    scatters.append(Scatter(grad_cross, ranks))
    d_heads, down_part = advance((d_heads, down_part), scatters)
    down_part = down_part.reshape(seq_count, local_tok, model_width)
    block_way = SumWay([down_part[k] for k in seq_range], "seq")
    scatters.append(Scatter(shared_rows(matmul(attn_o.T, d_attn)), ranks, 1))
    d_query, d_key, d_value = self_backward(packed, d_heads, inverse, local_heads, 256)
    d_query, total_up = advance((d_query, total_up), scatters + [block_way])
    up_way = Gather(total_up, [("seq", seq_bits, False)])
    d_qkv, gain_qk, bias_qk = prep_back(
        qkv_pre, d_query, d_key, d_value, tables, head_gains, local_heads, 256
    )
    d_one_part = matmul(d_qkv, part_qkv.T).astype(jnp.bfloat16).reshape(seq_count, local_tok, model_width)
    grad_qkv = matmul(n_one_all.T, d_qkv).astype(jnp.bfloat16)
    total_qkv = lax.psum_scatter(grad_qkv, "dp", scatter_dimension=0, tiled=True)
    d_n_one = sum_parts([d_one_part[k] for k in seq_range], "seq", jnp.bfloat16)
    d_n_one, total_down = advance(
        (d_n_one, total_down), []
    )
    down_way = Gather(total_down, [("seq", seq_bits, False)])
    back_one_x, gain_one, bias_one = pull_one(d_n_one)
    d_x_one = d_x_two + back_one_x
    d_y = d_x_one.astype(jnp.bfloat16)
    y_blocks = split_columns(d_y, ranks)
    y_cols = jnp.concatenate(exchange(y_blocks, "seq"), axis=0)
    grad_skip_w = matmul(h_all.T, y_cols).astype(jnp.bfloat16)
    grad_skip_w, d_n_one, y_blocks = lax.optimization_barrier((grad_skip_w, d_n_one, y_blocks))
    moving = scatters + [up_way, down_way, block_way]
    first_moving = moving
    if aligned(skip_rows):
        skip_scatter = PartScatter(grad_skip_w, ranks)
        y_blocks = advance(y_blocks, moving)
        first_moving, moving = [skip_scatter], [skip_scatter] + moving
    else:
        total_skip = lax.psum_scatter(grad_skip_w, "dp", scatter_dimension=0, tiled=True)

    d_shift = d_n_one.astype(jnp.bfloat16)
    d_image = matmul(member.astype(jnp.bfloat16).T, d_shift)
    d_h_zero = sum(dot_nt(y, w) for y, w in zip(y_blocks, skip_blocks))
    d_h_zero = advance(d_h_zero, first_moving)
    d_joined, gain_skip, bias_skip = advance(pull_skip(d_h_zero), moving)
    grad_tokens = d_joined[:, :model_width].astype(jnp.bfloat16)
    grad_skip = d_joined[:, model_width:].astype(jnp.bfloat16)
    qk_cols = 4 * HEAD
    mine = lax.broadcasted_iota(jnp.int32, (dp_count, 1, 1), 0) == dp_rank
    d_images = jnp.where(mine, d_image[None], 0.0).reshape(dp_count * IMGS, model_width)
    small = jnp.concatenate(
        [
            d_images,
            jnp.stack([gain_skip[:model_width], gain_skip[model_width:]]),
            jnp.stack([gain_one, gain_three, gain_four]),
            jnp.stack([bias_skip[:model_width], bias_skip[model_width:]]),
            jnp.stack([bias_one, bias_three, bias_four]),
            jnp.pad(
                jnp.concatenate([gain_qk[:, :HEAD], bias_qk[:, :HEAD]]).reshape(1, qk_cols),
                ((0, 0), (0, model_width - qk_cols)),
            ),
        ]
    )
    small = sum_all(sum_all(small, "dp"), "seq")
    cond_abs = lax.dynamic_slice_in_dim(
        cond_ranked, dp_rank * row_count, row_count, axis=1
    ).astype(jnp.float32)
    grad_mod = jnp.dot(
        cond_abs.T,
        small[: dp_count * IMGS],
        precision=lax.Precision.HIGHEST,
        preferred_element_type=jnp.float32,
    )
    d_image_all, small = small[: dp_count * IMGS], small[dp_count * IMGS :]
    qk_total = small[10, :qk_cols].reshape(4, HEAD)

    (grad_down,) = put_rows(down_way.finish(), ranks, [(seq_count * part, model_width)], [part])
    grad_up = put_columns(
        up_way.finish(),
        ranks,
        [[(at, first, size) for first, at, size in m] for m in up_moves],
        wide,
        jnp.float32,
    )
    grad_down, grad_up = advance((grad_down, grad_up), moving)
    if aligned(skip_rows):
        total_skip = skip_scatter.total()
    block_out = (x_three + block_way.total()).astype(jnp.bfloat16)
    share, ckv_share = share_of(row_count, seq_count), share_of(w_ckv.shape[0], seq_count)
    square = (row_count, model_width)
    grad_co, grad_cq, grad_ckv, grad_out = put_rows(
        blocks_of(jnp.concatenate([s.total() for s in scatters]), "seq"),
        ranks,
        [square, square, w_ckv.shape, square],
        [share, share, ckv_share, share],
    )
    grad_qkv = put_columns(
        blocks_of(total_qkv, "seq"),
        ranks,
        [[(at, first, size) for first, at, size in m] for m in qkv_moves],
        3 * model_width,
        jnp.float32,
    )
    grad_w_skip = join_columns(blocks_of(total_skip, "seq"), ranks, jnp.float32)
    return (
        block_out,
        grad_tokens,
        grad_skip,
        small[0:5],
        small[5:9],
        small[9],
        qk_total[0:2],
        qk_total[2:4],
        grad_w_skip,
        grad_mod,
        grad_qkv,
        grad_out,
        grad_cq,
        grad_ckv,
        grad_co,
        grad_up,
        grad_down,
    )


def solution(mesh):
    in_specs = (
        P(("dp", "seq"), None),
        P(("dp", "seq"), None),
        P("dp", None),
        P("dp", None),
        P("dp", None),
        P("dp", None),
        P("dp", None, None),
        P("dp", None, None),
        P(),
        P(),
        P(),
        P(),
        P("dp", None),
        P("dp", None),
        P("dp", None),
        P("dp", None),
        P("dp", None),
        P("dp", None),
        P("dp", None),
        P("dp", None),
        P("dp", None),
        P(("dp", "seq"), None),
    )
    out_specs = (
        P(("dp", "seq"), None),
        P(("dp", "seq"), None),
        P(("dp", "seq"), None),
        P(),
        P(),
        P(),
        P(),
        P(),
        P("dp", None),
        P("dp", None),
        P("dp", None),
        P("dp", None),
        P("dp", None),
        P("dp", None),
        P("dp", None),
        P("dp", None),
        P("dp", None),
    )
    return jax.shard_map(shards, mesh=mesh, in_specs=in_specs, out_specs=out_specs, check_vma=False)
```
